32 devices in a mesh: rows: 4 (over y, x), cols: 8 (over z, core).
Axes of the slice: x: 2, y: 2, z: 4, core: 2. Of those that a mesh axis runs over, the one named last changes fastest.
Arguments:
- features: bfloat16 [16, 96, 32, 512], P(None, 'rows', 'cols'), may hold values from -6 to 6
- extent: int32 [2, 16], replicated, may hold values from 4 to 96, as said below
- cotangent: bfloat16 [3, 16, 24, 8, 512], P(None, None, 'rows', 'cols'), may hold values from -6 to 6
- wide_w: float32 [4, 4608, 512], P(None, 'cols'), may hold values from -0.09375 to 0.09375
- wide_mom: float32 [4, 4608, 512], P(None, 'cols'), may hold values from -1.5 to 1.5
- wide_avg: float32 [4, 4608, 512], P(None, 'cols'), may hold values from -0.09375 to 0.09375
- point_w: float32 [6, 512, 512], P(None, 'cols'), may hold values from -0.25 to 0.25
- point_mom: float32 [6, 512, 512], P(None, 'cols'), may hold values from -1.5 to 1.5
- point_avg: float32 [6, 512, 512], P(None, 'cols'), may hold values from -0.25 to 0.25
- norm_w: float32 [2, 10, 512], replicated, as said below
- norm_mom: float32 [2, 10, 512], replicated, may hold values from -3 to 3
- norm_avg: float32 [2, 10, 512], replicated, as said below
Outputs:
- result: bfloat16 [3, 16, 24, 8, 512], P(None, None, 'rows', 'cols')
- input_grad: float32 [16, 96, 32, 512], P(None, 'rows', 'cols')
- wide_grad: float32 [4, 4608, 512], P(None, 'cols')
- wide_mom_new: float32 [4, 4608, 512], P(None, 'cols')
- wide_new: float32 [4, 4608, 512], P(None, 'cols')
- wide_avg_new: float32 [4, 4608, 512], P(None, 'cols')
- point_grad: float32 [6, 512, 512], P(None, 'cols')
- point_mom_new: float32 [6, 512, 512], P(None, 'cols')
- point_new: float32 [6, 512, 512], P(None, 'cols')
- point_avg_new: float32 [6, 512, 512], P(None, 'cols')
- norm_grad: float32 [2, 10, 512], replicated
- norm_mom_new: float32 [2, 10, 512], replicated
- norm_new: float32 [2, 10, 512], replicated
- norm_avg_new: float32 [2, 10, 512], replicated
The draws below stay inside these ranges and needn't reach their ends.
Inputs may be any that keep to these rules, and one draw needn't show every extreme that they name: `extent`: row 0 holds each image's valid height, row 1 its valid width, in pixels; all are multiples of 4, at least half of 96 (row 0) or of 32 (row 1); some image has the full 96 and some the full 32. `norm_w`: row 0 holds positive gains, row 1 biases. `norm_avg`: row 0 holds positive averaged gains, row 1 averaged biases.
All inputs are finite; a program needn't handle non-finite values.
Results may differ from the reference program's by a relative error of at most 0.028.
Values may be sent and summed in bfloat16 or wider, within the bound.
No kernel may reach another device: no remote copies, remote signals or barrier semaphores. Data moves between devices by JAX's collectives and lax.ppermute only.
A program may use at most 256 MiB of HBM per device.

```python
import jax
import jax.numpy as jnp
from jax import lax

C = 512
TASKS = 3
IMAGES = 16
NORMS = 10
HEIGHT = 96
WIDTH = 32


def norm_table(key, salt):
    folded = jax.random.fold_in(key, salt)
    subkeys = jax.random.split(folded, 2)
    gain_draw = jnp.exp(jax.random.uniform(subkeys[0], (NORMS, C), jnp.float32, -0.7, 0.7))
    bias_draw = 0.5 * jnp.clip(jax.random.normal(subkeys[1], (NORMS, C), jnp.float32), -4.0, 4.0)
    return jnp.stack([gain_draw, bias_draw]).astype(jnp.float32)


def draw_norm_w(key, part):
    return norm_table(key, 11)


def draw_norm_avg(key, part):
    return norm_table(key, 12)


def draw_extent(key, part):
    folded = jax.random.fold_in(key, 13)
    subkeys = jax.random.split(folded, 4)
    heights = 4 * jax.random.randint(subkeys[0], (IMAGES,), max(1, HEIGHT // 8), HEIGHT // 4 + 1)
    widths = 4 * jax.random.randint(subkeys[1], (IMAGES,), max(1, WIDTH // 8), WIDTH // 4 + 1)
    tall_one = jax.random.randint(subkeys[2], (), 0, IMAGES)
    wide_one = jax.random.randint(subkeys[3], (), 0, IMAGES)
    image_ids = jnp.arange(IMAGES, dtype=jnp.int32)
    heights = jnp.where(image_ids == tall_one, HEIGHT, heights)
    widths = jnp.where(image_ids == wide_one, WIDTH, widths)
    return jnp.stack([heights, widths]).astype(jnp.int32)


def steps_of(key, dims, cuts, low, high):
    gain = 1.0
    for axis_at, shards_of in cuts:
        steps = jax.random.uniform(jax.random.fold_in(jax.random.fold_in(key, 6), axis_at), (shards_of,), jnp.float32, low / len(cuts), high / len(cuts))
        gain = gain * jnp.repeat(jnp.exp(steps), dims[axis_at] // shards_of).reshape((-1,) + (1,) * (len(dims) - 1 - axis_at))
    return gain


def gaussian(own_key, shape, width, bound, cuts=(), kind=jnp.bfloat16):
    result = jax.random.normal(own_key, shape, jnp.float32) * width
    if len(cuts) > 0:
        result = steps_of(own_key, shape, cuts, -0.22, 0.18) * result
    return jnp.clip(result, min=-bound, max=bound).astype(kind)


def setup_inputs(seed: int = 0) -> dict:
    key_of = jax.random.split(jax.random.key(seed), 13)
    return {
        "features": gaussian(key_of[0], (IMAGES, HEIGHT, WIDTH, C), 1.0, 6.0, ((1, 4), (2, 8))),
        "extent": draw_extent(jax.random.fold_in(key_of[12], 71), 0),
        "cotangent": gaussian(key_of[2], (TASKS, IMAGES, HEIGHT // 4, WIDTH // 4, C), 1.0, 6.0, ((2, 4), (3, 8))),
        "wide_w": gaussian(key_of[3], (1 + TASKS, 9 * C, C), (9 * C) ** -0.5, 0.09375, ((1, 8),), jnp.float32),
        "wide_mom": gaussian(key_of[4], (1 + TASKS, 9 * C, C), 0.1, 1.5, ((1, 8),), jnp.float32),
        "wide_avg": gaussian(key_of[5], (1 + TASKS, 9 * C, C), (9 * C) ** -0.5, 0.09375, ((1, 8),), jnp.float32),
        "point_w": gaussian(key_of[6], (2 * TASKS, C, C), C ** -0.5, 0.25, ((1, 8),), jnp.float32),
        "point_mom": gaussian(key_of[7], (2 * TASKS, C, C), 0.1, 1.5, ((1, 8),), jnp.float32),
        "point_avg": gaussian(key_of[8], (2 * TASKS, C, C), C ** -0.5, 0.25, ((1, 8),), jnp.float32),
        "norm_w": draw_norm_w(jax.random.fold_in(key_of[12], 71), 0),
        "norm_mom": gaussian(key_of[10], (2, NORMS, C), 0.3, 3.0, (), jnp.float32),
        "norm_avg": draw_norm_avg(jax.random.fold_in(key_of[12], 71), 0),
    }


EPSILON = 1e-05
MOMENTUM = 0.9
WEIGHT_DECAY = 0.0001
AVERAGE = 0.6
RATE_NORM = 0.4
HIGHEST = lax.Precision.HIGHEST

@jax.custom_vjp
def low(v):
    return lax.optimization_barrier(v.astype(jnp.bfloat16)).astype(jnp.float32)

@jax.custom_vjp
def low_back(v):
    return v

def low_keep(v):
    return (low(v), None)

def low_pass(kept, grad):
    return (grad,)

def back_keep(v):
    return (v, None)

def back_low(kept, grad):
    return (low(grad),)
low.defvjp(low_keep, low_pass)
low_back.defvjp(back_keep, back_low)

def grid_mask(extent, height_cells, width_cells, factor):
    heights = extent[0] // factor
    widths = extent[1] // factor
    row_ids = jnp.arange(height_cells, dtype=jnp.int32)
    col_ids = jnp.arange(width_cells, dtype=jnp.int32)
    inside = (row_ids[None, :, None] < heights[:, None, None]) & (col_ids[None, None, :] < widths[:, None, None])
    return inside.astype(jnp.float32)[..., None]

def widen(statistic):
    return statistic.reshape(statistic.shape[:-1] + (1, 1, 1) + statistic.shape[-1:])

def normalize(values, valid_mask, pixel_count, gain_row, biases):
    summed = lax.optimization_barrier(jnp.sum(values * valid_mask, axis=(-4, -3, -2)))
    squares = lax.optimization_barrier(jnp.sum(values * values * valid_mask, axis=(-4, -3, -2)))
    center_val = summed / pixel_count
    spread = squares / pixel_count - center_val * center_val
    inverse = lax.rsqrt(spread + EPSILON)
    return (values - widen(center_val)) * widen(inverse) * widen(gain_row) + widen(biases)

def mean_pool(values):
    layout = values.shape
    grouped = values.reshape(layout[:-3] + (layout[-3] // 2, 2, layout[-2] // 2, 2, layout[-1]))
    return lax.optimization_barrier(jnp.mean(grouped, axis=(-4, -2)))

def conv_taps(values, weight):
    channels = values.shape[-1]
    height_cells, width_cells = (values.shape[1], values.shape[2])
    padded = jnp.pad(values, ((0, 0), (1, 1), (1, 1), (0, 0)))
    summed = jnp.zeros(values.shape[:-1] + (weight.shape[-1],), jnp.float32)
    for offset in range(9):
        window = padded[:, offset // 3:offset // 3 + height_cells, offset % 3:offset % 3 + width_cells, :]
        summed = summed + jnp.einsum('bhwc,cd->bhwd', window, weight[offset * channels:(offset + 1) * channels], precision=HIGHEST)
    return summed

def block_forward(inputs, wide_w, point_w, norm_w, full_mask, half_mask, full_count):
    task_count = point_w.shape[0] // 2
    wide_low = low(wide_w)
    point_low = low(point_w)
    half_count = full_count / 4.0
    gain_rows = norm_w[0, 1:].reshape(task_count, 3, -1)
    biases = norm_w[1, 1:].reshape(task_count, 3, -1)
    shared = low_back(conv_taps(inputs * full_mask, wide_low[0]))
    lifted = jax.nn.silu(normalize(shared, full_mask, full_count, norm_w[0, 0], norm_w[1, 0])) * full_mask
    pooled = low(mean_pool(lifted))
    first_proj = low_back(jnp.einsum('bhwc,tcd->tbhwd', pooled, point_low[:task_count], precision=HIGHEST))
    hidden = low(jax.nn.silu(normalize(first_proj, half_mask, half_count, gain_rows[:, 0], biases[:, 0])) * half_mask)
    second = low_back(jnp.einsum('tbhwc,tcd->tbhwd', hidden, point_low[task_count:], precision=HIGHEST))
    attention = jax.nn.sigmoid(normalize(second, half_mask, half_count, gain_rows[:, 1], biases[:, 1]))
    masked = low(attention * pooled)
    branch = low_back(jnp.stack([conv_taps(masked[task_id], wide_low[1 + task_id]) for task_id in range(task_count)]))
    active = jax.nn.silu(normalize(branch, half_mask, half_count, gain_rows[:, 2], biases[:, 2])) * half_mask
    return mean_pool(active)

def refresh(weight, gradient, moment, average, step_rate):
    descent = gradient + WEIGHT_DECAY * weight
    mom_new = MOMENTUM * moment + descent
    weight_new = weight - step_rate * (descent + MOMENTUM * mom_new)
    avg_new = AVERAGE * average + (1.0 - AVERAGE) * weight_new
    return (mom_new, weight_new, avg_new)

def reference(features, extent, cotangent, wide_w, wide_mom, wide_avg, point_w, point_mom, point_avg, norm_w, norm_mom, norm_avg):
    full_mask = grid_mask(extent, HEIGHT, WIDTH, 1)
    half_mask = grid_mask(extent, HEIGHT // 2, WIDTH // 2, 2)
    full_count = jnp.sum(extent[0] * extent[1]).astype(jnp.float32)
    rate_wide = 0.4 / (9.0 * C) ** 0.5
    rate_point = 2.0 / float(C) ** 0.5

    def forward(inputs, wide_in, point_in, norm_in):
        return block_forward(inputs, wide_in, point_in, norm_in, full_mask, half_mask, full_count)
    output_f, pullback = jax.vjp(forward, features.astype(jnp.float32), wide_w, point_w, norm_w)
    scaled = cotangent.astype(jnp.float32) * lax.rsqrt(full_count / 16.0)
    input_grad, wide_grad, point_grad, norm_grad = pullback(scaled)
    wide_mom_new, wide_new, wide_avg_new = refresh(wide_w, wide_grad, wide_mom, wide_avg, rate_wide)
    point_mom_new, point_new, point_avg_new = refresh(point_w, point_grad, point_mom, point_avg, rate_point)
    norm_mom_new, norm_new, norm_avg_new = refresh(norm_w, norm_grad, norm_mom, norm_avg, RATE_NORM)
    return (output_f.astype(jnp.bfloat16), input_grad, wide_grad, wide_mom_new, wide_new, wide_avg_new, point_grad, point_mom_new, point_new, point_avg_new, norm_grad, norm_mom_new, norm_new, norm_avg_new)
```

```python
import functools

import jax
import jax.numpy as jnp
from jax import lax
from jax.experimental import pallas as pl
from jax.experimental.pallas import tpu as pltpu
from jax.sharding import Mesh
from jax.sharding import PartitionSpec as P

EPSILON = 1e-05
MOMENTUM = 0.9
WEIGHT_DECAY = 0.0001
AVERAGE = 0.6
RATE_NORM = 0.4
F32 = jnp.float32
BF16 = jnp.bfloat16
EVERY = ("rows", "chips", "core")
PAIR = [(0, 1), (1, 0)]
VMEM_LIMIT = 56 * 1024 * 1024


def sigmoid(values):
    return 0.5 * jnp.tanh(0.5 * values) + 0.5


def flat(values):
    return values.reshape((-1, values.shape[-1]))


def mask_of(ext_ref, row, col, rows, cols):
    shape = (rows, cols) + ext_ref.shape[1:]
    row_ids = row + lax.broadcasted_iota(jnp.int32, shape, 0)
    col_ids = col + lax.broadcasted_iota(jnp.int32, shape, 1)
    inside = (row_ids < ext_ref[0][None, None]) & (col_ids < ext_ref[1][None, None])
    return inside


def keep(inside, values):
    return jnp.where(inside, values, 0.0)


def sums_of(first, second):
    return jnp.concatenate(
        [jnp.sum(flat(first), axis=0, keepdims=True), jnp.sum(flat(second), axis=0, keepdims=True)],
        axis=0,
    )


def moments(total, inv_count):
    center = total[0:1] * inv_count
    spread = total[1:2] * inv_count - center * center
    return center, lax.rsqrt(spread + EPSILON)


def taps_dot(source, weight, rows, cols, row, mirrored):
    channels = weight.shape[-1]
    total = None
    for tap in range(9):
        dr, dc = tap // 3, tap % 3
        if mirrored:
            dr, dc = 2 - dr, 2 - dc
        window = flat(source[pl.ds(row + dr, rows), dc : dc + cols])
        block = weight[tap * channels : (tap + 1) * channels, :]
        dims = (((1,), (1,)), ((), ())) if mirrored else (((1,), (0,)), ((), ()))
        part = lax.dot_general(window, block, dims, preferred_element_type=F32)
        total = part if total is None else total + part
    return total


def dot(left, right):
    return jnp.dot(left, right, preferred_element_type=F32)


def dot_nt(left, right):
    return lax.dot_general(left, right, (((1,), (1,)), ((), ())), preferred_element_type=F32)


def dot_tn(left, right):
    return lax.dot_general(left, right, (((0,), (0,)), ((), ())), preferred_element_type=F32)


def assemble(place_ref, pieces, w_ref, sem, task, start):
    chip, core, row = place_ref[0], place_ref[1], place_ref[2]
    half = len(pieces) // 2
    count = 0
    for side in range(2):
        own, parts = pieces[side * half], pieces[side * half + 1 : (side + 1) * half]
        depth = own.shape[1]
        width = parts[0].shape[-1]
        at_core = core if side == 0 else 1 - core

        def run(source, target, at):
            copy = pltpu.make_async_copy(source, target, sem.at[at])
            copy.start() if start else copy.wait()

        base = pl.multiple_of((2 * chip + at_core) * depth, 16)
        run(own.at[task], w_ref.at[pl.ds(base, depth)], count)
        count += 1
        for flip, part in enumerate(parts):
            lane = pl.multiple_of(jnp.bitwise_xor(row, flip) * width, 128)
            for hop in range(part.shape[0]):
                from_chip = jnp.bitwise_xor(chip, hop + 1)
                base = pl.multiple_of((2 * from_chip + at_core) * depth, 16)
                run(part.at[hop, task], w_ref.at[pl.ds(base, depth), pl.ds(lane, width)], count)
                count += 1


def gathered(place_ref, pieces, w_ref, sem):
    @pl.when(pl.program_id(0) == 0)
    def _():
        assemble(place_ref, pieces, w_ref, sem.at[0], 0, True)
        assemble(place_ref, pieces, w_ref, sem.at[0], 0, False)


def shared_fwd_kernel(rows, place_ref, x_ref, ext_ref, *refs):
    *pieces, z_ref, stat_ref, acc_ref, w_ref, sem = refs
    gathered(place_ref, pieces, w_ref, sem)
    step = pl.program_id(0)
    cols = z_ref.shape[1]
    z = taps_dot(x_ref, w_ref, rows, cols, step * rows, False).reshape(z_ref.shape)
    z_ref[...] = z
    zm = keep(mask_of(ext_ref, step * rows, 0, rows, cols), z)
    part = sums_of(zm, zm * z)

    @pl.when(step == 0)
    def _():
        acc_ref[...] = part

    @pl.when(step > 0)
    def _():
        acc_ref[...] += part

    @pl.when(step == pl.num_programs(0) - 1)
    def _():
        stat_ref[...] = jnp.broadcast_to(acc_ref[...][None], stat_ref.shape)


def pool_kernel(rows, z_ref, stat_ref, meta_ref, norm_ref, ext_ref, p_ref, out_ref, st_ref, pool_ref, aff_ref):
    step = pl.program_id(0)
    cols = z_ref.shape[1]

    @pl.when(step == 0)
    def _():
        center, inverse = moments(jnp.sum(stat_ref[...], axis=0), meta_ref[0:1])
        scale = inverse * norm_ref[0, 0:1]
        aff_ref[0:1] = scale
        aff_ref[1:2] = norm_ref[1, 0:1] - center * scale

    v = z_ref[...] * aff_ref[0:1] + aff_ref[1:2]
    lifted = keep(mask_of(ext_ref, step * rows, 0, rows, cols), v * sigmoid(v))
    grouped = lifted.reshape((rows // 2, 2, cols // 2, 2) + lifted.shape[2:])
    mean = 0.25 * (
        (grouped[:, 0, :, 0] + grouped[:, 0, :, 1]) + (grouped[:, 1, :, 0] + grouped[:, 1, :, 1])
    )
    low = mean.astype(BF16)
    out_ref[...] = low
    pool_ref[pl.ds(step * (rows // 2), rows // 2)] = low

    @pl.when(step == pl.num_programs(0) - 1)
    def _():
        left = flat(pool_ref[...])
        for task in range(p_ref.shape[0]):
            f = dot(left, p_ref[task])
            st_ref[:, task] = jnp.broadcast_to(
                sums_of(f, f * f)[None], (st_ref.shape[0],) + st_ref.shape[2:]
            )


def task_norm(stat_ref, meta_ref, norm_ref, task, slot):
    center, inverse = moments(jnp.sum(stat_ref[:, 0], axis=0), meta_ref[1:2])
    row = 1 + 3 * task + slot
    gain = norm_ref[0, pl.ds(row, 1)]
    bias = norm_ref[1, pl.ds(row, 1)]
    return center, inverse, gain, bias


def attend_kernel(pe_ref, stat_ref, meta_ref, norm_ref, ext_ref, p1_ref, p2_ref, first_ref, hidden_ref, second_ref, st_ref):
    task = pl.program_id(0)
    shape = pe_ref.shape
    rows, cols = shape[0] - 2, shape[1] - 2
    center, inverse, gain, bias = task_norm(stat_ref, meta_ref, norm_ref, task, 0)
    scale = inverse * gain
    shift = bias - center * scale
    first = dot(flat(pe_ref[...]), p1_ref[0])
    first_ref[0] = first.reshape(shape)[1 : 1 + rows, 1 : 1 + cols]
    v = first * scale + shift
    inside = mask_of(ext_ref, -1, -1, rows + 2, cols + 2)
    hidden = keep(inside, (v * sigmoid(v)).reshape(shape)).astype(BF16)
    hidden_ref[0] = hidden[1 : 1 + rows, 1 : 1 + cols]
    second = dot(flat(hidden), p2_ref[0]).reshape(shape)
    second_ref[0] = second
    own = second[1 : 1 + rows, 1 : 1 + cols]
    st_ref[:, 0] = jnp.broadcast_to(sums_of(own, own * own)[None], (st_ref.shape[0],) + st_ref.shape[2:])


def branch_fwd_kernel(second_ref, pe_ref, stat_ref, meta_ref, norm_ref, ext_ref, w_ref, masked_ref, branch_ref, st_ref):
    task = pl.program_id(0)
    rows, cols = branch_ref.shape[1:3]
    center, inverse, gain, bias = task_norm(stat_ref, meta_ref, norm_ref, task, 1)
    scale = inverse * gain
    shift = bias - center * scale
    attention = sigmoid(second_ref[0] * scale + shift)
    masked_ref[0] = (attention * pe_ref[...].astype(F32)).astype(BF16)
    z = taps_dot(masked_ref.at[0], w_ref.at[0], rows, cols, 0, False).reshape(branch_ref.shape[1:])
    branch_ref[0] = z
    zm = keep(mask_of(ext_ref, 0, 0, rows, cols), z)
    st_ref[:, 0] = jnp.broadcast_to(sums_of(zm, zm * z)[None], (st_ref.shape[0],) + st_ref.shape[2:])


def branch_grad_terms(branch_ref, cot_ref, stat_ref, meta_ref, norm_ref, ext_ref, task):
    rows, cols = branch_ref.shape[1:3]
    center, inverse, gain, bias = task_norm(stat_ref, meta_ref, norm_ref, task, 2)
    zhat = (branch_ref[0] - center) * inverse
    v = zhat * gain + bias
    s = sigmoid(v)
    inside = mask_of(ext_ref, 0, 0, rows, cols)
    c = cot_ref[0].astype(F32) * (0.25 * meta_ref[2:3])
    spread = jnp.broadcast_to(c[:, None, :, None], (rows // 2, 2, cols // 2, 2) + c.shape[2:])
    upstream = keep(inside, spread.reshape(v.shape) * (s * (1.0 + v * (1.0 - s))))
    return zhat, v, s, inside, upstream, gain * inverse


def result_kernel(branch_ref, cot_ref, stat_ref, meta_ref, norm_ref, ext_ref, out_ref, st_ref):
    task = pl.program_id(0)
    rows, cols = branch_ref.shape[1:3]
    zhat, v, s, inside, upstream, _ = branch_grad_terms(
        branch_ref, cot_ref, stat_ref, meta_ref, norm_ref, ext_ref, task
    )
    active = keep(inside, v * s)
    grouped = active.reshape((rows // 2, 2, cols // 2, 2) + active.shape[2:])
    mean = 0.25 * (
        (grouped[:, 0, :, 0] + grouped[:, 0, :, 1]) + (grouped[:, 1, :, 0] + grouped[:, 1, :, 1])
    )
    out_ref[0] = mean.astype(BF16)
    st_ref[:, 0] = jnp.broadcast_to(
        sums_of(upstream, upstream * zhat)[None], (st_ref.shape[0],) + st_ref.shape[2:]
    )


def back_sums(stat_ref, inv_count):
    total = jnp.sum(stat_ref[:, 0], axis=0)
    return total[0:1] * inv_count, total[1:2] * inv_count


def branch_dz_kernel(branch_ref, cot_ref, stat_ref, back_ref, meta_ref, norm_ref, ext_ref, dz_ref):
    task = pl.program_id(0)
    zhat, v, s, inside, upstream, factor = branch_grad_terms(
        branch_ref, cot_ref, stat_ref, meta_ref, norm_ref, ext_ref, task
    )
    bias_mean, gain_mean = back_sums(back_ref, meta_ref[1:2])
    dz_ref[0] = keep(inside, factor * (upstream - bias_mean - zhat * gain_mean)).astype(BF16)


def branch_dgrad_kernel(dz_ref, w_ref, second_ref, pooled_ref, stat_ref, meta_ref, norm_ref, ga_ref, prod_ref, st_ref):
    task = pl.program_id(0)
    shape = pooled_ref.shape
    rows, cols = shape[:2]
    center, inverse, gain, bias = task_norm(stat_ref, meta_ref, norm_ref, task, 1)
    grad = taps_dot(dz_ref.at[0], w_ref.at[0], rows, cols, 0, True).reshape(shape)
    zhat = (second_ref[0, 1 : 1 + rows, 1 : 1 + cols] - center) * inverse
    attention = sigmoid(zhat * gain + bias)
    through = grad * attention
    ga = through * pooled_ref[...].astype(F32) * (1.0 - attention)
    ga_ref[0] = ga

    @pl.when(task == 0)
    def _():
        prod_ref[...] = through

    @pl.when(task > 0)
    def _():
        prod_ref[...] += through

    st_ref[:, 0] = jnp.broadcast_to(sums_of(ga, ga * zhat)[None], (st_ref.shape[0],) + st_ref.shape[2:])


def branch_wgrad_kernel(own_ref, other_ref, dz_own_ref, dz_other_ref, out_ref):
    rows, cols = dz_own_ref.shape[1:3]
    own = flat(dz_own_ref[0])
    other = flat(dz_other_ref[0])
    for tap in range(9):
        dr, dc = tap // 3, tap % 3
        total = dot_tn(flat(own_ref[0, dr : dr + rows, dc : dc + cols]), own)
        total += dot_tn(flat(other_ref[0, dr : dr + rows, dc : dc + cols]), other)
        out_ref[0, tap] = total.astype(BF16)


def attend_back_kernel(ga_ref, second_ref, stat2_ref, back_ref, hidden_ref, p2_ref, first_ref, stat1_ref, meta_ref, norm_ref, ext_ref, wg_ref, gl_ref, st_ref):
    task = pl.program_id(0)
    shape = ga_ref.shape[1:]
    rows, cols = shape[:2]
    center, inverse, gain, _ = task_norm(stat2_ref, meta_ref, norm_ref, task, 1)
    zhat = (second_ref[0, 1 : 1 + rows, 1 : 1 + cols] - center) * inverse
    bias_mean, gain_mean = back_sums(back_ref, meta_ref[1:2])
    inside = mask_of(ext_ref, 0, 0, rows, cols)
    dz = keep(inside, gain * inverse * (ga_ref[0] - bias_mean - zhat * gain_mean)).astype(BF16)
    wg_ref[0] = dot_tn(flat(hidden_ref[0]), flat(dz)).astype(BF16)
    grad_hidden = dot_nt(flat(dz), p2_ref[0]).reshape(shape)
    center, inverse, gain, bias = task_norm(stat1_ref, meta_ref, norm_ref, task, 0)
    zhat = (first_ref[0] - center) * inverse
    v = zhat * gain + bias
    s = sigmoid(v)
    gl = keep(inside, grad_hidden * (s * (1.0 + v * (1.0 - s))))
    gl_ref[0] = gl
    st_ref[:, 0] = jnp.broadcast_to(sums_of(gl, gl * zhat)[None], (st_ref.shape[0],) + st_ref.shape[2:])


def unpool(grad, rows, cols):
    spread = jnp.broadcast_to(grad[:, None, :, None], (rows // 2, 2, cols // 2, 2) + grad.shape[2:])
    return spread.reshape((rows, cols) + grad.shape[2:])


def shared_grad_terms(z, grad, center, inverse, gain, bias, inside):
    zhat = (z - center) * inverse
    v = zhat * gain + bias
    s = sigmoid(v)
    upstream = keep(inside, unpool(0.25 * grad, z.shape[0], z.shape[1]) * (s * (1.0 + v * (1.0 - s))))
    return zhat, upstream


def pooled_back_kernel(chunk, gl_ref, first_ref, stat1_ref, back_ref, pooled_ref, p1_ref, prod_ref, z_ref, stat0_ref, meta_ref, norm_ref, ext_ref, full_ref, wg_ref, gp_ref, st_ref):
    task = pl.program_id(0)
    shape = gl_ref.shape[1:]
    rows, cols = shape[:2]
    center, inverse, gain, _ = task_norm(stat1_ref, meta_ref, norm_ref, task, 0)
    zhat = (first_ref[0] - center) * inverse
    bias_mean, gain_mean = back_sums(back_ref, meta_ref[1:2])
    inside = mask_of(ext_ref, 0, 0, rows, cols)
    dz = keep(inside, gain * inverse * (gl_ref[0] - bias_mean - zhat * gain_mean)).astype(BF16)
    wg_ref[0] = dot_tn(flat(pooled_ref[...]), flat(dz)).astype(BF16)
    grad = dot_nt(flat(dz), p1_ref[0]).reshape(shape)

    @pl.when(task == 0)
    def _():
        gp_ref[...] = prod_ref[...] + grad

    @pl.when(task > 0)
    def _():
        gp_ref[...] += grad

    @pl.when(task == pl.num_programs(0) - 1)
    def _():
        center, inverse = moments(jnp.sum(stat0_ref[...], axis=0), meta_ref[0:1])
        gain, bias = norm_ref[0, 0:1], norm_ref[1, 0:1]
        full_rows, full_cols = z_ref.shape[:2]

        def body(i, total):
            row = i * chunk
            inside = mask_of(full_ref, row, 0, chunk, full_cols)
            zhat, upstream = shared_grad_terms(
                z_ref[pl.ds(row, chunk)], gp_ref[pl.ds(i * (chunk // 2), chunk // 2)],
                center, inverse, gain, bias, inside,
            )
            return total + sums_of(upstream, upstream * zhat)

        total = lax.fori_loop(0, full_rows // chunk, body, jnp.zeros(st_ref.shape[1:], F32))
        st_ref[...] = jnp.broadcast_to(total[None], st_ref.shape)


def shared_dz_kernel(rows, z_ref, gp_ref, stat_ref, back_ref, meta_ref, norm_ref, ext_ref, dz_ref):
    step = pl.program_id(0)
    cols = z_ref.shape[1]
    center, inverse = moments(jnp.sum(stat_ref[...], axis=0), meta_ref[0:1])
    gain, bias = norm_ref[0, 0:1], norm_ref[1, 0:1]
    total = jnp.sum(back_ref[...], axis=0) * meta_ref[0:1]
    inside = mask_of(ext_ref, step * rows, 0, rows, cols)
    zhat, upstream = shared_grad_terms(z_ref[...], gp_ref[...], center, inverse, gain, bias, inside)
    dz = gain * inverse * (upstream - total[0:1] - zhat * total[1:2])
    dz_ref[...] = keep(inside, dz).astype(BF16)


def shared_wgrad_kernel(own_ref, other_ref, dz_own_ref, dz_other_ref, out_ref):
    tap = pl.program_id(0)
    rows, cols = dz_own_ref.shape[:2]
    row = tap // 3
    for dc in range(3):

        @pl.when(tap % 3 == dc)
        def _():
            total = dot_tn(flat(own_ref[pl.ds(row, rows), dc : dc + cols]), flat(dz_own_ref[...]))
            total += dot_tn(flat(other_ref[pl.ds(row, rows), dc : dc + cols]), flat(dz_other_ref[...]))
            out_ref[0] = total.astype(BF16)


def shared_dgrad_kernel(rows, place_ref, dz_ref, ext_ref, *refs):
    *pieces, out_ref, w_ref, sem = refs
    gathered(place_ref, pieces, w_ref, sem)
    step = pl.program_id(0)
    cols = out_ref.shape[1]
    grad = taps_dot(dz_ref, w_ref, rows, cols, step * rows, True).reshape(out_ref.shape)
    out_ref[...] = keep(mask_of(ext_ref, step * rows, 0, rows, cols), grad)


def whole(shape):
    return pl.BlockSpec(shape, lambda i: (0,) * len(shape))


def leading(shape):
    return pl.BlockSpec(shape, lambda i: (i,) + (0,) * (len(shape) - 1))


def second_dim(shape):
    return pl.BlockSpec(shape, lambda i: (0, i) + (0,) * (len(shape) - 2))


def call(kernel, grid, ins, outs, scratch=(), flops=0):
    arrays = [array for array, _ in ins]
    moved = sum(a.size * a.dtype.itemsize for a in arrays)
    moved += sum(s.size * s.dtype.itemsize for s, _ in outs)
    return pl.pallas_call(
        kernel,
        grid=(grid,),
        in_specs=[spec for _, spec in ins],
        out_specs=[spec for _, spec in outs],
        out_shape=[shape for shape, _ in outs],
        scratch_shapes=list(scratch),
        compiler_params=pltpu.CompilerParams(vmem_limit_bytes=VMEM_LIMIT),
        cost_estimate=pl.CostEstimate(flops=flops, bytes_accessed=moved, transcendentals=0),
    )(*arrays)


def shape_of(shape, dtype):
    return jax.ShapeDtypeStruct(shape, dtype)


def shift_cols(array, step):
    chips, cores = lax.axis_size("chips"), lax.axis_size("core")
    total = chips * cores
    pairs = [(i, i + step) for i in range(total) if 0 <= i + step < total]
    return lax.ppermute(array, ("chips", "core"), pairs)


def shift_rows(array, step):
    total = lax.axis_size("rows")
    pairs = [(i, i + step) for i in range(total) if 0 <= i + step < total]
    return lax.ppermute(array, "rows", pairs)


def extended(array, row_dim):
    length = array.shape[row_dim]
    before = shift_rows(lax.slice_in_dim(array, length - 1, length, axis=row_dim), 1)
    after = shift_rows(lax.slice_in_dim(array, 0, 1, axis=row_dim), -1)
    array = jnp.concatenate([before, array, after], axis=row_dim)
    dim = row_dim + 1
    length = array.shape[dim]
    before = shift_cols(lax.slice_in_dim(array, length - 1, length, axis=dim), 1)
    after = shift_cols(lax.slice_in_dim(array, 0, 1, axis=dim), -1)
    return jnp.concatenate([before, array, after], axis=dim)


def spread_all(stats):
    return lax.all_to_all(stats, EVERY, 0, 0)


def swap(array, axis, flip):
    total = lax.axis_size(axis)
    return lax.ppermute(array, axis, [(i, i ^ flip) for i in range(total)])


def spread_chips(shard):
    chips, rows = lax.axis_size("chips"), lax.axis_size("rows")
    width = shard.shape[-1] // rows
    mine = lax.dynamic_slice_in_dim(shard, lax.axis_index("rows") * width, width, axis=2)
    return [swap(mine, "chips", hop) for hop in range(1, chips)]


def spread_rows(shard, hops):
    line = jnp.stack(hops)
    return [shard, line] + [swap(line, "rows", flip) for flip in range(1, lax.axis_size("rows"))]


def spread_cores(pieces):
    return pieces + [swap(piece, "core", 1) for piece in pieces]


def gather_weights(shard):
    rows = lax.axis_size("rows")
    part = shard.shape[1] // rows
    mine = lax.dynamic_slice_in_dim(shard, lax.axis_index("rows") * part, part, axis=1)
    return lax.all_gather(mine.astype(BF16), ("chips", "core", "rows"), axis=1, tiled=True)


def pick(array, axis, index):
    return lax.dynamic_index_in_dim(array, index, axis=axis, keepdims=False)


def summed(parts):
    total = parts[0].astype(F32)
    for part in parts[1:]:
        total = total + part.astype(F32)
    return total.astype(BF16)


def reduce_rows(half):
    groups, depth, width = half.shape
    rows, chips = lax.axis_size("rows"), lax.axis_size("chips")
    row = lax.axis_index("rows")
    parts = half.reshape(groups, chips, 2, rows, depth // (2 * rows * chips), width)
    mine = pick(parts, 3, row)
    return [mine] + [swap(pick(parts, 3, row ^ flip), "rows", flip) for flip in range(1, rows)]


def reduce_chips(parts):
    total = summed(parts)
    chip = lax.axis_index("chips")
    chips = lax.axis_size("chips")
    return [pick(total, 1, chip)] + [
        swap(pick(total, 1, chip ^ hop), "chips", hop) for hop in range(1, chips)
    ]


def share_rows(parts):
    total = summed(parts)
    core = lax.axis_index("core")
    kept = pick(total, 1, core)
    got = swap(pick(total, 1, 1 - core), "core", 1)
    low = jnp.where(core == 0, kept, got)
    high = jnp.where(core == 0, got, kept)
    share = jnp.concatenate([low, high], axis=-1)
    return [share] + [swap(share, "rows", flip) for flip in range(1, lax.axis_size("rows"))]


def reduce_half(half):
    return share_rows(reduce_chips(reduce_rows(half)))


def update_kernel(rate, count, place_ref, weight_ref, moment_ref, average_ref, *refs):
    parts, outs = refs[:count], refs[-4:]
    turn = pl.program_id(1)
    for flip, part in enumerate(parts):

        @pl.when(turn == flip)
        def _():
            grad = part[...].astype(F32)[:, None]
            weight = weight_ref[...]
            descent = grad + WEIGHT_DECAY * weight
            mom_new = MOMENTUM * moment_ref[...] + descent
            weight_new = weight - rate * (descent + MOMENTUM * mom_new)
            outs[0][...] = grad
            outs[1][...] = mom_new
            outs[2][...] = weight_new
            outs[3][...] = AVERAGE * average_ref[...] + (1.0 - AVERAGE) * weight_new


def update(parts, weight, moment, average, rate, first, block, earlier=()):
    groups, depth, channels = weight.shape
    rows = lax.axis_size("rows")
    piece = depth // rows
    count = parts[0].shape[0]
    split = (groups, rows, piece, channels)
    weight, moment, average = (a.reshape(split) for a in (weight, moment, average))
    earlier = [a.reshape(split) for a in earlier]
    state = pl.BlockSpec(
        (block, 1, piece, channels), lambda g, t, p: (g + first // block, jnp.bitwise_xor(p[2], t), 0, 0)
    )
    grads = pl.BlockSpec((block, piece, channels), lambda g, t, p: (g, 0, 0))
    anywhere = pl.BlockSpec(memory_space=pl.ANY)
    outs = pl.pallas_call(
        functools.partial(update_kernel, rate, len(parts)),
        grid_spec=pltpu.PrefetchScalarGridSpec(
            num_scalar_prefetch=1,
            grid=(count // block, rows),
            in_specs=[state] * 3 + [grads] * len(parts) + [anywhere] * len(earlier),
            out_specs=[state] * 4,
        ),
        out_shape=[jax.ShapeDtypeStruct(split, F32)] * 4,
        input_output_aliases={4 + len(parts) + i: i for i in range(len(earlier))},
        compiler_params=pltpu.CompilerParams(vmem_limit_bytes=VMEM_LIMIT),
        cost_estimate=pl.CostEstimate(
            flops=0, bytes_accessed=30 * count * depth * channels, transcendentals=0
        ),
    )(place_of(), weight, moment, average, *parts, *earlier)
    return [a.reshape(groups, depth, channels) for a in outs]


def place_of():
    place = jnp.stack([lax.axis_index("chips"), lax.axis_index("core"), lax.axis_index("rows")])
    return place.astype(jnp.int32)


def halves(array):
    core = lax.axis_index("core")
    half = array.shape[-1] // 2
    mine = lax.dynamic_slice_in_dim(array, core * half, half, axis=array.ndim - 1)
    other = lax.dynamic_slice_in_dim(array, (1 - core) * half, half, axis=array.ndim - 1)
    return mine, lax.ppermute(other, "core", PAIR)


def refresh(weight, gradient, moment, average, step_rate):
    descent = gradient + WEIGHT_DECAY * weight
    mom_new = MOMENTUM * moment + descent
    weight_new = weight - step_rate * (descent + MOMENTUM * mom_new)
    avg_new = AVERAGE * average + (1.0 - AVERAGE) * weight_new
    return (mom_new, weight_new, avg_new)


def shards(
    features,
    extent,
    cotangent,
    wide_w,
    wide_mom,
    wide_avg,
    point_w,
    point_mom,
    point_avg,
    norm_w,
    norm_mom,
    norm_avg,
):
    tasks = point_w.shape[0] // 2
    images, rows, cols, channels = features.shape
    half_rows, half_cols = rows // 2, cols // 2
    rate_wide = 0.4 / (9.0 * channels) ** 0.5
    rate_point = 2.0 / float(channels) ** 0.5
    devices = lax.axis_size("rows") * lax.axis_size("chips") * lax.axis_size("core")
    row_start = lax.axis_index("rows") * rows
    col_start = (lax.axis_index("chips") * lax.axis_size("core") + lax.axis_index("core")) * cols
    starts = jnp.stack([row_start, col_start]).astype(jnp.int32)[:, None]
    full_ext = jnp.broadcast_to((extent - starts)[:, :, None], (2, images, channels))
    half_ext = jnp.broadcast_to((extent // 2 - starts // 2)[:, :, None], (2, images, channels))
    full_count = jnp.sum(extent[0] * extent[1]).astype(F32)
    meta = jnp.broadcast_to(
        jnp.stack([1.0 / full_count, 4.0 / full_count, lax.rsqrt(full_count / 16.0)])[:, None],
        (3, channels),
    )
    place = place_of()
    shared_own = wide_w[:1].astype(BF16)
    hops = spread_chips(shared_own)
    features, hops[0] = lax.optimization_barrier((features, hops[0]))
    pieces = spread_rows(shared_own, hops)
    point_full = gather_weights(point_w)
    first_w, second_w = point_full[:tasks], point_full[tasks:]

    maps = features.transpose(1, 2, 0, 3)
    row_ids = jnp.arange(rows, dtype=jnp.int32)[:, None, None]
    col_ids = jnp.arange(cols, dtype=jnp.int32)[None, :, None]
    inside = (row_ids < (extent[0] - row_start)[None, None]) & (col_ids < (extent[1] - col_start)[None, None])
    maps = jnp.where(inside[..., None], maps, jnp.zeros((), BF16))
    x_pad = extended(maps, 0)
    pieces, x_pad = lax.optimization_barrier((pieces, x_pad))
    later_w, _ = lax.optimization_barrier((wide_w[1:], pieces))
    branch_w = gather_weights(later_w)
    branch_in = (branch_w, leading((1,) + branch_w.shape[1:]))
    pieces = spread_cores(pieces)
    x_other = lax.ppermute(x_pad, "core", PAIR)
    cot = cotangent.transpose(0, 2, 3, 1, 4)

    full = (rows, cols, images, channels)
    half = (half_rows, half_cols, images, channels)
    wide = (half_rows + 2, half_cols + 2, images, channels)
    quarter = (half_rows // 2, half_cols // 2, images, channels)
    stat = (devices, 2, channels)
    task_stat = (devices, tasks, 2, channels)
    one_stat = second_dim((devices, 1, 2, channels))
    meta_in = (meta, whole(meta.shape))
    norm_in = (norm_w, whole(norm_w.shape))
    full_in = (full_ext, whole(full_ext.shape))
    half_in = (half_ext, whole(half_ext.shape))
    vec = pltpu.VMEM((2, channels), F32)
    place_in = (place, pl.BlockSpec(memory_space=pltpu.SMEM))
    anywhere = pl.BlockSpec(memory_space=pl.ANY)
    copies = 2 * (1 + lax.axis_size("rows") * (lax.axis_size("chips") - 1))

    def weight_room(slots):
        shape = (slots, 9 * channels, channels) if slots > 1 else (9 * channels, channels)
        return [pltpu.VMEM(shape, BF16), pltpu.SemaphoreType.DMA((slots, copies))]

    full_flops = 2 * 9 * rows * cols * images * channels * channels
    half_flops = full_flops // 4 * tasks
    task_of = lambda shape: leading((1,) + shape)

    block = 4
    z, local = call(
        functools.partial(shared_fwd_kernel, block),
        rows // block,
        [place_in, (x_pad, whole(x_pad.shape)), full_in] + [(p, anywhere) for p in pieces],
        [(shape_of(full, F32), leading((block,) + full[1:])), (shape_of(stat, F32), whole(stat))],
        [vec] + weight_room(1),
        full_flops,
    )
    stat0 = spread_all(local)

    pooled, local = call(
        functools.partial(pool_kernel, block),
        rows // block,
        [
            (z, leading((block,) + full[1:])),
            (stat0, whole(stat)),
            meta_in,
            norm_in,
            full_in,
            (first_w, whole(first_w.shape)),
        ],
        [
            (shape_of(half, BF16), leading((block // 2,) + half[1:])),
            (shape_of(task_stat, F32), whole(task_stat)),
        ],
        [pltpu.VMEM(half, BF16), vec],
    )
    pooled_wide = extended(pooled, 0)
    stat1 = spread_all(local)

    first, hidden, second, local = call(
        attend_kernel,
        tasks,
        [
            (pooled_wide, whole(wide)),
            (stat1, one_stat),
            meta_in,
            norm_in,
            half_in,
            (first_w, task_of(first_w.shape[1:])),
            (second_w, task_of(second_w.shape[1:])),
        ],
        [
            (shape_of((tasks,) + half, F32), task_of(half)),
            (shape_of((tasks,) + half, BF16), task_of(half)),
            (shape_of((tasks,) + wide, F32), task_of(wide)),
            (shape_of(task_stat, F32), one_stat),
        ],
    )
    stat2 = spread_all(local)

    masked, branch, local = call(
        branch_fwd_kernel,
        tasks,
        [
            (second, task_of(wide)),
            (pooled_wide, whole(wide)),
            (stat2, one_stat),
            meta_in,
            norm_in,
            half_in,
            branch_in,
        ],
        [
            (shape_of((tasks,) + wide, BF16), task_of(wide)),
            (shape_of((tasks,) + half, F32), task_of(half)),
            (shape_of(task_stat, F32), one_stat),
        ],
        flops=half_flops,
    )
    masked_other = lax.ppermute(masked, "core", PAIR)
    stat3 = spread_all(local)

    branch_ins = [
        (branch, task_of(half)),
        (cot, task_of(quarter)),
        (stat3, one_stat),
    ]
    result, local = call(
        result_kernel,
        tasks,
        branch_ins + [meta_in, norm_in, half_in],
        [
            (shape_of((tasks,) + quarter, BF16), task_of(quarter)),
            (shape_of(task_stat, F32), one_stat),
        ],
    )
    back3 = spread_all(local)

    (branch_dz,) = call(
        branch_dz_kernel,
        tasks,
        branch_ins + [(back3, one_stat), meta_in, norm_in, half_in],
        [(shape_of((tasks,) + half, BF16), task_of(half))],
    )
    dz_own, dz_other = halves(branch_dz)
    dz_wide = extended(branch_dz, 1)
    narrow = half[:-1] + (channels // 2,)
    (branch_grad,) = call(
        branch_wgrad_kernel,
        tasks,
        [
            (masked, task_of(wide)),
            (masked_other, task_of(wide)),
            (dz_own, task_of(narrow)),
            (dz_other, task_of(narrow)),
        ],
        [
            (
                shape_of((tasks, 9, channels, channels // 2), BF16),
                task_of((9, channels, channels // 2)),
            )
        ],
        flops=half_flops,
    )
    branch_share = reduce_half(branch_grad.reshape(tasks, 9 * channels, channels // 2))

    ga, product, local = call(
        branch_dgrad_kernel,
        tasks,
        [
            (dz_wide, task_of(wide)),
            branch_in,
            (second, task_of(wide)),
            (pooled, whole(half)),
            (stat2, one_stat),
            meta_in,
            norm_in,
        ],
        [
            (shape_of((tasks,) + half, F32), task_of(half)),
            (shape_of(half, F32), whole(half)),
            (shape_of(task_stat, F32), one_stat),
        ],
        flops=half_flops,
    )
    back2 = spread_all(local)

    square = (channels, channels)
    second_grad, gl, local = call(
        attend_back_kernel,
        tasks,
        [
            (ga, task_of(half)),
            (second, task_of(wide)),
            (stat2, one_stat),
            (back2, one_stat),
            (hidden, task_of(half)),
            (second_w, task_of(square)),
            (first, task_of(half)),
            (stat1, one_stat),
            meta_in,
            norm_in,
            half_in,
        ],
        [
            (shape_of((tasks,) + square, BF16), task_of(square)),
            (shape_of((tasks,) + half, F32), task_of(half)),
            (shape_of(task_stat, F32), one_stat),
        ],
    )
    back1 = spread_all(local)

    first_grad, grad_pooled, local = call(
        functools.partial(pooled_back_kernel, block),
        tasks,
        [
            (gl, task_of(half)),
            (first, task_of(half)),
            (stat1, one_stat),
            (back1, one_stat),
            (pooled, whole(half)),
            (first_w, task_of(square)),
            (product, whole(half)),
            (z, whole(full)),
            (stat0, whole(stat)),
            meta_in,
            norm_in,
            half_in,
            full_in,
        ],
        [
            (shape_of((tasks,) + square, BF16), task_of(square)),
            (shape_of(half, F32), whole(half)),
            (shape_of(stat, F32), whole(stat)),
        ],
    )
    back0 = spread_all(local)
    point_local = jnp.concatenate([first_grad, second_grad], axis=0)
    point_own, point_other = halves(point_local)
    point_share = reduce_half(point_own + point_other)

    (shared_dz,) = call(
        functools.partial(shared_dz_kernel, block),
        rows // block,
        [
            (z, leading((block,) + full[1:])),
            (grad_pooled, leading((block // 2,) + half[1:])),
            (stat0, whole(stat)),
            (back0, whole(stat)),
            meta_in,
            norm_in,
            full_in,
        ],
        [(shape_of(full, BF16), leading((block,) + full[1:]))],
    )
    dz_own, dz_other = halves(shared_dz)
    (shared_grad,) = call(
        shared_wgrad_kernel,
        9,
        [
            (x_pad, whole(x_pad.shape)),
            (x_other, whole(x_other.shape)),
            (dz_own, whole(dz_own.shape)),
            (dz_other, whole(dz_other.shape)),
        ],
        [(shape_of((9, channels, channels // 2), BF16), leading((1, channels, channels // 2)))],
        flops=full_flops,
    )
    shared_share = reduce_half(shared_grad.reshape(1, 9 * channels, channels // 2))
    dz_pad = extended(shared_dz, 0)
    (input_grad,) = call(
        functools.partial(shared_dgrad_kernel, block),
        rows // block,
        [place_in, (dz_pad, whole(dz_pad.shape)), full_in] + [(p, anywhere) for p in pieces],
        [(shape_of(full, F32), leading((block,) + full[1:]))],
        weight_room(1),
        full_flops,
    )
    input_grad = input_grad.transpose(2, 0, 1, 3)

    branch_state = update(branch_share, wide_w, wide_mom, wide_avg, rate_wide, 1, 1)
    wide_share, wide_mom_new, wide_new, wide_avg_new = update(
        shared_share, wide_w, wide_mom, wide_avg, rate_wide, 0, 1, branch_state
    )
    point_share, point_mom_new, point_new, point_avg_new = update(
        point_share, point_w, point_mom, point_avg, rate_point, 0, 2 * tasks
    )
    bsum = jnp.stack([jnp.sum(b, axis=0) for b in (back1, back2, back3)], axis=1)
    bsum = bsum.transpose(2, 0, 1, 3).reshape(2, 3 * tasks, channels)
    norm_grad = jnp.concatenate([jnp.sum(back0, axis=0)[:, None], bsum], axis=1)[::-1]
    norm_mom_new, norm_new, norm_avg_new = refresh(norm_w, norm_grad, norm_mom, norm_avg, RATE_NORM)
    return (
        result.transpose(0, 3, 1, 2, 4),
        input_grad,
        wide_share,
        wide_mom_new,
        wide_new,
        wide_avg_new,
        point_share,
        point_mom_new,
        point_new,
        point_avg_new,
        norm_grad,
        norm_mom_new,
        norm_new,
        norm_avg_new,
    )


def solution(mesh):
    rows, cols = mesh.devices.shape
    cores = 2
    fine = Mesh(mesh.devices.reshape(rows, cols // cores, cores), EVERY)
    across = ("chips", "core")
    weights = P(None, across, None)
    placed = (
        P(None, "rows", across, None),
        P(),
        P(None, None, "rows", across, None),
        weights,
        weights,
        weights,
        weights,
        weights,
        weights,
        P(),
        P(),
        P(),
    )
    return jax.shard_map(
        shards,
        mesh=fine,
        in_specs=placed,
        out_specs=(
            P(None, None, "rows", across, None),
            P(None, "rows", across, None),
            weights,
            weights,
            weights,
            weights,
            weights,
            weights,
            weights,
            weights,
            P(),
            P(),
            P(),
            P(),
        ),
        check_vma=False,
    )
```

```python
import functools

import jax
import jax.numpy as jnp
from jax import lax
from jax.experimental import pallas as pl
from jax.experimental.pallas import tpu as pltpu
from jax.sharding import Mesh
from jax.sharding import PartitionSpec as P

EPSILON = 1e-05
MOMENTUM = 0.9
WEIGHT_DECAY = 0.0001
AVERAGE = 0.6
RATE_NORM = 0.4
F32 = jnp.float32
BF16 = jnp.bfloat16
EVERY = ("rows", "chips", "core")
PAIR = [(0, 1), (1, 0)]
VMEM_LIMIT = 56 * 1024 * 1024


def sigmoid(values):
    return 0.5 * jnp.tanh(0.5 * values) + 0.5


def flat(values):
    return values.reshape((-1, values.shape[-1]))


def mask_of(ext_ref, row, col, rows, cols):
    shape = (rows, cols) + ext_ref.shape[1:]
    row_ids = row + lax.broadcasted_iota(jnp.int32, shape, 0)
    col_ids = col + lax.broadcasted_iota(jnp.int32, shape, 1)
    inside = (row_ids < ext_ref[0][None, None]) & (col_ids < ext_ref[1][None, None])
    return inside


def keep(inside, values):
    return jnp.where(inside, values, 0.0)


def sums_of(first, second):
    return jnp.concatenate(
        [jnp.sum(flat(first), axis=0, keepdims=True), jnp.sum(flat(second), axis=0, keepdims=True)],
        axis=0,
    )


def centered(sums, local):
    center = (sums[0:1] * local[1:2]).astype(BF16)
    wide = center.astype(F32)
    spread = sums[1:2] - 2.0 * wide * sums[0:1] + local[0:1] * wide * wide
    return jnp.concatenate([wide, spread], axis=0).astype(BF16)


def moments(stats, counts, inv_count):
    stats = stats.astype(F32)
    centers = stats[:, 0:1]
    center = jnp.sum(counts * centers, axis=0) * inv_count
    off = centers - center[None]
    spread = jnp.sum(stats[:, 1:2] + counts * off * off, axis=0) * inv_count
    return center, lax.rsqrt(spread + EPSILON)


def taps_dot(source, weight, rows, cols, row, mirrored):
    channels = weight.shape[-1]
    total = None
    for tap in range(9):
        dr, dc = tap // 3, tap % 3
        if mirrored:
            dr, dc = 2 - dr, 2 - dc
        window = flat(source[pl.ds(row + dr, rows), dc : dc + cols])
        block = weight[tap * channels : (tap + 1) * channels, :]
        dims = (((1,), (1,)), ((), ())) if mirrored else (((1,), (0,)), ((), ()))
        part = lax.dot_general(window, block, dims, preferred_element_type=F32)
        total = part if total is None else total + part
    return total


def dot(left, right):
    return jnp.dot(left, right, preferred_element_type=F32)


def dot_nt(left, right):
    return lax.dot_general(left, right, (((1,), (1,)), ((), ())), preferred_element_type=F32)


def dot_tn(left, right):
    return lax.dot_general(left, right, (((0,), (0,)), ((), ())), preferred_element_type=F32)


def assemble(place_ref, pieces, w_ref, sem, task, start):
    chip, core, row = place_ref[0], place_ref[1], place_ref[2]
    half = len(pieces) // 2
    count = 0
    for side in range(2):
        own, parts = pieces[side * half], pieces[side * half + 1 : (side + 1) * half]
        depth = own.shape[1]
        width = parts[0].shape[-1]
        at_core = core if side == 0 else 1 - core

        def run(source, target, at):
            copy = pltpu.make_async_copy(source, target, sem.at[at])
            copy.start() if start else copy.wait()

        base = pl.multiple_of((2 * chip + at_core) * depth, 16)
        run(own.at[task], w_ref.at[pl.ds(base, depth)], count)
        count += 1
        for flip, part in enumerate(parts):
            lane = pl.multiple_of(jnp.bitwise_xor(row, flip) * width, 128)
            for hop in range(part.shape[0]):
                from_chip = jnp.bitwise_xor(chip, hop + 1)
                base = pl.multiple_of((2 * from_chip + at_core) * depth, 16)
                run(part.at[hop, task], w_ref.at[pl.ds(base, depth), pl.ds(lane, width)], count)
                count += 1


def gathered(place_ref, pieces, w_ref, sem):
    @pl.when(pl.program_id(0) == 0)
    def _():
        assemble(place_ref, pieces, w_ref, sem.at[0], 0, True)
        assemble(place_ref, pieces, w_ref, sem.at[0], 0, False)


def shared_fwd_kernel(rows, place_ref, x_ref, meta_ref, ext_ref, *refs):
    *pieces, z_ref, stat_ref, acc_ref, w_ref, sem = refs
    gathered(place_ref, pieces, w_ref, sem)
    step = pl.program_id(0)
    cols = z_ref.shape[1]
    z = taps_dot(x_ref, w_ref, rows, cols, step * rows, False).reshape(z_ref.shape)
    z_ref[...] = z
    zm = keep(mask_of(ext_ref, step * rows, 0, rows, cols), z)
    part = sums_of(zm, zm * z)

    @pl.when(step == 0)
    def _():
        acc_ref[...] = part

    @pl.when(step > 0)
    def _():
        acc_ref[...] += part

    @pl.when(step == pl.num_programs(0) - 1)
    def _():
        stat_ref[...] = jnp.broadcast_to(centered(acc_ref[...], meta_ref[3:5])[None], stat_ref.shape)


def pool_kernel(rows, z_ref, stat_ref, count_ref, meta_ref, norm_ref, ext_ref, p_ref, out_ref, st_ref, pool_ref, aff_ref):
    step = pl.program_id(0)
    cols = z_ref.shape[1]

    @pl.when(step == 0)
    def _():
        center, inverse = moments(stat_ref[...], count_ref[0], meta_ref[0:1])
        scale = inverse * norm_ref[0, 0:1]
        aff_ref[0:1] = scale
        aff_ref[1:2] = norm_ref[1, 0:1] - center * scale

    v = z_ref[...] * aff_ref[0:1] + aff_ref[1:2]
    lifted = keep(mask_of(ext_ref, step * rows, 0, rows, cols), v * sigmoid(v))
    grouped = lifted.reshape((rows // 2, 2, cols // 2, 2) + lifted.shape[2:])
    mean = 0.25 * (
        (grouped[:, 0, :, 0] + grouped[:, 0, :, 1]) + (grouped[:, 1, :, 0] + grouped[:, 1, :, 1])
    )
    low = mean.astype(BF16)
    out_ref[...] = low
    pool_ref[pl.ds(step * (rows // 2), rows // 2)] = low

    @pl.when(step == pl.num_programs(0) - 1)
    def _():
        left = flat(pool_ref[...])
        for task in range(p_ref.shape[0]):
            f = dot(left, p_ref[task])
            st_ref[:, task] = jnp.broadcast_to(
                centered(sums_of(f, f * f), meta_ref[5:7])[None], (st_ref.shape[0],) + st_ref.shape[2:]
            )


def task_norm(stat_ref, count_ref, meta_ref, norm_ref, task, slot):
    center, inverse = moments(stat_ref[:, 0], count_ref[1], meta_ref[1:2])
    row = 1 + 3 * task + slot
    gain = norm_ref[0, pl.ds(row, 1)]
    bias = norm_ref[1, pl.ds(row, 1)]
    return center, inverse, gain, bias


def attend_kernel(pe_ref, stat_ref, count_ref, meta_ref, norm_ref, ext_ref, p1_ref, p2_ref, first_ref, hidden_ref, second_ref, st_ref):
    task = pl.program_id(0)
    shape = pe_ref.shape
    rows, cols = shape[0] - 2, shape[1] - 2
    center, inverse, gain, bias = task_norm(stat_ref, count_ref, meta_ref, norm_ref, task, 0)
    scale = inverse * gain
    shift = bias - center * scale
    first = dot(flat(pe_ref[...]), p1_ref[0])
    first_ref[0] = first.reshape(shape)[1 : 1 + rows, 1 : 1 + cols]
    v = first * scale + shift
    inside = mask_of(ext_ref, -1, -1, rows + 2, cols + 2)
    hidden = keep(inside, (v * sigmoid(v)).reshape(shape)).astype(BF16)
    hidden_ref[0] = hidden[1 : 1 + rows, 1 : 1 + cols]
    second = dot(flat(hidden), p2_ref[0]).reshape(shape)
    second_ref[0] = second
    own = second[1 : 1 + rows, 1 : 1 + cols]
    local = centered(sums_of(own, own * own), meta_ref[5:7])
    st_ref[:, 0] = jnp.broadcast_to(local[None], (st_ref.shape[0],) + st_ref.shape[2:])


def branch_fwd_kernel(second_ref, pe_ref, stat_ref, count_ref, meta_ref, norm_ref, ext_ref, w_ref, masked_ref, branch_ref, st_ref):
    task = pl.program_id(0)
    rows, cols = branch_ref.shape[1:3]
    center, inverse, gain, bias = task_norm(stat_ref, count_ref, meta_ref, norm_ref, task, 1)
    scale = inverse * gain
    shift = bias - center * scale
    attention = sigmoid(second_ref[0] * scale + shift)
    masked_ref[0] = (attention * pe_ref[...].astype(F32)).astype(BF16)
    z = taps_dot(masked_ref.at[0], w_ref.at[0], rows, cols, 0, False).reshape(branch_ref.shape[1:])
    branch_ref[0] = z
    zm = keep(mask_of(ext_ref, 0, 0, rows, cols), z)
    local = centered(sums_of(zm, zm * z), meta_ref[5:7])
    st_ref[:, 0] = jnp.broadcast_to(local[None], (st_ref.shape[0],) + st_ref.shape[2:])


def branch_grad_terms(branch_ref, cot_ref, stat_ref, count_ref, meta_ref, norm_ref, ext_ref, task):
    rows, cols = branch_ref.shape[1:3]
    center, inverse, gain, bias = task_norm(stat_ref, count_ref, meta_ref, norm_ref, task, 2)
    zhat = (branch_ref[0] - center) * inverse
    v = zhat * gain + bias
    s = sigmoid(v)
    inside = mask_of(ext_ref, 0, 0, rows, cols)
    c = cot_ref[0].astype(F32) * (0.25 * meta_ref[2:3])
    spread = jnp.broadcast_to(c[:, None, :, None], (rows // 2, 2, cols // 2, 2) + c.shape[2:])
    upstream = keep(inside, spread.reshape(v.shape) * (s * (1.0 + v * (1.0 - s))))
    return zhat, v, s, inside, upstream, gain * inverse


def result_kernel(branch_ref, cot_ref, stat_ref, count_ref, meta_ref, norm_ref, ext_ref, out_ref, st_ref):
    task = pl.program_id(0)
    rows, cols = branch_ref.shape[1:3]
    zhat, v, s, inside, upstream, _ = branch_grad_terms(
        branch_ref, cot_ref, stat_ref, count_ref, meta_ref, norm_ref, ext_ref, task
    )
    active = keep(inside, v * s)
    grouped = active.reshape((rows // 2, 2, cols // 2, 2) + active.shape[2:])
    mean = 0.25 * (
        (grouped[:, 0, :, 0] + grouped[:, 0, :, 1]) + (grouped[:, 1, :, 0] + grouped[:, 1, :, 1])
    )
    out_ref[0] = mean.astype(BF16)
    st_ref[:, 0] = jnp.broadcast_to(
        sums_of(upstream, upstream * zhat).astype(BF16)[None], (st_ref.shape[0],) + st_ref.shape[2:]
    )


def back_sums(stat_ref, inv_count):
    total = jnp.sum(stat_ref[:, 0].astype(F32), axis=0)
    return total[0:1] * inv_count, total[1:2] * inv_count


def branch_dz_kernel(branch_ref, cot_ref, stat_ref, back_ref, count_ref, meta_ref, norm_ref, ext_ref, dz_ref):
    task = pl.program_id(0)
    zhat, v, s, inside, upstream, factor = branch_grad_terms(
        branch_ref, cot_ref, stat_ref, count_ref, meta_ref, norm_ref, ext_ref, task
    )
    bias_mean, gain_mean = back_sums(back_ref, meta_ref[1:2])
    dz_ref[0] = keep(inside, factor * (upstream - bias_mean - zhat * gain_mean)).astype(BF16)


def branch_dgrad_kernel(dz_ref, w_ref, second_ref, pooled_ref, stat_ref, count_ref, meta_ref, norm_ref, ga_ref, prod_ref, st_ref):
    task = pl.program_id(0)
    shape = pooled_ref.shape
    rows, cols = shape[:2]
    center, inverse, gain, bias = task_norm(stat_ref, count_ref, meta_ref, norm_ref, task, 1)
    grad = taps_dot(dz_ref.at[0], w_ref.at[0], rows, cols, 0, True).reshape(shape)
    zhat = (second_ref[0, 1 : 1 + rows, 1 : 1 + cols] - center) * inverse
    attention = sigmoid(zhat * gain + bias)
    through = grad * attention
    ga = through * pooled_ref[...].astype(F32) * (1.0 - attention)
    ga_ref[0] = ga

    @pl.when(task == 0)
    def _():
        prod_ref[...] = through

    @pl.when(task > 0)
    def _():
        prod_ref[...] += through

    st_ref[:, 0] = jnp.broadcast_to(sums_of(ga, ga * zhat).astype(BF16)[None], (st_ref.shape[0],) + st_ref.shape[2:])


def scatter_tap(out_ref, task, tap, total):
    quarters, piece = out_ref.shape[0], out_ref.shape[4]
    channels = total.shape[0]
    at, end = tap * channels, (tap + 1) * channels
    while at < end:
        block, inside = at // piece, at % piece
        size = min(piece - inside, end - at)
        shard, quarter = block // quarters, block % quarters
        out_ref[quarter, shard // 2, task, shard % 2, inside : inside + size] = total[
            at - tap * channels : at - tap * channels + size
        ]
        at += size


def branch_wgrad_kernel(own_ref, other_ref, dz_own_ref, dz_other_ref, out_ref):
    rows, cols = dz_own_ref.shape[1:3]
    own = flat(dz_own_ref[0])
    other = flat(dz_other_ref[0])
    for tap in range(9):
        dr, dc = tap // 3, tap % 3
        total = dot_tn(flat(own_ref[0, dr : dr + rows, dc : dc + cols]), own)
        total += dot_tn(flat(other_ref[0, dr : dr + rows, dc : dc + cols]), other)
        scatter_tap(out_ref, 0, tap, total.astype(BF16))


def attend_back_kernel(ga_ref, second_ref, stat2_ref, back_ref, hidden_ref, p2_ref, first_ref, stat1_ref, count_ref, meta_ref, norm_ref, ext_ref, wg_ref, gl_ref, st_ref):
    task = pl.program_id(0)
    shape = ga_ref.shape[1:]
    rows, cols = shape[:2]
    center, inverse, gain, _ = task_norm(stat2_ref, count_ref, meta_ref, norm_ref, task, 1)
    zhat = (second_ref[0, 1 : 1 + rows, 1 : 1 + cols] - center) * inverse
    bias_mean, gain_mean = back_sums(back_ref, meta_ref[1:2])
    inside = mask_of(ext_ref, 0, 0, rows, cols)
    dz = keep(inside, gain * inverse * (ga_ref[0] - bias_mean - zhat * gain_mean)).astype(BF16)
    wg_ref[0] = dot_tn(flat(hidden_ref[0]), flat(dz)).astype(BF16)
    grad_hidden = dot_nt(flat(dz), p2_ref[0]).reshape(shape)
    center, inverse, gain, bias = task_norm(stat1_ref, count_ref, meta_ref, norm_ref, task, 0)
    zhat = (first_ref[0] - center) * inverse
    v = zhat * gain + bias
    s = sigmoid(v)
    gl = keep(inside, grad_hidden * (s * (1.0 + v * (1.0 - s))))
    gl_ref[0] = gl
    st_ref[:, 0] = jnp.broadcast_to(sums_of(gl, gl * zhat).astype(BF16)[None], (st_ref.shape[0],) + st_ref.shape[2:])


def unpool(grad, rows, cols):
    spread = jnp.broadcast_to(grad[:, None, :, None], (rows // 2, 2, cols // 2, 2) + grad.shape[2:])
    return spread.reshape((rows, cols) + grad.shape[2:])


def shared_grad_terms(z, grad, center, inverse, gain, bias, inside):
    zhat = (z - center) * inverse
    v = zhat * gain + bias
    s = sigmoid(v)
    upstream = keep(inside, unpool(0.25 * grad, z.shape[0], z.shape[1]) * (s * (1.0 + v * (1.0 - s))))
    return zhat, upstream


def pooled_back_kernel(chunk, gl_ref, first_ref, stat1_ref, back_ref, pooled_ref, p1_ref, prod_ref, z_ref, stat0_ref, count_ref, meta_ref, norm_ref, ext_ref, full_ref, wg_ref, gp_ref, st_ref):
    task = pl.program_id(0)
    shape = gl_ref.shape[1:]
    rows, cols = shape[:2]
    center, inverse, gain, _ = task_norm(stat1_ref, count_ref, meta_ref, norm_ref, task, 0)
    zhat = (first_ref[0] - center) * inverse
    bias_mean, gain_mean = back_sums(back_ref, meta_ref[1:2])
    inside = mask_of(ext_ref, 0, 0, rows, cols)
    dz = keep(inside, gain * inverse * (gl_ref[0] - bias_mean - zhat * gain_mean)).astype(BF16)
    wg_ref[0] = dot_tn(flat(pooled_ref[...]), flat(dz)).astype(BF16)
    grad = dot_nt(flat(dz), p1_ref[0]).reshape(shape)

    @pl.when(task == 0)
    def _():
        gp_ref[...] = prod_ref[...] + grad

    @pl.when(task > 0)
    def _():
        gp_ref[...] += grad

    @pl.when(task == pl.num_programs(0) - 1)
    def _():
        center, inverse = moments(stat0_ref[...], count_ref[0], meta_ref[0:1])
        gain, bias = norm_ref[0, 0:1], norm_ref[1, 0:1]
        full_rows, full_cols = z_ref.shape[:2]

        def body(i, total):
            row = i * chunk
            inside = mask_of(full_ref, row, 0, chunk, full_cols)
            zhat, upstream = shared_grad_terms(
                z_ref[pl.ds(row, chunk)], gp_ref[pl.ds(i * (chunk // 2), chunk // 2)],
                center, inverse, gain, bias, inside,
            )
            return total + sums_of(upstream, upstream * zhat)

        total = lax.fori_loop(0, full_rows // chunk, body, jnp.zeros((2, st_ref.shape[2]), F32))
        st_ref[...] = jnp.broadcast_to(total.astype(BF16)[None], st_ref.shape)


def shared_dz_kernel(rows, z_ref, gp_ref, stat_ref, back_ref, count_ref, meta_ref, norm_ref, ext_ref, dz_ref):
    step = pl.program_id(0)
    cols = z_ref.shape[1]
    center, inverse = moments(stat_ref[...], count_ref[0], meta_ref[0:1])
    gain, bias = norm_ref[0, 0:1], norm_ref[1, 0:1]
    total = jnp.sum(back_ref[...].astype(F32), axis=0) * meta_ref[0:1]
    inside = mask_of(ext_ref, step * rows, 0, rows, cols)
    zhat, upstream = shared_grad_terms(z_ref[...], gp_ref[...], center, inverse, gain, bias, inside)
    dz = gain * inverse * (upstream - total[0:1] - zhat * total[1:2])
    dz_ref[...] = keep(inside, dz).astype(BF16)


def shared_wgrad_kernel(own_ref, other_ref, dz_own_ref, dz_other_ref, out_ref):
    turn = pl.program_id(0)
    rows, cols = dz_own_ref.shape[:2]
    own = flat(dz_own_ref[...])
    other = flat(dz_other_ref[...])
    for tap in range(9):

        @pl.when(turn == tap)
        def _():
            dr, dc = tap // 3, tap % 3
            total = dot_tn(flat(own_ref[dr : dr + rows, dc : dc + cols]), own)
            total += dot_tn(flat(other_ref[dr : dr + rows, dc : dc + cols]), other)
            scatter_tap(out_ref, 0, tap, total.astype(BF16))


def shared_dgrad_kernel(rows, place_ref, dz_ref, ext_ref, *refs):
    *pieces, out_ref, w_ref, sem = refs
    gathered(place_ref, pieces, w_ref, sem)
    step = pl.program_id(0)
    cols = out_ref.shape[1]
    grad = taps_dot(dz_ref, w_ref, rows, cols, step * rows, True).reshape(out_ref.shape)
    out_ref[...] = keep(mask_of(ext_ref, step * rows, 0, rows, cols), grad)


def whole(shape):
    return pl.BlockSpec(shape, lambda i: (0,) * len(shape))


def leading(shape):
    return pl.BlockSpec(shape, lambda i: (i,) + (0,) * (len(shape) - 1))


def second_dim(shape):
    return pl.BlockSpec(shape, lambda i: (0, i) + (0,) * (len(shape) - 2))


def call(kernel, grid, ins, outs, scratch=(), flops=0):
    arrays = [array for array, _ in ins]
    moved = sum(a.size * a.dtype.itemsize for a in arrays)
    moved += sum(s.size * s.dtype.itemsize for s, _ in outs)
    return pl.pallas_call(
        kernel,
        grid=(grid,),
        in_specs=[spec for _, spec in ins],
        out_specs=[spec for _, spec in outs],
        out_shape=[shape for shape, _ in outs],
        scratch_shapes=list(scratch),
        compiler_params=pltpu.CompilerParams(vmem_limit_bytes=VMEM_LIMIT),
        cost_estimate=pl.CostEstimate(flops=flops, bytes_accessed=moved, transcendentals=0),
    )(*arrays)


def shape_of(shape, dtype):
    return jax.ShapeDtypeStruct(shape, dtype)


def shift_cols(array, step):
    chips, cores = lax.axis_size("chips"), lax.axis_size("core")
    total = chips * cores
    pairs = [(i, i + step) for i in range(total) if 0 <= i + step < total]
    return lax.ppermute(array, ("chips", "core"), pairs)


def shift_rows(array, step):
    total = lax.axis_size("rows")
    pairs = [(i, i + step) for i in range(total) if 0 <= i + step < total]
    return lax.ppermute(array, "rows", pairs)


def rims(array, dim, shift):
    length = array.shape[dim]
    before = shift(lax.slice_in_dim(array, length - 1, length, axis=dim), 1)
    after = shift(lax.slice_in_dim(array, 0, 1, axis=dim), -1)
    return before, after


def joined(rim, array, dim):
    return jnp.concatenate([rim[0], array, rim[1]], axis=dim)


def extended(array, row_dim):
    array = joined(rims(array, row_dim, shift_rows), array, row_dim)
    return joined(rims(array, row_dim + 1, shift_cols), array, row_dim + 1)


def spread_all(stats):
    return lax.all_to_all(stats, EVERY, 0, 0)


def swap(array, axis, flip):
    total = lax.axis_size(axis)
    return lax.ppermute(array, axis, [(i, i ^ flip) for i in range(total)])


def spread_chips(shard):
    chips, rows = lax.axis_size("chips"), lax.axis_size("rows")
    width = shard.shape[-1] // rows
    mine = lax.dynamic_slice_in_dim(shard, lax.axis_index("rows") * width, width, axis=2)
    return [swap(mine, "chips", hop) for hop in range(1, chips)]


def spread_rows(shard, hops):
    line = jnp.stack(hops)
    return [shard, line] + [swap(line, "rows", flip) for flip in range(1, lax.axis_size("rows"))]


def spread_cores(pieces):
    return pieces + [swap(piece, "core", 1) for piece in pieces]


def gather_points(shard):
    groups, depth, channels = shard.shape
    part = depth // lax.axis_size("rows")
    mine = lax.dynamic_slice_in_dim(shard, lax.axis_index("rows") * part, part, axis=1)
    full = lax.all_gather(mine.astype(BF16), ("chips", "core", "rows"))
    return full.transpose(1, 0, 2, 3).reshape(groups, -1, channels)


def gather_weights(shard):
    rows = lax.axis_size("rows")
    part = shard.shape[1] // rows
    mine = lax.dynamic_slice_in_dim(shard, lax.axis_index("rows") * part, part, axis=1)
    return lax.all_gather(mine.astype(BF16), ("chips", "core", "rows"), axis=1, tiled=True)


def pick(array, axis, index):
    return lax.dynamic_index_in_dim(array, index, axis=axis, keepdims=False)


def summed(parts):
    total = parts[0].astype(F32)
    for part in parts[1:]:
        total = total + part.astype(F32)
    return total.astype(BF16)


def row_sends(parts):
    row = lax.axis_index("rows")
    return [pick(parts, 0, row ^ flip) for flip in range(lax.axis_size("rows"))]


def reduce_rows(sends):
    return [sends[0]] + [swap(part, "rows", flip) for flip, part in enumerate(sends) if flip]


def reduce_chips(parts):
    total = summed(parts)
    chip = lax.axis_index("chips")
    chips = lax.axis_size("chips")
    return [pick(total, 0, chip)] + [
        swap(pick(total, 0, chip ^ hop), "chips", hop) for hop in range(1, chips)
    ]


def share_rows(parts):
    total = summed(parts)
    core = lax.axis_index("core")
    kept = pick(total, 1, core)
    got = swap(pick(total, 1, 1 - core), "core", 1)
    low = jnp.where(core == 0, kept, got)
    high = jnp.where(core == 0, got, kept)
    share = jnp.concatenate([low, high], axis=-1)
    return [share] + [swap(share, "rows", flip) for flip in range(1, lax.axis_size("rows"))]


def update_kernel(rate, count, place_ref, weight_ref, moment_ref, average_ref, *refs):
    parts, outs = refs[:count], refs[-4:]
    turn = pl.program_id(1)
    for flip, part in enumerate(parts):

        @pl.when(turn == flip)
        def _():
            grad = part[...].astype(F32)[:, None]
            weight = weight_ref[...]
            descent = grad + WEIGHT_DECAY * weight
            mom_new = MOMENTUM * moment_ref[...] + descent
            weight_new = weight - rate * (descent + MOMENTUM * mom_new)
            outs[0][...] = grad
            outs[1][...] = mom_new
            outs[2][...] = weight_new
            outs[3][...] = AVERAGE * average_ref[...] + (1.0 - AVERAGE) * weight_new


def update(parts, weight, moment, average, rate, first, block, earlier=()):
    groups, depth, channels = weight.shape
    rows = lax.axis_size("rows")
    piece = depth // rows
    count = parts[0].shape[0]
    split = (groups, rows, piece, channels)
    weight, moment, average = (a.reshape(split) for a in (weight, moment, average))
    earlier = [a.reshape(split) for a in earlier]
    state = pl.BlockSpec(
        (block, 1, piece, channels), lambda g, t, p: (g + first // block, jnp.bitwise_xor(p[2], t), 0, 0)
    )
    grads = pl.BlockSpec((block, piece, channels), lambda g, t, p: (g, 0, 0))
    anywhere = pl.BlockSpec(memory_space=pl.ANY)
    outs = pl.pallas_call(
        functools.partial(update_kernel, rate, len(parts)),
        grid_spec=pltpu.PrefetchScalarGridSpec(
            num_scalar_prefetch=1,
            grid=(count // block, rows),
            in_specs=[state] * 3 + [grads] * len(parts) + [anywhere] * len(earlier),
            out_specs=[state] * 4,
        ),
        out_shape=[jax.ShapeDtypeStruct(split, F32)] * 4,
        input_output_aliases={4 + len(parts) + i: i for i in range(len(earlier))},
        compiler_params=pltpu.CompilerParams(vmem_limit_bytes=VMEM_LIMIT),
        cost_estimate=pl.CostEstimate(
            flops=0, bytes_accessed=30 * count * depth * channels, transcendentals=0
        ),
    )(place_of(), weight, moment, average, *parts, *earlier)
    return [a.reshape(groups, depth, channels) for a in outs]


def place_of():
    place = jnp.stack([lax.axis_index("chips"), lax.axis_index("core"), lax.axis_index("rows")])
    return place.astype(jnp.int32)


def halves(array):
    core = lax.axis_index("core")
    half = array.shape[-1] // 2
    mine = lax.dynamic_slice_in_dim(array, core * half, half, axis=array.ndim - 1)
    other = lax.dynamic_slice_in_dim(array, (1 - core) * half, half, axis=array.ndim - 1)
    return mine, lax.ppermute(other, "core", PAIR)


def refresh(weight, gradient, moment, average, step_rate):
    descent = gradient + WEIGHT_DECAY * weight
    mom_new = MOMENTUM * moment + descent
    weight_new = weight - step_rate * (descent + MOMENTUM * mom_new)
    avg_new = AVERAGE * average + (1.0 - AVERAGE) * weight_new
    return (mom_new, weight_new, avg_new)


def shards(
    features,
    extent,
    cotangent,
    wide_w,
    wide_mom,
    wide_avg,
    point_w,
    point_mom,
    point_avg,
    norm_w,
    norm_mom,
    norm_avg,
):
    tasks = point_w.shape[0] // 2
    images, rows, cols, channels = features.shape
    half_rows, half_cols = rows // 2, cols // 2
    rate_wide = 0.4 / (9.0 * channels) ** 0.5
    rate_point = 2.0 / float(channels) ** 0.5
    devices = lax.axis_size("rows") * lax.axis_size("chips") * lax.axis_size("core")
    row_start = lax.axis_index("rows") * rows
    col_start = (lax.axis_index("chips") * lax.axis_size("core") + lax.axis_index("core")) * cols
    starts = jnp.stack([row_start, col_start]).astype(jnp.int32)[:, None]
    full_ext = jnp.broadcast_to((extent - starts)[:, :, None], (2, images, channels))
    half_ext = jnp.broadcast_to((extent // 2 - starts // 2)[:, :, None], (2, images, channels))
    full_count = jnp.sum(extent[0] * extent[1]).astype(F32)
    all_rows = jnp.arange(lax.axis_size("rows"), dtype=jnp.int32)[:, None, None] * rows
    all_cols = jnp.arange(devices // lax.axis_size("rows"), dtype=jnp.int32)[None, :, None] * cols
    valid = jnp.clip(extent[0] - all_rows, 0, rows) * jnp.clip(extent[1] - all_cols, 0, cols)
    counts = jnp.sum(valid, axis=2).astype(F32).reshape(devices)
    own_count = jnp.sum(
        jnp.clip(extent[0] - row_start, 0, rows) * jnp.clip(extent[1] - col_start, 0, cols)
    ).astype(F32)
    own_inv = 1.0 / jnp.maximum(own_count, 1.0)
    meta = jnp.broadcast_to(
        jnp.stack(
            [
                1.0 / full_count,
                4.0 / full_count,
                lax.rsqrt(full_count / 16.0),
                own_count,
                own_inv,
                0.25 * own_count,
                4.0 * own_inv,
            ]
        )[:, None],
        (7, channels),
    )
    counts = jnp.broadcast_to(
        jnp.stack([counts, 0.25 * counts])[:, :, None, None], (2, devices, 1, channels)
    )
    place = place_of()
    shared_own = wide_w[:1].astype(BF16)
    hops = spread_chips(shared_own)
    features, hops = lax.optimization_barrier((features, hops))
    pieces = spread_rows(shared_own, hops)
    point_full = gather_points(point_w)
    first_w, second_w = point_full[:tasks], point_full[tasks:]

    maps = features.transpose(1, 2, 0, 3)
    row_ids = jnp.arange(rows, dtype=jnp.int32)[:, None, None]
    col_ids = jnp.arange(cols, dtype=jnp.int32)[None, :, None]
    inside = (row_ids < (extent[0] - row_start)[None, None]) & (col_ids < (extent[1] - col_start)[None, None])
    maps = jnp.where(inside[..., None], maps, jnp.zeros((), BF16))
    x_pad = extended(maps, 0)
    pieces, x_pad = lax.optimization_barrier((pieces, x_pad))
    later_w, _ = lax.optimization_barrier((wide_w[1:], pieces))
    branch_w = gather_weights(later_w)
    branch_in = (branch_w, leading((1,) + branch_w.shape[1:]))
    pieces = spread_cores(pieces)
    x_other = lax.ppermute(x_pad, "core", PAIR)
    cot = cotangent.transpose(0, 2, 3, 1, 4)

    full = (rows, cols, images, channels)
    half = (half_rows, half_cols, images, channels)
    wide = (half_rows + 2, half_cols + 2, images, channels)
    quarter = (half_rows // 2, half_cols // 2, images, channels)
    stat = (devices, 2, channels)
    task_stat = (devices, tasks, 2, channels)
    one_stat = second_dim((devices, 1, 2, channels))
    meta_in = (meta, whole(meta.shape))
    count_in = (counts, whole(counts.shape))
    norm_in = (norm_w, whole(norm_w.shape))
    full_in = (full_ext, whole(full_ext.shape))
    half_in = (half_ext, whole(half_ext.shape))
    vec = pltpu.VMEM((2, channels), F32)
    place_in = (place, pl.BlockSpec(memory_space=pltpu.SMEM))
    anywhere = pl.BlockSpec(memory_space=pl.ANY)
    copies = 2 * (1 + lax.axis_size("rows") * (lax.axis_size("chips") - 1))

    def weight_room(slots):
        shape = (slots, 9 * channels, channels) if slots > 1 else (9 * channels, channels)
        return [pltpu.VMEM(shape, BF16), pltpu.SemaphoreType.DMA((slots, copies))]

    full_flops = 2 * 9 * rows * cols * images * channels * channels
    half_flops = full_flops // 4 * tasks
    task_of = lambda shape: leading((1,) + shape)

    block = 4
    z, local = call(
        functools.partial(shared_fwd_kernel, block),
        rows // block,
        [place_in, (x_pad, whole(x_pad.shape)), meta_in, full_in] + [(p, anywhere) for p in pieces],
        [(shape_of(full, F32), leading((block,) + full[1:])), (shape_of(stat, BF16), whole(stat))],
        [vec] + weight_room(1),
        full_flops,
    )
    stat0 = spread_all(local)

    pooled, local = call(
        functools.partial(pool_kernel, block),
        rows // block,
        [
            (z, leading((block,) + full[1:])),
            (stat0, whole(stat)),
            count_in,
            meta_in,
            norm_in,
            full_in,
            (first_w, whole(first_w.shape)),
        ],
        [
            (shape_of(half, BF16), leading((block // 2,) + half[1:])),
            (shape_of(task_stat, BF16), whole(task_stat)),
        ],
        [pltpu.VMEM(half, BF16), vec],
    )
    pooled_wide = extended(pooled, 0)
    stat1 = spread_all(local)

    first, hidden, second, local = call(
        attend_kernel,
        tasks,
        [
            (pooled_wide, whole(wide)),
            (stat1, one_stat),
            count_in,
            meta_in,
            norm_in,
            half_in,
            (first_w, task_of(first_w.shape[1:])),
            (second_w, task_of(second_w.shape[1:])),
        ],
        [
            (shape_of((tasks,) + half, F32), task_of(half)),
            (shape_of((tasks,) + half, BF16), task_of(half)),
            (shape_of((tasks,) + wide, F32), task_of(wide)),
            (shape_of(task_stat, BF16), one_stat),
        ],
    )
    stat2 = spread_all(local)

    masked, branch, local = call(
        branch_fwd_kernel,
        tasks,
        [
            (second, task_of(wide)),
            (pooled_wide, whole(wide)),
            (stat2, one_stat),
            count_in,
            meta_in,
            norm_in,
            half_in,
            branch_in,
        ],
        [
            (shape_of((tasks,) + wide, BF16), task_of(wide)),
            (shape_of((tasks,) + half, F32), task_of(half)),
            (shape_of(task_stat, BF16), one_stat),
        ],
        flops=half_flops,
    )
    masked_other = lax.ppermute(masked, "core", PAIR)
    stat3 = spread_all(local)

    branch_ins = [
        (branch, task_of(half)),
        (cot, task_of(quarter)),
        (stat3, one_stat),
    ]
    result, local = call(
        result_kernel,
        tasks,
        branch_ins + [count_in, meta_in, norm_in, half_in],
        [
            (shape_of((tasks,) + quarter, BF16), task_of(quarter)),
            (shape_of(task_stat, BF16), one_stat),
        ],
    )
    back3 = spread_all(local)

    (branch_dz,) = call(
        branch_dz_kernel,
        tasks,
        branch_ins + [(back3, one_stat), count_in, meta_in, norm_in, half_in],
        [(shape_of((tasks,) + half, BF16), task_of(half))],
    )
    dz_own, dz_other = halves(branch_dz)
    dz_tall = joined(rims(branch_dz, 1, shift_rows), branch_dz, 1)
    dz_rim = rims(dz_tall, 2, shift_cols)
    narrow = half[:-1] + (channels // 2,)
    chips, quarters = lax.axis_size("chips"), lax.axis_size("rows")
    piece = 9 * channels // (2 * chips * quarters)
    (branch_grad,) = call(
        branch_wgrad_kernel,
        tasks,
        [
            (masked, task_of(wide)),
            (masked_other, task_of(wide)),
            (dz_own, task_of(narrow)),
            (dz_other, task_of(narrow)),
        ],
        [
            (
                shape_of((quarters, chips, tasks, 2, piece, channels // 2), BF16),
                pl.BlockSpec(
                    (quarters, chips, 1, 2, piece, channels // 2), lambda i: (0, 0, i, 0, 0, 0)
                ),
            )
        ],
        flops=half_flops,
    )
    branch_grad, dz_rim = lax.optimization_barrier((branch_grad, dz_rim))
    branch_parts = lax.psum_scatter(branch_grad, "rows", scatter_dimension=0, tiled=True)[0]
    dz_wide = joined(dz_rim, dz_tall, 2)

    ga, product, local = call(
        branch_dgrad_kernel,
        tasks,
        [
            (dz_wide, task_of(wide)),
            branch_in,
            (second, task_of(wide)),
            (pooled, whole(half)),
            (stat2, one_stat),
            count_in,
            meta_in,
            norm_in,
        ],
        [
            (shape_of((tasks,) + half, F32), task_of(half)),
            (shape_of(half, F32), whole(half)),
            (shape_of(task_stat, BF16), one_stat),
        ],
        flops=half_flops,
    )
    back2 = spread_all(local)

    square = (channels, channels)
    second_grad, gl, local = call(
        attend_back_kernel,
        tasks,
        [
            (ga, task_of(half)),
            (second, task_of(wide)),
            (stat2, one_stat),
            (back2, one_stat),
            (hidden, task_of(half)),
            (second_w, task_of(square)),
            (first, task_of(half)),
            (stat1, one_stat),
            count_in,
            meta_in,
            norm_in,
            half_in,
        ],
        [
            (shape_of((tasks,) + square, BF16), task_of(square)),
            (shape_of((tasks,) + half, F32), task_of(half)),
            (shape_of(task_stat, BF16), one_stat),
        ],
    )
    back1 = spread_all(local)

    first_grad, grad_pooled, local = call(
        functools.partial(pooled_back_kernel, block),
        tasks,
        [
            (gl, task_of(half)),
            (first, task_of(half)),
            (stat1, one_stat),
            (back1, one_stat),
            (pooled, whole(half)),
            (first_w, task_of(square)),
            (product, whole(half)),
            (z, whole(full)),
            (stat0, whole(stat)),
            count_in,
            meta_in,
            norm_in,
            half_in,
            full_in,
        ],
        [
            (shape_of((tasks,) + square, BF16), task_of(square)),
            (shape_of(half, F32), whole(half)),
            (shape_of(stat, BF16), whole(stat)),
        ],
    )
    back0 = spread_all(local)
    point_local = jnp.concatenate([first_grad, second_grad], axis=0)
    point_own, point_other = halves(point_local)
    point_half, back0 = lax.optimization_barrier((point_own + point_other, back0))
    point_split = (2 * tasks, chips, 2, quarters, channels // (2 * chips * quarters), channels // 2)
    point_parts = reduce_rows(row_sends(point_half.reshape(point_split).transpose(3, 1, 0, 2, 4, 5)))

    (shared_dz,) = call(
        functools.partial(shared_dz_kernel, block),
        rows // block,
        [
            (z, leading((block,) + full[1:])),
            (grad_pooled, leading((block // 2,) + half[1:])),
            (stat0, whole(stat)),
            (back0, whole(stat)),
            count_in,
            meta_in,
            norm_in,
            full_in,
        ],
        [(shape_of(full, BF16), leading((block,) + full[1:]))],
    )
    branch_parts, shared_dz = lax.optimization_barrier((branch_parts, shared_dz))
    branch_parts = lax.psum_scatter(branch_parts, "chips", scatter_dimension=0, tiled=True)
    dz_own, dz_other = halves(shared_dz)
    dz_rim = rims(shared_dz, 0, shift_rows)
    (shared_grad,) = call(
        shared_wgrad_kernel,
        9,
        [
            (x_pad, whole(x_pad.shape)),
            (x_other, whole(x_other.shape)),
            (dz_own, whole(dz_own.shape)),
            (dz_other, whole(dz_other.shape)),
        ],
        [
            (
                shape_of((quarters, chips, 1, 2, piece, channels // 2), BF16),
                whole((quarters, chips, 1, 2, piece, channels // 2)),
            )
        ],
        flops=full_flops,
    )
    sends = row_sends(shared_grad)
    point_parts, sends, dz_rim = lax.optimization_barrier((point_parts, sends, dz_rim))
    branch_parts, _ = lax.optimization_barrier((branch_parts, sends))
    shared_parts = reduce_rows(sends)
    dz_tall = joined(dz_rim, shared_dz, 0)
    dz_pad = joined(rims(dz_tall, 1, shift_cols), dz_tall, 1)
    point_parts = reduce_chips(point_parts)
    (input_grad,) = call(
        functools.partial(shared_dgrad_kernel, block),
        rows // block,
        [place_in, (dz_pad, whole(dz_pad.shape)), full_in] + [(p, anywhere) for p in pieces],
        [(shape_of(full, F32), leading((block,) + full[1:]))],
        weight_room(1),
        full_flops,
    )
    branch_share = share_rows(branch_parts)
    shared_parts, point_parts, input_grad = lax.optimization_barrier(
        (shared_parts, point_parts, input_grad)
    )
    shared_parts = reduce_chips(shared_parts)
    point_share = share_rows(point_parts)
    branch_share, _ = lax.optimization_barrier((branch_share, input_grad))
    branch_state = update(branch_share, wide_w, wide_mom, wide_avg, rate_wide, 1, 1)
    shared_parts, branch_state, input_grad = lax.optimization_barrier(
        (shared_parts, branch_state, input_grad)
    )
    shared_share = share_rows(shared_parts)
    input_grad = input_grad.transpose(2, 0, 1, 3)
    point_state = update(point_share, point_w, point_mom, point_avg, rate_point, 0, 2 * tasks)
    shared_share, point_state, input_grad = lax.optimization_barrier(
        (shared_share, point_state, input_grad)
    )
    point_share, point_mom_new, point_new, point_avg_new = point_state

    wide_share, wide_mom_new, wide_new, wide_avg_new = update(
        shared_share, wide_w, wide_mom, wide_avg, rate_wide, 0, 1, branch_state
    )
    bsum = jnp.stack([jnp.sum(b.astype(F32), axis=0) for b in (back1, back2, back3)], axis=1)
    bsum = bsum.transpose(2, 0, 1, 3).reshape(2, 3 * tasks, channels)
    norm_grad = jnp.concatenate([jnp.sum(back0.astype(F32), axis=0)[:, None], bsum], axis=1)[::-1]
    norm_mom_new, norm_new, norm_avg_new = refresh(norm_w, norm_grad, norm_mom, norm_avg, RATE_NORM)
    return (
        result.transpose(0, 3, 1, 2, 4),
        input_grad,
        wide_share,
        wide_mom_new,
        wide_new,
        wide_avg_new,
        point_share,
        point_mom_new,
        point_new,
        point_avg_new,
        norm_grad,
        norm_mom_new,
        norm_new,
        norm_avg_new,
    )


def solution(mesh):
    rows, cols = mesh.devices.shape
    cores = 2
    fine = Mesh(mesh.devices.reshape(rows, cols // cores, cores), EVERY)
    across = ("chips", "core")
    weights = P(None, across, None)
    placed = (
        P(None, "rows", across, None),
        P(),
        P(None, None, "rows", across, None),
        weights,
        weights,
        weights,
        weights,
        weights,
        weights,
        P(),
        P(),
        P(),
    )
    return jax.shard_map(
        shards,
        mesh=fine,
        in_specs=placed,
        out_specs=(
            P(None, None, "rows", across, None),
            P(None, "rows", across, None),
            weights,
            weights,
            weights,
            weights,
            weights,
            weights,
            weights,
            weights,
            P(),
            P(),
            P(),
            P(),
        ),
        check_vma=False,
    )
```

```python
import functools

import jax
import jax.numpy as jnp
from jax import lax
from jax.experimental import pallas as pl
from jax.experimental.pallas import tpu as pltpu
from jax.sharding import Mesh
from jax.sharding import PartitionSpec as P

EPSILON = 1e-05
MOMENTUM = 0.9
WEIGHT_DECAY = 0.0001
AVERAGE = 0.6
RATE_NORM = 0.4
F32 = jnp.float32
BF16 = jnp.bfloat16
EVERY = ("rows", "chips", "core")
PAIR = [(0, 1), (1, 0)]
VMEM_LIMIT = 56 * 1024 * 1024


def sigmoid(values):
    return 0.5 * jnp.tanh(0.5 * values) + 0.5


def flat(values):
    return values.reshape((-1, values.shape[-1]))


def square_of(ref):
    return ref[...].reshape(ref.shape[-1], ref.shape[-1])


def mask_of(ext_ref, row, col, rows, cols):
    shape = (rows, cols) + ext_ref.shape[1:]
    row_ids = row + lax.broadcasted_iota(jnp.int32, shape, 0)
    col_ids = col + lax.broadcasted_iota(jnp.int32, shape, 1)
    inside = (row_ids < ext_ref[0][None, None]) & (col_ids < ext_ref[1][None, None])
    return inside


def keep(inside, values):
    return jnp.where(inside, values, 0.0)


def sums_of(first, second):
    return jnp.concatenate(
        [jnp.sum(flat(first), axis=0, keepdims=True), jnp.sum(flat(second), axis=0, keepdims=True)],
        axis=0,
    )


def centered(sums, local):
    center = (sums[0:1] * local[1:2]).astype(BF16)
    wide = center.astype(F32)
    spread = sums[1:2] - 2.0 * wide * sums[0:1] + local[0:1] * wide * wide
    return jnp.concatenate([wide, spread], axis=0).astype(BF16)


def moments(stats, counts, inv_count):
    stats = stats.astype(F32)
    centers = stats[:, 0:1]
    center = jnp.sum(counts * centers, axis=0) * inv_count
    off = centers - center[None]
    spread = jnp.sum(stats[:, 1:2] + counts * off * off, axis=0) * inv_count
    return center, lax.rsqrt(spread + EPSILON)


def taps_dot(source, weight, rows, cols, row, mirrored):
    channels = weight.shape[-1]
    total = None
    for tap in range(9):
        dr, dc = tap // 3, tap % 3
        if mirrored:
            dr, dc = 2 - dr, 2 - dc
        window = flat(source[pl.ds(row + dr, rows), dc : dc + cols])
        block = weight[tap * channels : (tap + 1) * channels, :]
        dims = (((1,), (1,)), ((), ())) if mirrored else (((1,), (0,)), ((), ()))
        part = lax.dot_general(window, block, dims, preferred_element_type=F32)
        total = part if total is None else total + part
    return total


def dot(left, right):
    return jnp.dot(left, right, preferred_element_type=F32)


def dot_nt(left, right):
    return lax.dot_general(left, right, (((1,), (1,)), ((), ())), preferred_element_type=F32)


def dot_tn(left, right):
    return lax.dot_general(left, right, (((0,), (0,)), ((), ())), preferred_element_type=F32)


def assemble(place_ref, pieces, w_ref, point_ref, sem, start):
    chip, core, row = place_ref[0], place_ref[1], place_ref[2]
    half = len(pieces) // 2
    depth = w_ref.shape[0] // point_ref.shape[0]
    count = 0
    for side in range(2):
        own, parts = pieces[side * half], pieces[side * half + 1 : (side + 1) * half]
        width = parts[0].shape[-1]
        at_core = core if side == 0 else 1 - core

        def run(source, shard, lanes, at):
            base = pl.multiple_of(shard * depth, 16)
            rest = source.shape[0] - depth
            pairs = (
                (source.at[pl.ds(0, depth)], w_ref.at[pl.ds(base, depth), lanes]),
                (source.at[pl.ds(depth, rest)], point_ref.at[shard, :, lanes]),
            )
            for i, (left, right) in enumerate(pairs):
                copy = pltpu.make_async_copy(left, right, sem.at[at + i])
                copy.start() if start else copy.wait()

        run(own, 2 * chip + at_core, pl.ds(0, own.shape[1]), count)
        count += 2
        for flip, part in enumerate(parts):
            lane = pl.multiple_of(jnp.bitwise_xor(row, flip) * width, 128)
            for hop in range(part.shape[0]):
                shard = 2 * jnp.bitwise_xor(chip, hop + 1) + at_core
                run(part.at[hop], shard, pl.ds(lane, width), count)
                count += 2


def gathered(place_ref, pieces, w_ref, point_ref, sem, w_out, point_out, out_sem):
    copies = (
        pltpu.make_async_copy(w_ref, w_out, out_sem.at[0]),
        pltpu.make_async_copy(point_ref, point_out, out_sem.at[1]),
    )

    @pl.when(pl.program_id(0) == 0)
    def _():
        assemble(place_ref, pieces, w_ref, point_ref, sem, True)
        assemble(place_ref, pieces, w_ref, point_ref, sem, False)
        for copy in copies:
            copy.start()

    @pl.when(pl.program_id(0) == pl.num_programs(0) - 1)
    def _():
        for copy in copies:
            copy.wait()


def shared_fwd_kernel(rows, place_ref, x_ref, meta_ref, ext_ref, *refs):
    *pieces, z_ref, stat_ref, w_out, point_out, acc_ref, w_ref, point_ref, sem, out_sem = refs
    gathered(place_ref, pieces, w_ref, point_ref, sem, w_out, point_out, out_sem)
    step = pl.program_id(0)
    cols = z_ref.shape[1]
    z = taps_dot(x_ref, w_ref, rows, cols, step * rows, False).reshape(z_ref.shape)
    z_ref[...] = z
    zm = keep(mask_of(ext_ref, step * rows, 0, rows, cols), z)
    part = sums_of(zm, zm * z)

    @pl.when(step == 0)
    def _():
        acc_ref[...] = part

    @pl.when(step > 0)
    def _():
        acc_ref[...] += part

    @pl.when(step == pl.num_programs(0) - 1)
    def _():
        stat_ref[...] = jnp.broadcast_to(centered(acc_ref[...], meta_ref[3:5])[None], stat_ref.shape)


def pool_kernel(rows, z_ref, stat_ref, count_ref, meta_ref, norm_ref, ext_ref, p_ref, out_ref, st_ref, pool_ref, aff_ref):
    step = pl.program_id(0)
    cols = z_ref.shape[1]

    @pl.when(step == 0)
    def _():
        center, inverse = moments(stat_ref[...], count_ref[0], meta_ref[0:1])
        scale = inverse * norm_ref[0, 0:1]
        aff_ref[0:1] = scale
        aff_ref[1:2] = norm_ref[1, 0:1] - center * scale

    v = z_ref[...] * aff_ref[0:1] + aff_ref[1:2]
    lifted = keep(mask_of(ext_ref, step * rows, 0, rows, cols), v * sigmoid(v))
    grouped = lifted.reshape((rows // 2, 2, cols // 2, 2) + lifted.shape[2:])
    mean = 0.25 * (
        (grouped[:, 0, :, 0] + grouped[:, 0, :, 1]) + (grouped[:, 1, :, 0] + grouped[:, 1, :, 1])
    )
    low = mean.astype(BF16)
    out_ref[...] = low
    pool_ref[pl.ds(step * (rows // 2), rows // 2)] = low

    @pl.when(step == pl.num_programs(0) - 1)
    def _():
        left = flat(pool_ref[...])
        channels = left.shape[-1]
        for task in range(p_ref.shape[1]):
            f = dot(left, p_ref[:, task].reshape(channels, channels))
            st_ref[:, task] = jnp.broadcast_to(
                centered(sums_of(f, f * f), meta_ref[5:7])[None], (st_ref.shape[0],) + st_ref.shape[2:]
            )


def task_norm(stat_ref, count_ref, meta_ref, norm_ref, task, slot):
    center, inverse = moments(stat_ref[:, 0], count_ref[1], meta_ref[1:2])
    row = 1 + 3 * task + slot
    gain = norm_ref[0, pl.ds(row, 1)]
    bias = norm_ref[1, pl.ds(row, 1)]
    return center, inverse, gain, bias


def attend_kernel(pe_ref, stat_ref, count_ref, meta_ref, norm_ref, ext_ref, p1_ref, p2_ref, first_ref, hidden_ref, second_ref, st_ref):
    task = pl.program_id(0)
    shape = pe_ref.shape
    rows, cols = shape[0] - 2, shape[1] - 2
    center, inverse, gain, bias = task_norm(stat_ref, count_ref, meta_ref, norm_ref, task, 0)
    scale = inverse * gain
    shift = bias - center * scale
    first = dot(flat(pe_ref[...]), square_of(p1_ref))
    first_ref[0] = first.reshape(shape)[1 : 1 + rows, 1 : 1 + cols]
    v = first * scale + shift
    inside = mask_of(ext_ref, -1, -1, rows + 2, cols + 2)
    hidden = keep(inside, (v * sigmoid(v)).reshape(shape)).astype(BF16)
    hidden_ref[0] = hidden[1 : 1 + rows, 1 : 1 + cols]
    second = dot(flat(hidden), square_of(p2_ref)).reshape(shape)
    second_ref[0] = second
    own = second[1 : 1 + rows, 1 : 1 + cols]
    local = centered(sums_of(own, own * own), meta_ref[5:7])
    st_ref[:, 0] = jnp.broadcast_to(local[None], (st_ref.shape[0],) + st_ref.shape[2:])


def branch_fwd_kernel(second_ref, pe_ref, stat_ref, count_ref, meta_ref, norm_ref, ext_ref, w_ref, masked_ref, branch_ref, st_ref):
    task = pl.program_id(0)
    rows, cols = branch_ref.shape[1:3]
    center, inverse, gain, bias = task_norm(stat_ref, count_ref, meta_ref, norm_ref, task, 1)
    scale = inverse * gain
    shift = bias - center * scale
    attention = sigmoid(second_ref[0] * scale + shift)
    masked_ref[0] = (attention * pe_ref[...].astype(F32)).astype(BF16)
    z = taps_dot(masked_ref.at[0], w_ref.at[0], rows, cols, 0, False).reshape(branch_ref.shape[1:])
    branch_ref[0] = z
    zm = keep(mask_of(ext_ref, 0, 0, rows, cols), z)
    local = centered(sums_of(zm, zm * z), meta_ref[5:7])
    st_ref[:, 0] = jnp.broadcast_to(local[None], (st_ref.shape[0],) + st_ref.shape[2:])


def branch_grad_terms(branch_ref, cot_ref, stat_ref, count_ref, meta_ref, norm_ref, ext_ref, task):
    rows, cols = branch_ref.shape[1:3]
    center, inverse, gain, bias = task_norm(stat_ref, count_ref, meta_ref, norm_ref, task, 2)
    zhat = (branch_ref[0] - center) * inverse
    v = zhat * gain + bias
    s = sigmoid(v)
    inside = mask_of(ext_ref, 0, 0, rows, cols)
    c = cot_ref[0].astype(F32) * (0.25 * meta_ref[2:3])
    spread = jnp.broadcast_to(c[:, None, :, None], (rows // 2, 2, cols // 2, 2) + c.shape[2:])
    upstream = keep(inside, spread.reshape(v.shape) * (s * (1.0 + v * (1.0 - s))))
    return zhat, v, s, inside, upstream, gain * inverse


def result_kernel(branch_ref, cot_ref, stat_ref, count_ref, meta_ref, norm_ref, ext_ref, out_ref, st_ref):
    task = pl.program_id(0)
    rows, cols = branch_ref.shape[1:3]
    zhat, v, s, inside, upstream, _ = branch_grad_terms(
        branch_ref, cot_ref, stat_ref, count_ref, meta_ref, norm_ref, ext_ref, task
    )
    active = keep(inside, v * s)
    grouped = active.reshape((rows // 2, 2, cols // 2, 2) + active.shape[2:])
    mean = 0.25 * (
        (grouped[:, 0, :, 0] + grouped[:, 0, :, 1]) + (grouped[:, 1, :, 0] + grouped[:, 1, :, 1])
    )
    out_ref[0] = mean.astype(BF16)
    st_ref[:, 0] = jnp.broadcast_to(
        sums_of(upstream, upstream * zhat).astype(BF16)[None], (st_ref.shape[0],) + st_ref.shape[2:]
    )


def back_sums(stat_ref, inv_count):
    total = jnp.sum(stat_ref[:, 0].astype(F32), axis=0)
    return total[0:1] * inv_count, total[1:2] * inv_count


def branch_dz_kernel(branch_ref, cot_ref, stat_ref, back_ref, count_ref, meta_ref, norm_ref, ext_ref, dz_ref):
    task = pl.program_id(0)
    zhat, v, s, inside, upstream, factor = branch_grad_terms(
        branch_ref, cot_ref, stat_ref, count_ref, meta_ref, norm_ref, ext_ref, task
    )
    bias_mean, gain_mean = back_sums(back_ref, meta_ref[1:2])
    dz_ref[0] = keep(inside, factor * (upstream - bias_mean - zhat * gain_mean)).astype(BF16)


def branch_dgrad_kernel(dz_ref, w_ref, second_ref, pooled_ref, stat_ref, count_ref, meta_ref, norm_ref, ga_ref, prod_ref, st_ref):
    task = pl.program_id(0)
    shape = pooled_ref.shape
    rows, cols = shape[:2]
    center, inverse, gain, bias = task_norm(stat_ref, count_ref, meta_ref, norm_ref, task, 1)
    grad = taps_dot(dz_ref.at[0], w_ref.at[0], rows, cols, 0, True).reshape(shape)
    zhat = (second_ref[0, 1 : 1 + rows, 1 : 1 + cols] - center) * inverse
    attention = sigmoid(zhat * gain + bias)
    through = grad * attention
    ga = through * pooled_ref[...].astype(F32) * (1.0 - attention)
    ga_ref[0] = ga

    @pl.when(task == 0)
    def _():
        prod_ref[...] = through

    @pl.when(task > 0)
    def _():
        prod_ref[...] += through

    st_ref[:, 0] = jnp.broadcast_to(sums_of(ga, ga * zhat).astype(BF16)[None], (st_ref.shape[0],) + st_ref.shape[2:])


def scatter_tap(out_ref, task, tap, total):
    quarters, piece = out_ref.shape[0], out_ref.shape[4]
    channels = total.shape[0]
    at, end = tap * channels, (tap + 1) * channels
    while at < end:
        block, inside = at // piece, at % piece
        size = min(piece - inside, end - at)
        shard, quarter = block // quarters, block % quarters
        out_ref[quarter, shard // 2, task, shard % 2, inside : inside + size] = total[
            at - tap * channels : at - tap * channels + size
        ]
        at += size


def branch_wgrad_kernel(own_ref, other_ref, dz_own_ref, dz_other_ref, out_ref):
    rows, cols = dz_own_ref.shape[1:3]
    own = flat(dz_own_ref[0])
    other = flat(dz_other_ref[0])
    for tap in range(9):
        dr, dc = tap // 3, tap % 3
        total = dot_tn(flat(own_ref[0, dr : dr + rows, dc : dc + cols]), own)
        total += dot_tn(flat(other_ref[0, dr : dr + rows, dc : dc + cols]), other)
        scatter_tap(out_ref, 0, tap, total.astype(BF16))


def attend_back_kernel(ga_ref, second_ref, stat2_ref, back_ref, hidden_ref, p2_ref, first_ref, stat1_ref, count_ref, meta_ref, norm_ref, ext_ref, wg_ref, gl_ref, st_ref):
    task = pl.program_id(0)
    shape = ga_ref.shape[1:]
    rows, cols = shape[:2]
    center, inverse, gain, _ = task_norm(stat2_ref, count_ref, meta_ref, norm_ref, task, 1)
    zhat = (second_ref[0, 1 : 1 + rows, 1 : 1 + cols] - center) * inverse
    bias_mean, gain_mean = back_sums(back_ref, meta_ref[1:2])
    inside = mask_of(ext_ref, 0, 0, rows, cols)
    dz = keep(inside, gain * inverse * (ga_ref[0] - bias_mean - zhat * gain_mean)).astype(BF16)
    wg_ref[0] = dot_tn(flat(hidden_ref[0]), flat(dz)).astype(BF16)
    grad_hidden = dot_nt(flat(dz), square_of(p2_ref)).reshape(shape)
    center, inverse, gain, bias = task_norm(stat1_ref, count_ref, meta_ref, norm_ref, task, 0)
    zhat = (first_ref[0] - center) * inverse
    v = zhat * gain + bias
    s = sigmoid(v)
    gl = keep(inside, grad_hidden * (s * (1.0 + v * (1.0 - s))))
    gl_ref[0] = gl
    st_ref[:, 0] = jnp.broadcast_to(sums_of(gl, gl * zhat).astype(BF16)[None], (st_ref.shape[0],) + st_ref.shape[2:])


def unpool(grad, rows, cols):
    spread = jnp.broadcast_to(grad[:, None, :, None], (rows // 2, 2, cols // 2, 2) + grad.shape[2:])
    return spread.reshape((rows, cols) + grad.shape[2:])


def shared_grad_terms(z, grad, center, inverse, gain, bias, inside):
    zhat = (z - center) * inverse
    v = zhat * gain + bias
    s = sigmoid(v)
    upstream = keep(inside, unpool(0.25 * grad, z.shape[0], z.shape[1]) * (s * (1.0 + v * (1.0 - s))))
    return zhat, upstream


def pooled_back_kernel(chunk, gl_ref, first_ref, stat1_ref, back_ref, pooled_ref, p1_ref, prod_ref, z_ref, stat0_ref, count_ref, meta_ref, norm_ref, ext_ref, full_ref, wg_ref, gp_ref, st_ref):
    task = pl.program_id(0)
    shape = gl_ref.shape[1:]
    rows, cols = shape[:2]
    center, inverse, gain, _ = task_norm(stat1_ref, count_ref, meta_ref, norm_ref, task, 0)
    zhat = (first_ref[0] - center) * inverse
    bias_mean, gain_mean = back_sums(back_ref, meta_ref[1:2])
    inside = mask_of(ext_ref, 0, 0, rows, cols)
    dz = keep(inside, gain * inverse * (gl_ref[0] - bias_mean - zhat * gain_mean)).astype(BF16)
    wg_ref[0] = dot_tn(flat(pooled_ref[...]), flat(dz)).astype(BF16)
    grad = dot_nt(flat(dz), square_of(p1_ref)).reshape(shape)

    @pl.when(task == 0)
    def _():
        gp_ref[...] = prod_ref[...] + grad

    @pl.when(task > 0)
    def _():
        gp_ref[...] += grad

    @pl.when(task == pl.num_programs(0) - 1)
    def _():
        center, inverse = moments(stat0_ref[...], count_ref[0], meta_ref[0:1])
        gain, bias = norm_ref[0, 0:1], norm_ref[1, 0:1]
        full_rows, full_cols = z_ref.shape[:2]

        def body(i, total):
            row = i * chunk
            inside = mask_of(full_ref, row, 0, chunk, full_cols)
            zhat, upstream = shared_grad_terms(
                z_ref[pl.ds(row, chunk)], gp_ref[pl.ds(i * (chunk // 2), chunk // 2)],
                center, inverse, gain, bias, inside,
            )
            return total + sums_of(upstream, upstream * zhat)

        total = lax.fori_loop(0, full_rows // chunk, body, jnp.zeros((2, st_ref.shape[2]), F32))
        st_ref[...] = jnp.broadcast_to(total.astype(BF16)[None], st_ref.shape)


def shared_dz_kernel(rows, z_ref, gp_ref, stat_ref, back_ref, count_ref, meta_ref, norm_ref, ext_ref, dz_ref):
    step = pl.program_id(0)
    cols = z_ref.shape[1]
    center, inverse = moments(stat_ref[...], count_ref[0], meta_ref[0:1])
    gain, bias = norm_ref[0, 0:1], norm_ref[1, 0:1]
    total = jnp.sum(back_ref[...].astype(F32), axis=0) * meta_ref[0:1]
    inside = mask_of(ext_ref, step * rows, 0, rows, cols)
    zhat, upstream = shared_grad_terms(z_ref[...], gp_ref[...], center, inverse, gain, bias, inside)
    dz = gain * inverse * (upstream - total[0:1] - zhat * total[1:2])
    dz_ref[...] = keep(inside, dz).astype(BF16)


def shared_wgrad_kernel(own_ref, other_ref, dz_own_ref, dz_other_ref, out_ref):
    turn = pl.program_id(0)
    rows, cols = dz_own_ref.shape[:2]
    own = flat(dz_own_ref[...])
    other = flat(dz_other_ref[...])
    for tap in range(9):

        @pl.when(turn == tap)
        def _():
            dr, dc = tap // 3, tap % 3
            total = dot_tn(flat(own_ref[dr : dr + rows, dc : dc + cols]), own)
            total += dot_tn(flat(other_ref[dr : dr + rows, dc : dc + cols]), other)
            scatter_tap(out_ref, 0, tap, total.astype(BF16))


def shared_dgrad_kernel(rows, dz_ref, w_ref, ext_ref, out_ref):
    step = pl.program_id(0)
    cols = out_ref.shape[1]
    grad = taps_dot(dz_ref, w_ref, rows, cols, step * rows, True).reshape(out_ref.shape)
    out_ref[...] = keep(mask_of(ext_ref, step * rows, 0, rows, cols), grad)


def whole(shape):
    return pl.BlockSpec(shape, lambda i: (0,) * len(shape))


def leading(shape):
    return pl.BlockSpec(shape, lambda i: (i,) + (0,) * (len(shape) - 1))


def second_dim(shape):
    return pl.BlockSpec(shape, lambda i: (0, i) + (0,) * (len(shape) - 2))


def call(kernel, grid, ins, outs, scratch=(), flops=0):
    arrays = [array for array, _ in ins]
    moved = sum(a.size * a.dtype.itemsize for a in arrays)
    moved += sum(s.size * s.dtype.itemsize for s, _ in outs)
    return pl.pallas_call(
        kernel,
        grid=(grid,),
        in_specs=[spec for _, spec in ins],
        out_specs=[spec for _, spec in outs],
        out_shape=[shape for shape, _ in outs],
        scratch_shapes=list(scratch),
        compiler_params=pltpu.CompilerParams(vmem_limit_bytes=VMEM_LIMIT),
        cost_estimate=pl.CostEstimate(flops=flops, bytes_accessed=moved, transcendentals=0),
    )(*arrays)


def shape_of(shape, dtype):
    return jax.ShapeDtypeStruct(shape, dtype)


def shift_cols(array, step):
    chips, cores = lax.axis_size("chips"), lax.axis_size("core")
    total = chips * cores
    pairs = [(i, i + step) for i in range(total) if 0 <= i + step < total]
    return lax.ppermute(array, ("chips", "core"), pairs)


def shift_rows(array, step):
    total = lax.axis_size("rows")
    pairs = [(i, i + step) for i in range(total) if 0 <= i + step < total]
    return lax.ppermute(array, "rows", pairs)


def rims(array, dim, shift):
    length = array.shape[dim]
    before = shift(lax.slice_in_dim(array, length - 1, length, axis=dim), 1)
    after = shift(lax.slice_in_dim(array, 0, 1, axis=dim), -1)
    return before, after


def joined(rim, array, dim):
    return jnp.concatenate([rim[0], array, rim[1]], axis=dim)


def extended(array, row_dim):
    array = joined(rims(array, row_dim, shift_rows), array, row_dim)
    return joined(rims(array, row_dim + 1, shift_cols), array, row_dim + 1)


def spread_all(stats):
    return lax.all_to_all(stats, EVERY, 0, 0)


def swap(array, axis, flip):
    total = lax.axis_size(axis)
    return lax.ppermute(array, axis, [(i, i ^ flip) for i in range(total)])


def spread_chips(shard):
    chips, rows = lax.axis_size("chips"), lax.axis_size("rows")
    width = shard.shape[-1] // rows
    mine = lax.dynamic_slice_in_dim(shard, lax.axis_index("rows") * width, width, axis=1)
    return [swap(mine, "chips", hop) for hop in range(1, chips)]


def spread_rows(shard, hops):
    line = jnp.stack(hops)
    return [shard, line] + [swap(line, "rows", flip) for flip in range(1, lax.axis_size("rows"))]


def spread_cores(pieces):
    return pieces + [swap(piece, "core", 1) for piece in pieces]


def gather_weights(shard):
    rows = lax.axis_size("rows")
    part = shard.shape[1] // rows
    mine = lax.dynamic_slice_in_dim(shard, lax.axis_index("rows") * part, part, axis=1)
    return lax.all_gather(mine.astype(BF16), ("chips", "core", "rows"), axis=1, tiled=True)


def pick(array, axis, index):
    return lax.dynamic_index_in_dim(array, index, axis=axis, keepdims=False)


def summed(parts):
    total = parts[0].astype(F32)
    for part in parts[1:]:
        total = total + part.astype(F32)
    return total.astype(BF16)


def row_sends(parts):
    row = lax.axis_index("rows")
    return [pick(parts, 0, row ^ flip) for flip in range(lax.axis_size("rows"))]


def reduce_rows(sends):
    return [sends[0]] + [swap(part, "rows", flip) for flip, part in enumerate(sends) if flip]


def reduce_chips(parts):
    total = summed(parts)
    chip = lax.axis_index("chips")
    chips = lax.axis_size("chips")
    return [pick(total, 0, chip)] + [
        swap(pick(total, 0, chip ^ hop), "chips", hop) for hop in range(1, chips)
    ]


def pair_share(parts):
    total = summed(parts)
    core = lax.axis_index("core")
    kept = pick(total, 1, core)
    got = swap(pick(total, 1, 1 - core), "core", 1)
    low = jnp.where(core == 0, kept, got)
    high = jnp.where(core == 0, got, kept)
    return jnp.concatenate([low, high], axis=-1)


def share_rows(share):
    return [share] + [swap(share, "rows", flip) for flip in range(1, lax.axis_size("rows"))]


def update_kernel(rate, count, place_ref, weight_ref, moment_ref, average_ref, *refs):
    parts, outs = refs[:count], refs[-4:]
    turn = pl.program_id(1)
    for flip, part in enumerate(parts):

        @pl.when(turn == flip)
        def _():
            grad = part[...].astype(F32)[:, None]
            weight = weight_ref[...]
            descent = grad + WEIGHT_DECAY * weight
            mom_new = MOMENTUM * moment_ref[...] + descent
            weight_new = weight - rate * (descent + MOMENTUM * mom_new)
            outs[0][...] = grad
            outs[1][...] = mom_new
            outs[2][...] = weight_new
            outs[3][...] = AVERAGE * average_ref[...] + (1.0 - AVERAGE) * weight_new


def update(parts, weight, moment, average, rate, first, block, earlier=()):
    groups, depth, channels = weight.shape
    rows = lax.axis_size("rows")
    piece = depth // rows
    count = parts[0].shape[0]
    split = (groups, rows, piece, channels)
    weight, moment, average = (a.reshape(split) for a in (weight, moment, average))
    earlier = [a.reshape(split) for a in earlier]
    state = pl.BlockSpec(
        (block, 1, piece, channels), lambda g, t, p: (g + first // block, jnp.bitwise_xor(p[2], t), 0, 0)
    )
    grads = pl.BlockSpec((block, piece, channels), lambda g, t, p: (g, 0, 0))
    anywhere = pl.BlockSpec(memory_space=pl.ANY)
    outs = pl.pallas_call(
        functools.partial(update_kernel, rate, len(parts)),
        grid_spec=pltpu.PrefetchScalarGridSpec(
            num_scalar_prefetch=1,
            grid=(count // block, rows),
            in_specs=[state] * 3 + [grads] * len(parts) + [anywhere] * len(earlier),
            out_specs=[state] * 4,
        ),
        out_shape=[jax.ShapeDtypeStruct(split, F32)] * 4,
        input_output_aliases={4 + len(parts) + i: i for i in range(len(earlier))},
        compiler_params=pltpu.CompilerParams(vmem_limit_bytes=VMEM_LIMIT),
        cost_estimate=pl.CostEstimate(
            flops=0, bytes_accessed=30 * count * depth * channels, transcendentals=0
        ),
    )(place_of(), weight, moment, average, *parts, *earlier)
    return [a.reshape(groups, depth, channels) for a in outs]


def place_of():
    place = jnp.stack([lax.axis_index("chips"), lax.axis_index("core"), lax.axis_index("rows")])
    return place.astype(jnp.int32)


def halves(array):
    core = lax.axis_index("core")
    half = array.shape[-1] // 2
    mine = lax.dynamic_slice_in_dim(array, core * half, half, axis=array.ndim - 1)
    other = lax.dynamic_slice_in_dim(array, (1 - core) * half, half, axis=array.ndim - 1)
    return mine, lax.ppermute(other, "core", PAIR)


def refresh(weight, gradient, moment, average, step_rate):
    descent = gradient + WEIGHT_DECAY * weight
    mom_new = MOMENTUM * moment + descent
    weight_new = weight - step_rate * (descent + MOMENTUM * mom_new)
    avg_new = AVERAGE * average + (1.0 - AVERAGE) * weight_new
    return (mom_new, weight_new, avg_new)


def shards(
    features,
    extent,
    cotangent,
    wide_w,
    wide_mom,
    wide_avg,
    point_w,
    point_mom,
    point_avg,
    norm_w,
    norm_mom,
    norm_avg,
):
    tasks = point_w.shape[0] // 2
    images, rows, cols, channels = features.shape
    half_rows, half_cols = rows // 2, cols // 2
    rate_wide = 0.4 / (9.0 * channels) ** 0.5
    rate_point = 2.0 / float(channels) ** 0.5
    devices = lax.axis_size("rows") * lax.axis_size("chips") * lax.axis_size("core")
    row_start = lax.axis_index("rows") * rows
    col_start = (lax.axis_index("chips") * lax.axis_size("core") + lax.axis_index("core")) * cols
    starts = jnp.stack([row_start, col_start]).astype(jnp.int32)[:, None]
    full_ext = jnp.broadcast_to((extent - starts)[:, :, None], (2, images, channels))
    half_ext = jnp.broadcast_to((extent // 2 - starts // 2)[:, :, None], (2, images, channels))
    full_count = jnp.sum(extent[0] * extent[1]).astype(F32)
    all_rows = jnp.arange(lax.axis_size("rows"), dtype=jnp.int32)[:, None, None] * rows
    all_cols = jnp.arange(devices // lax.axis_size("rows"), dtype=jnp.int32)[None, :, None] * cols
    valid = jnp.clip(extent[0] - all_rows, 0, rows) * jnp.clip(extent[1] - all_cols, 0, cols)
    counts = jnp.sum(valid, axis=2).astype(F32).reshape(devices)
    own_count = jnp.sum(
        jnp.clip(extent[0] - row_start, 0, rows) * jnp.clip(extent[1] - col_start, 0, cols)
    ).astype(F32)
    own_inv = 1.0 / jnp.maximum(own_count, 1.0)
    meta = jnp.broadcast_to(
        jnp.stack(
            [
                1.0 / full_count,
                4.0 / full_count,
                lax.rsqrt(full_count / 16.0),
                own_count,
                own_inv,
                0.25 * own_count,
                4.0 * own_inv,
            ]
        )[:, None],
        (7, channels),
    )
    counts = jnp.broadcast_to(
        jnp.stack([counts, 0.25 * counts])[:, :, None, None], (2, devices, 1, channels)
    )
    place = place_of()
    shared_own = jnp.concatenate([wide_w[0], point_w.reshape(-1, channels)], axis=0).astype(BF16)
    hops = spread_chips(shared_own)
    features, hops = lax.optimization_barrier((features, hops))
    pieces = spread_rows(shared_own, hops)
    maps = features.transpose(1, 2, 0, 3)
    row_ids = jnp.arange(rows, dtype=jnp.int32)[:, None, None]
    col_ids = jnp.arange(cols, dtype=jnp.int32)[None, :, None]
    inside = (row_ids < (extent[0] - row_start)[None, None]) & (col_ids < (extent[1] - col_start)[None, None])
    maps = jnp.where(inside[..., None], maps, jnp.zeros((), BF16))
    x_tall = joined(rims(maps, 0, shift_rows), maps, 0)
    later_w, x_tall = lax.optimization_barrier((wide_w[1:], x_tall))
    x_pad = joined(rims(x_tall, 1, shift_cols), x_tall, 1)
    pieces, x_pad = lax.optimization_barrier((pieces, x_pad))
    branch_w = gather_weights(later_w)
    branch_in = (branch_w, leading((1,) + branch_w.shape[1:]))
    pieces = spread_cores(pieces)
    x_other = lax.ppermute(x_pad, "core", PAIR)
    cot = cotangent.transpose(0, 2, 3, 1, 4)

    full = (rows, cols, images, channels)
    half = (half_rows, half_cols, images, channels)
    wide = (half_rows + 2, half_cols + 2, images, channels)
    quarter = (half_rows // 2, half_cols // 2, images, channels)
    stat = (devices, 2, channels)
    task_stat = (devices, tasks, 2, channels)
    one_stat = second_dim((devices, 1, 2, channels))
    meta_in = (meta, whole(meta.shape))
    count_in = (counts, whole(counts.shape))
    norm_in = (norm_w, whole(norm_w.shape))
    full_in = (full_ext, whole(full_ext.shape))
    half_in = (half_ext, whole(half_ext.shape))
    vec = pltpu.VMEM((2, channels), F32)
    place_in = (place, pl.BlockSpec(memory_space=pltpu.SMEM))
    anywhere = pl.BlockSpec(memory_space=pl.ANY)
    copies = 4 * (1 + lax.axis_size("rows") * (lax.axis_size("chips") - 1))

    point_split = (2 * lax.axis_size("chips"), 2 * tasks, point_w.shape[1], channels)
    point_flat = (point_split[0], point_split[1] * point_split[2], channels)
    point_block = (point_split[0], 1) + point_split[2:]
    weight = (9 * channels, channels)

    full_flops = 2 * 9 * rows * cols * images * channels * channels
    half_flops = full_flops // 4 * tasks
    task_of = lambda shape: leading((1,) + shape)

    block = 4
    z, local, shared_w, point_full = call(
        functools.partial(shared_fwd_kernel, block),
        rows // block,
        [place_in, (x_pad, whole(x_pad.shape)), meta_in, full_in] + [(p, anywhere) for p in pieces],
        [
            (shape_of(full, F32), leading((block,) + full[1:])),
            (shape_of(stat, BF16), whole(stat)),
            (shape_of(weight, BF16), anywhere),
            (shape_of(point_flat, BF16), anywhere),
        ],
        [
            vec,
            pltpu.VMEM(weight, BF16),
            pltpu.VMEM(point_flat, BF16),
            pltpu.SemaphoreType.DMA((copies,)),
            pltpu.SemaphoreType.DMA((2,)),
        ],
        full_flops,
    )
    point_full = point_full.reshape(point_split)
    first_ws = (point_full, pl.BlockSpec(point_block, lambda i: (0, i, 0, 0)))
    second_ws = (point_full, pl.BlockSpec(point_block, lambda i: (0, i + tasks, 0, 0)))
    stat0 = spread_all(local)

    pooled, local = call(
        functools.partial(pool_kernel, block),
        rows // block,
        [
            (z, leading((block,) + full[1:])),
            (stat0, whole(stat)),
            count_in,
            meta_in,
            norm_in,
            full_in,
            (
                point_full,
                pl.BlockSpec((point_split[0], tasks) + point_split[2:], lambda i: (0, 0, 0, 0)),
            ),
        ],
        [
            (shape_of(half, BF16), leading((block // 2,) + half[1:])),
            (shape_of(task_stat, BF16), whole(task_stat)),
        ],
        [pltpu.VMEM(half, BF16), vec],
    )
    pooled_wide = extended(pooled, 0)
    stat1 = spread_all(local)

    first, hidden, second, local = call(
        attend_kernel,
        tasks,
        [
            (pooled_wide, whole(wide)),
            (stat1, one_stat),
            count_in,
            meta_in,
            norm_in,
            half_in,
            first_ws,
            second_ws,
        ],
        [
            (shape_of((tasks,) + half, F32), task_of(half)),
            (shape_of((tasks,) + half, BF16), task_of(half)),
            (shape_of((tasks,) + wide, F32), task_of(wide)),
            (shape_of(task_stat, BF16), one_stat),
        ],
    )
    stat2 = spread_all(local)

    masked, branch, local = call(
        branch_fwd_kernel,
        tasks,
        [
            (second, task_of(wide)),
            (pooled_wide, whole(wide)),
            (stat2, one_stat),
            count_in,
            meta_in,
            norm_in,
            half_in,
            branch_in,
        ],
        [
            (shape_of((tasks,) + wide, BF16), task_of(wide)),
            (shape_of((tasks,) + half, F32), task_of(half)),
            (shape_of(task_stat, BF16), one_stat),
        ],
        flops=half_flops,
    )
    masked_other = lax.ppermute(masked, "core", PAIR)
    stat3 = spread_all(local)

    branch_ins = [
        (branch, task_of(half)),
        (cot, task_of(quarter)),
        (stat3, one_stat),
    ]
    result, local = call(
        result_kernel,
        tasks,
        branch_ins + [count_in, meta_in, norm_in, half_in],
        [
            (shape_of((tasks,) + quarter, BF16), task_of(quarter)),
            (shape_of(task_stat, BF16), one_stat),
        ],
    )
    back3 = spread_all(local)

    (branch_dz,) = call(
        branch_dz_kernel,
        tasks,
        branch_ins + [(back3, one_stat), count_in, meta_in, norm_in, half_in],
        [(shape_of((tasks,) + half, BF16), task_of(half))],
    )
    dz_own, dz_other = halves(branch_dz)
    dz_tall = joined(rims(branch_dz, 1, shift_rows), branch_dz, 1)
    dz_rim = rims(dz_tall, 2, shift_cols)
    narrow = half[:-1] + (channels // 2,)
    chips, quarters = lax.axis_size("chips"), lax.axis_size("rows")
    piece = 9 * channels // (2 * chips * quarters)
    (branch_grad,) = call(
        branch_wgrad_kernel,
        tasks,
        [
            (masked, task_of(wide)),
            (masked_other, task_of(wide)),
            (dz_own, task_of(narrow)),
            (dz_other, task_of(narrow)),
        ],
        [
            (
                shape_of((quarters, chips, tasks, 2, piece, channels // 2), BF16),
                pl.BlockSpec(
                    (quarters, chips, 1, 2, piece, channels // 2), lambda i: (0, 0, i, 0, 0, 0)
                ),
            )
        ],
        flops=half_flops,
    )
    branch_grad, dz_rim = lax.optimization_barrier((branch_grad, dz_rim))
    branch_parts = lax.psum_scatter(branch_grad, "rows", scatter_dimension=0, tiled=True)[0]
    dz_wide = joined(dz_rim, dz_tall, 2)

    ga, product, local = call(
        branch_dgrad_kernel,
        tasks,
        [
            (dz_wide, task_of(wide)),
            branch_in,
            (second, task_of(wide)),
            (pooled, whole(half)),
            (stat2, one_stat),
            count_in,
            meta_in,
            norm_in,
        ],
        [
            (shape_of((tasks,) + half, F32), task_of(half)),
            (shape_of(half, F32), whole(half)),
            (shape_of(task_stat, BF16), one_stat),
        ],
        flops=half_flops,
    )
    back2 = spread_all(local)

    square = (channels, channels)
    second_grad, gl, local = call(
        attend_back_kernel,
        tasks,
        [
            (ga, task_of(half)),
            (second, task_of(wide)),
            (stat2, one_stat),
            (back2, one_stat),
            (hidden, task_of(half)),
            second_ws,
            (first, task_of(half)),
            (stat1, one_stat),
            count_in,
            meta_in,
            norm_in,
            half_in,
        ],
        [
            (shape_of((tasks,) + square, BF16), task_of(square)),
            (shape_of((tasks,) + half, F32), task_of(half)),
            (shape_of(task_stat, BF16), one_stat),
        ],
    )
    back1 = spread_all(local)

    first_grad, grad_pooled, local = call(
        functools.partial(pooled_back_kernel, block),
        tasks,
        [
            (gl, task_of(half)),
            (first, task_of(half)),
            (stat1, one_stat),
            (back1, one_stat),
            (pooled, whole(half)),
            first_ws,
            (product, whole(half)),
            (z, whole(full)),
            (stat0, whole(stat)),
            count_in,
            meta_in,
            norm_in,
            half_in,
            full_in,
        ],
        [
            (shape_of((tasks,) + square, BF16), task_of(square)),
            (shape_of(half, F32), whole(half)),
            (shape_of(stat, BF16), whole(stat)),
        ],
    )
    back0 = spread_all(local)
    point_local = jnp.concatenate([first_grad, second_grad], axis=0)
    point_own, point_other = halves(point_local)
    point_half, back0 = lax.optimization_barrier((point_own + point_other, back0))
    point_shape = (2 * tasks, chips, 2, quarters, channels // (2 * chips * quarters), channels // 2)
    point_parts = reduce_rows(row_sends(point_half.reshape(point_shape).transpose(3, 1, 0, 2, 4, 5)))

    (shared_dz,) = call(
        functools.partial(shared_dz_kernel, block),
        rows // block,
        [
            (z, leading((block,) + full[1:])),
            (grad_pooled, leading((block // 2,) + half[1:])),
            (stat0, whole(stat)),
            (back0, whole(stat)),
            count_in,
            meta_in,
            norm_in,
            full_in,
        ],
        [(shape_of(full, BF16), leading((block,) + full[1:]))],
    )
    branch_parts, shared_dz = lax.optimization_barrier((branch_parts, shared_dz))
    branch_parts = lax.psum_scatter(branch_parts, "chips", scatter_dimension=0, tiled=True)
    dz_own, dz_other = halves(shared_dz)
    dz_rim = rims(shared_dz, 0, shift_rows)
    (shared_grad,) = call(
        shared_wgrad_kernel,
        9,
        [
            (x_pad, whole(x_pad.shape)),
            (x_other, whole(x_other.shape)),
            (dz_own, whole(dz_own.shape)),
            (dz_other, whole(dz_other.shape)),
        ],
        [
            (
                shape_of((quarters, chips, 1, 2, piece, channels // 2), BF16),
                whole((quarters, chips, 1, 2, piece, channels // 2)),
            )
        ],
        flops=full_flops,
    )
    sends = row_sends(shared_grad)
    point_parts, sends, dz_rim = lax.optimization_barrier((point_parts, sends, dz_rim))
    branch_parts, _ = lax.optimization_barrier((branch_parts, sends))
    shared_parts = reduce_rows(sends)
    dz_tall = joined(dz_rim, shared_dz, 0)
    dz_pad = joined(rims(dz_tall, 1, shift_cols), dz_tall, 1)
    branch_parts, dz_pad = lax.optimization_barrier((pair_share(branch_parts), dz_pad))
    branch_share = share_rows(branch_parts)
    point_parts = reduce_chips(point_parts)
    (input_grad,) = call(
        functools.partial(shared_dgrad_kernel, block),
        rows // block,
        [(dz_pad, whole(dz_pad.shape)), (shared_w, whole(weight)), full_in],
        [(shape_of(full, F32), leading((block,) + full[1:]))],
        flops=full_flops,
    )
    shared_parts, point_parts, input_grad = lax.optimization_barrier(
        (shared_parts, point_parts, input_grad)
    )
    shared_parts = reduce_chips(shared_parts)
    branch_share, _ = lax.optimization_barrier((branch_share, input_grad))
    branch_state = update(branch_share, wide_w, wide_mom, wide_avg, rate_wide, 1, 1)
    shared_parts, point_parts, branch_state = lax.optimization_barrier(
        (shared_parts, point_parts, branch_state)
    )
    shared_share = share_rows(pair_share(shared_parts))
    point_share = share_rows(pair_share(point_parts))
    input_grad = input_grad.transpose(2, 0, 1, 3)
    point_state = update(point_share, point_w, point_mom, point_avg, rate_point, 0, 2 * tasks)
    shared_share, point_state, input_grad = lax.optimization_barrier(
        (shared_share, point_state, input_grad)
    )
    point_share, point_mom_new, point_new, point_avg_new = point_state

    wide_share, wide_mom_new, wide_new, wide_avg_new = update(
        shared_share, wide_w, wide_mom, wide_avg, rate_wide, 0, 1, branch_state
    )
    bsum = jnp.stack([jnp.sum(b.astype(F32), axis=0) for b in (back1, back2, back3)], axis=1)
    bsum = bsum.transpose(2, 0, 1, 3).reshape(2, 3 * tasks, channels)
    norm_grad = jnp.concatenate([jnp.sum(back0.astype(F32), axis=0)[:, None], bsum], axis=1)[::-1]
    norm_mom_new, norm_new, norm_avg_new = refresh(norm_w, norm_grad, norm_mom, norm_avg, RATE_NORM)
    return (
        result.transpose(0, 3, 1, 2, 4),
        input_grad,
        wide_share,
        wide_mom_new,
        wide_new,
        wide_avg_new,
        point_share,
        point_mom_new,
        point_new,
        point_avg_new,
        norm_grad,
        norm_mom_new,
        norm_new,
        norm_avg_new,
    )


def solution(mesh):
    rows, cols = mesh.devices.shape
    cores = 2
    fine = Mesh(mesh.devices.reshape(rows, cols // cores, cores), EVERY)
    across = ("chips", "core")
    weights = P(None, across, None)
    placed = (
        P(None, "rows", across, None),
        P(),
        P(None, None, "rows", across, None),
        weights,
        weights,
        weights,
        weights,
        weights,
        weights,
        P(),
        P(),
        P(),
    )
    return jax.shard_map(
        shards,
        mesh=fine,
        in_specs=placed,
        out_specs=(
            P(None, None, "rows", across, None),
            P(None, "rows", across, None),
            weights,
            weights,
            weights,
            weights,
            weights,
            weights,
            weights,
            weights,
            P(),
            P(),
            P(),
            P(),
        ),
        check_vma=False,
    )
```

```python
import functools

import jax
import jax.numpy as jnp
from jax import lax
from jax.experimental import pallas as pl
from jax.experimental.pallas import tpu as pltpu
from jax.sharding import Mesh
from jax.sharding import PartitionSpec as P

EPSILON = 1e-05
MOMENTUM = 0.9
WEIGHT_DECAY = 0.0001
AVERAGE = 0.6
RATE_NORM = 0.4
F32 = jnp.float32
BF16 = jnp.bfloat16
EVERY = ("rows", "chips", "core")
PAIR = [(0, 1), (1, 0)]
VMEM_LIMIT = 56 * 1024 * 1024


def sigmoid(values):
    return 0.5 * jnp.tanh(0.5 * values) + 0.5


def flat(values):
    return values.reshape((-1, values.shape[-1]))


def square_of(ref):
    return ref[...].reshape(ref.shape[-1], ref.shape[-1])


def mask_of(ext_ref, row, col, rows, cols):
    shape = (rows, cols) + ext_ref.shape[1:]
    row_ids = row + lax.broadcasted_iota(jnp.int32, shape, 0)
    col_ids = col + lax.broadcasted_iota(jnp.int32, shape, 1)
    inside = (row_ids < ext_ref[0][None, None]) & (col_ids < ext_ref[1][None, None])
    return inside


def keep(inside, values):
    return jnp.where(inside, values, 0.0)


def sums_of(first, second):
    return jnp.concatenate(
        [jnp.sum(flat(first), axis=0, keepdims=True), jnp.sum(flat(second), axis=0, keepdims=True)],
        axis=0,
    )


def centered(sums, local):
    center = (sums[0:1] * local[1:2]).astype(BF16)
    wide = center.astype(F32)
    spread = sums[1:2] - 2.0 * wide * sums[0:1] + local[0:1] * wide * wide
    return jnp.concatenate([wide, spread], axis=0).astype(BF16)


def moments(stats, counts, inv_count):
    stats = stats.astype(F32)
    centers = stats[:, 0:1]
    center = jnp.sum(counts * centers, axis=0) * inv_count
    off = centers - center[None]
    spread = jnp.sum(stats[:, 1:2] + counts * off * off, axis=0) * inv_count
    return center, lax.rsqrt(spread + EPSILON)


def taps_dot(source, weight, rows, cols, row, mirrored):
    channels = weight.shape[-1]
    total = None
    for tap in range(9):
        dr, dc = tap // 3, tap % 3
        if mirrored:
            dr, dc = 2 - dr, 2 - dc
        window = flat(source[pl.ds(row + dr, rows), dc : dc + cols])
        block = weight[tap * channels : (tap + 1) * channels, :]
        dims = (((1,), (1,)), ((), ())) if mirrored else (((1,), (0,)), ((), ()))
        part = lax.dot_general(window, block, dims, preferred_element_type=F32)
        total = part if total is None else total + part
    return total


def dot(left, right):
    return jnp.dot(left, right, preferred_element_type=F32)


def dot_nt(left, right):
    return lax.dot_general(left, right, (((1,), (1,)), ((), ())), preferred_element_type=F32)


def dot_tn(left, right):
    return lax.dot_general(left, right, (((0,), (0,)), ((), ())), preferred_element_type=F32)


def assemble(place_ref, pieces, w_ref, point_ref, sem, start):
    chip, core, row = place_ref[0], place_ref[1], place_ref[2]
    half = len(pieces) // 2
    depth = w_ref.shape[0] // point_ref.shape[0]
    count = 0
    for side in range(2):
        own, parts = pieces[side * half], pieces[side * half + 1 : (side + 1) * half]
        width = parts[0].shape[-1]
        at_core = core if side == 0 else 1 - core

        def run(source, shard, lanes, at):
            base = pl.multiple_of(shard * depth, 16)
            rest = source.shape[0] - depth
            pairs = (
                (source.at[pl.ds(0, depth)], w_ref.at[pl.ds(base, depth), lanes]),
                (source.at[pl.ds(depth, rest)], point_ref.at[shard, :, lanes]),
            )
            for i, (left, right) in enumerate(pairs):
                copy = pltpu.make_async_copy(left, right, sem.at[at + i])
                copy.start() if start else copy.wait()

        run(own, 2 * chip + at_core, pl.ds(0, own.shape[1]), count)
        count += 2
        for flip, part in enumerate(parts):
            lane = pl.multiple_of(jnp.bitwise_xor(row, flip) * width, 128)
            for hop in range(part.shape[0]):
                shard = 2 * jnp.bitwise_xor(chip, hop + 1) + at_core
                run(part.at[hop], shard, pl.ds(lane, width), count)
                count += 2


def gathered(place_ref, pieces, w_ref, point_ref, sem, w_out, point_out, out_sem):
    copies = (
        pltpu.make_async_copy(w_ref, w_out, out_sem.at[0]),
        pltpu.make_async_copy(point_ref, point_out, out_sem.at[1]),
    )

    @pl.when(pl.program_id(0) == 0)
    def _():
        assemble(place_ref, pieces, w_ref, point_ref, sem, True)
        assemble(place_ref, pieces, w_ref, point_ref, sem, False)
        for copy in copies:
            copy.start()

    @pl.when(pl.program_id(0) == pl.num_programs(0) - 1)
    def _():
        for copy in copies:
            copy.wait()


def shared_fwd_kernel(rows, place_ref, x_ref, meta_ref, ext_ref, *refs):
    *pieces, z_ref, stat_ref, w_out, point_out, acc_ref, w_ref, point_ref, sem, out_sem = refs
    gathered(place_ref, pieces, w_ref, point_ref, sem, w_out, point_out, out_sem)
    step = pl.program_id(0)
    cols = z_ref.shape[1]
    z = taps_dot(x_ref, w_ref, rows, cols, step * rows, False).reshape(z_ref.shape)
    z_ref[...] = z
    zm = keep(mask_of(ext_ref, step * rows, 0, rows, cols), z)
    part = sums_of(zm, zm * z)

    @pl.when(step == 0)
    def _():
        acc_ref[...] = part

    @pl.when(step > 0)
    def _():
        acc_ref[...] += part

    @pl.when(step == pl.num_programs(0) - 1)
    def _():
        stat_ref[...] = jnp.broadcast_to(centered(acc_ref[...], meta_ref[3:5])[None], stat_ref.shape)


def pool_kernel(rows, z_ref, stat_ref, count_ref, meta_ref, norm_ref, ext_ref, p_ref, out_ref, st_ref, pool_ref, aff_ref):
    step = pl.program_id(0)
    cols = z_ref.shape[1]

    @pl.when(step == 0)
    def _():
        center, inverse = moments(stat_ref[...], count_ref[0], meta_ref[0:1])
        scale = inverse * norm_ref[0, 0:1]
        aff_ref[0:1] = scale
        aff_ref[1:2] = norm_ref[1, 0:1] - center * scale

    v = z_ref[...] * aff_ref[0:1] + aff_ref[1:2]
    lifted = keep(mask_of(ext_ref, step * rows, 0, rows, cols), v * sigmoid(v))
    grouped = lifted.reshape((rows // 2, 2, cols // 2, 2) + lifted.shape[2:])
    mean = 0.25 * (
        (grouped[:, 0, :, 0] + grouped[:, 0, :, 1]) + (grouped[:, 1, :, 0] + grouped[:, 1, :, 1])
    )
    low = mean.astype(BF16)
    out_ref[...] = low
    pool_ref[pl.ds(step * (rows // 2), rows // 2)] = low

    @pl.when(step == pl.num_programs(0) - 1)
    def _():
        left = flat(pool_ref[...])
        channels = left.shape[-1]
        for task in range(p_ref.shape[1]):
            f = dot(left, p_ref[:, task].reshape(channels, channels))
            st_ref[:, task] = jnp.broadcast_to(
                centered(sums_of(f, f * f), meta_ref[5:7])[None], (st_ref.shape[0],) + st_ref.shape[2:]
            )


def task_norm(stat_ref, count_ref, meta_ref, norm_ref, task, slot):
    center, inverse = moments(stat_ref[:, 0], count_ref[1], meta_ref[1:2])
    row = 1 + 3 * task + slot
    gain = norm_ref[0, pl.ds(row, 1)]
    bias = norm_ref[1, pl.ds(row, 1)]
    return center, inverse, gain, bias


def attend_kernel(pe_ref, stat_ref, count_ref, meta_ref, norm_ref, ext_ref, p1_ref, p2_ref, first_ref, hidden_ref, second_ref, st_ref):
    task = pl.program_id(0)
    shape = pe_ref.shape
    rows, cols = shape[0] - 2, shape[1] - 2
    center, inverse, gain, bias = task_norm(stat_ref, count_ref, meta_ref, norm_ref, task, 0)
    scale = inverse * gain
    shift = bias - center * scale
    first = dot(flat(pe_ref[...]), square_of(p1_ref))
    first_ref[0] = first.reshape(shape)[1 : 1 + rows, 1 : 1 + cols]
    v = first * scale + shift
    inside = mask_of(ext_ref, -1, -1, rows + 2, cols + 2)
    hidden = keep(inside, (v * sigmoid(v)).reshape(shape)).astype(BF16)
    hidden_ref[0] = hidden[1 : 1 + rows, 1 : 1 + cols]
    second = dot(flat(hidden), square_of(p2_ref)).reshape(shape)
    second_ref[0] = second
    own = second[1 : 1 + rows, 1 : 1 + cols]
    local = centered(sums_of(own, own * own), meta_ref[5:7])
    st_ref[:, 0] = jnp.broadcast_to(local[None], (st_ref.shape[0],) + st_ref.shape[2:])


def branch_fwd_kernel(second_ref, pe_ref, stat_ref, count_ref, meta_ref, norm_ref, ext_ref, w_ref, masked_ref, branch_ref, st_ref):
    task = pl.program_id(0)
    rows, cols = branch_ref.shape[1:3]
    center, inverse, gain, bias = task_norm(stat_ref, count_ref, meta_ref, norm_ref, task, 1)
    scale = inverse * gain
    shift = bias - center * scale
    attention = sigmoid(second_ref[0] * scale + shift)
    masked_ref[0] = (attention * pe_ref[...].astype(F32)).astype(BF16)
    z = taps_dot(masked_ref.at[0], w_ref.at[0], rows, cols, 0, False).reshape(branch_ref.shape[1:])
    branch_ref[0] = z
    zm = keep(mask_of(ext_ref, 0, 0, rows, cols), z)
    local = centered(sums_of(zm, zm * z), meta_ref[5:7])
    st_ref[:, 0] = jnp.broadcast_to(local[None], (st_ref.shape[0],) + st_ref.shape[2:])


def branch_grad_terms(branch_ref, cot_ref, stat_ref, count_ref, meta_ref, norm_ref, ext_ref, task):
    rows, cols = branch_ref.shape[1:3]
    center, inverse, gain, bias = task_norm(stat_ref, count_ref, meta_ref, norm_ref, task, 2)
    zhat = (branch_ref[0] - center) * inverse
    v = zhat * gain + bias
    s = sigmoid(v)
    inside = mask_of(ext_ref, 0, 0, rows, cols)
    c = cot_ref[0].astype(F32) * (0.25 * meta_ref[2:3])
    spread = jnp.broadcast_to(c[:, None, :, None], (rows // 2, 2, cols // 2, 2) + c.shape[2:])
    upstream = keep(inside, spread.reshape(v.shape) * (s * (1.0 + v * (1.0 - s))))
    return zhat, v, s, inside, upstream, gain * inverse


def result_kernel(branch_ref, cot_ref, stat_ref, count_ref, meta_ref, norm_ref, ext_ref, out_ref, st_ref):
    task = pl.program_id(0)
    rows, cols = branch_ref.shape[1:3]
    zhat, v, s, inside, upstream, _ = branch_grad_terms(
        branch_ref, cot_ref, stat_ref, count_ref, meta_ref, norm_ref, ext_ref, task
    )
    active = keep(inside, v * s)
    grouped = active.reshape((rows // 2, 2, cols // 2, 2) + active.shape[2:])
    mean = 0.25 * (
        (grouped[:, 0, :, 0] + grouped[:, 0, :, 1]) + (grouped[:, 1, :, 0] + grouped[:, 1, :, 1])
    )
    out_ref[0] = mean.astype(BF16)
    st_ref[:, 0] = jnp.broadcast_to(
        sums_of(upstream, upstream * zhat).astype(BF16)[None], (st_ref.shape[0],) + st_ref.shape[2:]
    )


def back_sums(stat_ref, inv_count):
    total = jnp.sum(stat_ref[:, 0].astype(F32), axis=0)
    return total[0:1] * inv_count, total[1:2] * inv_count


def branch_dz_kernel(branch_ref, cot_ref, stat_ref, back_ref, count_ref, meta_ref, norm_ref, ext_ref, dz_ref):
    task = pl.program_id(0)
    zhat, v, s, inside, upstream, factor = branch_grad_terms(
        branch_ref, cot_ref, stat_ref, count_ref, meta_ref, norm_ref, ext_ref, task
    )
    bias_mean, gain_mean = back_sums(back_ref, meta_ref[1:2])
    dz_ref[0] = keep(inside, factor * (upstream - bias_mean - zhat * gain_mean)).astype(BF16)


def branch_dgrad_kernel(dz_ref, w_ref, second_ref, pooled_ref, stat_ref, count_ref, meta_ref, norm_ref, ga_ref, prod_ref, st_ref):
    task = pl.program_id(0)
    shape = pooled_ref.shape
    rows, cols = shape[:2]
    center, inverse, gain, bias = task_norm(stat_ref, count_ref, meta_ref, norm_ref, task, 1)
    grad = taps_dot(dz_ref.at[0], w_ref.at[0], rows, cols, 0, True).reshape(shape)
    zhat = (second_ref[0, 1 : 1 + rows, 1 : 1 + cols] - center) * inverse
    attention = sigmoid(zhat * gain + bias)
    through = grad * attention
    ga = through * pooled_ref[...].astype(F32) * (1.0 - attention)
    ga_ref[0] = ga

    @pl.when(task == 0)
    def _():
        prod_ref[...] = through

    @pl.when(task > 0)
    def _():
        prod_ref[...] += through

    st_ref[:, 0] = jnp.broadcast_to(sums_of(ga, ga * zhat).astype(BF16)[None], (st_ref.shape[0],) + st_ref.shape[2:])


def scatter_tap(out_ref, task, tap, total):
    quarters, piece = out_ref.shape[0], out_ref.shape[4]
    channels = total.shape[0]
    at, end = tap * channels, (tap + 1) * channels
    while at < end:
        block, inside = at // piece, at % piece
        size = min(piece - inside, end - at)
        shard, quarter = block // quarters, block % quarters
        out_ref[quarter, shard // 2, task, shard % 2, inside : inside + size] = total[
            at - tap * channels : at - tap * channels + size
        ]
        at += size


def own_half(place_ref, ref):
    half = ref.shape[-1] // 2
    lanes = pl.ds(pl.multiple_of(place_ref[1] * half, 128), half)
    return flat(ref[..., lanes].reshape(-1, half))


def branch_wgrad_kernel(place_ref, own_ref, other_ref, dz_own_ref, dz_other_ref, out_ref):
    rows, cols = dz_own_ref.shape[1:3]
    own = own_half(place_ref, dz_own_ref)
    other = flat(dz_other_ref[0])
    for tap in range(9):
        dr, dc = tap // 3, tap % 3
        total = dot_tn(flat(own_ref[0, dr : dr + rows, dc : dc + cols]), own)
        total += dot_tn(flat(other_ref[0, dr : dr + rows, dc : dc + cols]), other)
        scatter_tap(out_ref, 0, tap, total.astype(BF16))


def attend_back_kernel(ga_ref, second_ref, stat2_ref, back_ref, hidden_ref, p2_ref, first_ref, stat1_ref, count_ref, meta_ref, norm_ref, ext_ref, wg_ref, gl_ref, st_ref):
    task = pl.program_id(0)
    shape = ga_ref.shape[1:]
    rows, cols = shape[:2]
    center, inverse, gain, _ = task_norm(stat2_ref, count_ref, meta_ref, norm_ref, task, 1)
    zhat = (second_ref[0, 1 : 1 + rows, 1 : 1 + cols] - center) * inverse
    bias_mean, gain_mean = back_sums(back_ref, meta_ref[1:2])
    inside = mask_of(ext_ref, 0, 0, rows, cols)
    dz = keep(inside, gain * inverse * (ga_ref[0] - bias_mean - zhat * gain_mean)).astype(BF16)
    wg_ref[0] = dot_tn(flat(hidden_ref[0]), flat(dz)).astype(BF16)
    grad_hidden = dot_nt(flat(dz), square_of(p2_ref)).reshape(shape)
    center, inverse, gain, bias = task_norm(stat1_ref, count_ref, meta_ref, norm_ref, task, 0)
    zhat = (first_ref[0] - center) * inverse
    v = zhat * gain + bias
    s = sigmoid(v)
    gl = keep(inside, grad_hidden * (s * (1.0 + v * (1.0 - s))))
    gl_ref[0] = gl
    st_ref[:, 0] = jnp.broadcast_to(sums_of(gl, gl * zhat).astype(BF16)[None], (st_ref.shape[0],) + st_ref.shape[2:])


def unpool(grad, rows, cols):
    spread = jnp.broadcast_to(grad[:, None, :, None], (rows // 2, 2, cols // 2, 2) + grad.shape[2:])
    return spread.reshape((rows, cols) + grad.shape[2:])


def shared_grad_terms(z, grad, center, inverse, gain, bias, inside):
    zhat = (z - center) * inverse
    v = zhat * gain + bias
    s = sigmoid(v)
    upstream = keep(inside, unpool(0.25 * grad, z.shape[0], z.shape[1]) * (s * (1.0 + v * (1.0 - s))))
    return zhat, upstream


def pooled_back_kernel(chunk, gl_ref, first_ref, stat1_ref, back_ref, pooled_ref, p1_ref, prod_ref, z_ref, stat0_ref, count_ref, meta_ref, norm_ref, ext_ref, full_ref, wg_ref, gp_ref, st_ref):
    task = pl.program_id(0)
    shape = gl_ref.shape[1:]
    rows, cols = shape[:2]
    center, inverse, gain, _ = task_norm(stat1_ref, count_ref, meta_ref, norm_ref, task, 0)
    zhat = (first_ref[0] - center) * inverse
    bias_mean, gain_mean = back_sums(back_ref, meta_ref[1:2])
    inside = mask_of(ext_ref, 0, 0, rows, cols)
    dz = keep(inside, gain * inverse * (gl_ref[0] - bias_mean - zhat * gain_mean)).astype(BF16)
    wg_ref[0] = dot_tn(flat(pooled_ref[...]), flat(dz)).astype(BF16)
    grad = dot_nt(flat(dz), square_of(p1_ref)).reshape(shape)

    @pl.when(task == 0)
    def _():
        gp_ref[...] = prod_ref[...] + grad

    @pl.when(task > 0)
    def _():
        gp_ref[...] += grad

    @pl.when(task == pl.num_programs(0) - 1)
    def _():
        center, inverse = moments(stat0_ref[...], count_ref[0], meta_ref[0:1])
        gain, bias = norm_ref[0, 0:1], norm_ref[1, 0:1]
        full_rows, full_cols = z_ref.shape[:2]

        def body(i, total):
            row = i * chunk
            inside = mask_of(full_ref, row, 0, chunk, full_cols)
            zhat, upstream = shared_grad_terms(
                z_ref[pl.ds(row, chunk)], gp_ref[pl.ds(i * (chunk // 2), chunk // 2)],
                center, inverse, gain, bias, inside,
            )
            return total + sums_of(upstream, upstream * zhat)

        total = lax.fori_loop(0, full_rows // chunk, body, jnp.zeros((2, st_ref.shape[2]), F32))
        st_ref[...] = jnp.broadcast_to(total.astype(BF16)[None], st_ref.shape)


def shared_dz_kernel(rows, z_ref, gp_ref, stat_ref, back_ref, count_ref, meta_ref, norm_ref, ext_ref, dz_ref):
    step = pl.program_id(0)
    cols = z_ref.shape[1]
    center, inverse = moments(stat_ref[...], count_ref[0], meta_ref[0:1])
    gain, bias = norm_ref[0, 0:1], norm_ref[1, 0:1]
    total = jnp.sum(back_ref[...].astype(F32), axis=0) * meta_ref[0:1]
    inside = mask_of(ext_ref, step * rows, 0, rows, cols)
    zhat, upstream = shared_grad_terms(z_ref[...], gp_ref[...], center, inverse, gain, bias, inside)
    dz = gain * inverse * (upstream - total[0:1] - zhat * total[1:2])
    dz_ref[...] = keep(inside, dz).astype(BF16)


def shared_wgrad_kernel(place_ref, own_ref, other_ref, dz_own_ref, dz_other_ref, out_ref):
    turn = pl.program_id(0)
    rows, cols = dz_own_ref.shape[:2]
    own = own_half(place_ref, dz_own_ref)
    other = flat(dz_other_ref[...])
    for tap in range(9):

        @pl.when(turn == tap)
        def _():
            dr, dc = tap // 3, tap % 3
            total = dot_tn(flat(own_ref[dr : dr + rows, dc : dc + cols]), own)
            total += dot_tn(flat(other_ref[dr : dr + rows, dc : dc + cols]), other)
            scatter_tap(out_ref, 0, tap, total.astype(BF16))


def shared_dgrad_kernel(rows, dz_ref, w_ref, ext_ref, out_ref):
    step = pl.program_id(0)
    cols = out_ref.shape[1]
    grad = taps_dot(dz_ref, w_ref, rows, cols, step * rows, True).reshape(out_ref.shape)
    out_ref[...] = keep(mask_of(ext_ref, step * rows, 0, rows, cols), grad)


def whole(shape):
    return pl.BlockSpec(shape, lambda i: (0,) * len(shape))


def leading(shape):
    return pl.BlockSpec(shape, lambda i: (i,) + (0,) * (len(shape) - 1))


def second_dim(shape):
    return pl.BlockSpec(shape, lambda i: (0, i) + (0,) * (len(shape) - 2))


def call(kernel, grid, ins, outs, scratch=(), flops=0):
    arrays = [array for array, _ in ins]
    moved = sum(a.size * a.dtype.itemsize for a in arrays)
    moved += sum(s.size * s.dtype.itemsize for s, _ in outs)
    return pl.pallas_call(
        kernel,
        grid=(grid,),
        in_specs=[spec for _, spec in ins],
        out_specs=[spec for _, spec in outs],
        out_shape=[shape for shape, _ in outs],
        scratch_shapes=list(scratch),
        compiler_params=pltpu.CompilerParams(vmem_limit_bytes=VMEM_LIMIT),
        cost_estimate=pl.CostEstimate(flops=flops, bytes_accessed=moved, transcendentals=0),
    )(*arrays)


def shape_of(shape, dtype):
    return jax.ShapeDtypeStruct(shape, dtype)


def shift_cols(array, step):
    chips, cores = lax.axis_size("chips"), lax.axis_size("core")
    total = chips * cores
    pairs = [(i, i + step) for i in range(total) if 0 <= i + step < total]
    return lax.ppermute(array, ("chips", "core"), pairs)


def shift_rows(array, step):
    total = lax.axis_size("rows")
    pairs = [(i, i + step) for i in range(total) if 0 <= i + step < total]
    return lax.ppermute(array, "rows", pairs)


def rims(array, dim, shift):
    length = array.shape[dim]
    before = shift(lax.slice_in_dim(array, length - 1, length, axis=dim), 1)
    after = shift(lax.slice_in_dim(array, 0, 1, axis=dim), -1)
    return before, after


def joined(rim, array, dim):
    return jnp.concatenate([rim[0], array, rim[1]], axis=dim)


def extended(array, row_dim):
    array = joined(rims(array, row_dim, shift_rows), array, row_dim)
    return joined(rims(array, row_dim + 1, shift_cols), array, row_dim + 1)


def spread_all(stats):
    return lax.all_to_all(stats, EVERY, 0, 0)


def swap(array, axis, flip):
    total = lax.axis_size(axis)
    return lax.ppermute(array, axis, [(i, i ^ flip) for i in range(total)])


def spread_chips(shard):
    chips, rows = lax.axis_size("chips"), lax.axis_size("rows")
    width = shard.shape[-1] // rows
    mine = lax.dynamic_slice_in_dim(shard, lax.axis_index("rows") * width, width, axis=1)
    return [swap(mine, "chips", hop) for hop in range(1, chips)]


def spread_rows(shard, line):
    return [shard, line] + [swap(line, "rows", flip) for flip in range(1, lax.axis_size("rows"))]


def spread_cores(pieces):
    return pieces + [swap(piece, "core", 1) for piece in pieces]


def gather_weights(shard):
    rows = lax.axis_size("rows")
    part = shard.shape[1] // rows
    mine = lax.dynamic_slice_in_dim(shard, lax.axis_index("rows") * part, part, axis=1)
    return lax.all_gather(mine.astype(BF16), ("chips", "core", "rows"), axis=1, tiled=True)


def pick(array, axis, index):
    return lax.dynamic_index_in_dim(array, index, axis=axis, keepdims=False)


def summed(parts):
    total = parts[0].astype(F32)
    for part in parts[1:]:
        total = total + part.astype(F32)
    return total.astype(BF16)


def row_sends(parts):
    row = lax.axis_index("rows")
    return [pick(parts, 0, row ^ flip) for flip in range(lax.axis_size("rows"))]


def reduce_rows(sends):
    return [sends[0]] + [swap(part, "rows", flip) for flip, part in enumerate(sends) if flip]


def reduce_chips(parts):
    total = summed(parts)
    chip = lax.axis_index("chips")
    chips = lax.axis_size("chips")
    return [pick(total, 0, chip)] + [
        swap(pick(total, 0, chip ^ hop), "chips", hop) for hop in range(1, chips)
    ]


def pair_share(parts):
    total = summed(parts)
    core = lax.axis_index("core")
    kept = pick(total, 1, core)
    got = swap(pick(total, 1, 1 - core), "core", 1)
    low = jnp.where(core == 0, kept, got)
    high = jnp.where(core == 0, got, kept)
    return jnp.concatenate([low, high], axis=-1)


def share_rows(share):
    return [share] + [swap(share, "rows", flip) for flip in range(1, lax.axis_size("rows"))]


def update_kernel(rate, count, place_ref, weight_ref, moment_ref, average_ref, *refs):
    parts, outs = refs[:count], refs[-4:]
    turn = pl.program_id(1)
    for flip, part in enumerate(parts):

        @pl.when(turn == flip)
        def _():
            grad = part[...].astype(F32)[:, None]
            weight = weight_ref[...]
            descent = grad + WEIGHT_DECAY * weight
            mom_new = MOMENTUM * moment_ref[...] + descent
            weight_new = weight - rate * (descent + MOMENTUM * mom_new)
            outs[0][...] = grad
            outs[1][...] = mom_new
            outs[2][...] = weight_new
            outs[3][...] = AVERAGE * average_ref[...] + (1.0 - AVERAGE) * weight_new


def update(parts, weight, moment, average, rate, first, block, earlier=()):
    groups, depth, channels = weight.shape
    rows = lax.axis_size("rows")
    piece = depth // rows
    count = parts[0].shape[0]
    split = (groups, rows, piece, channels)
    weight, moment, average = (a.reshape(split) for a in (weight, moment, average))
    earlier = [a.reshape(split) for a in earlier]
    state = pl.BlockSpec(
        (pl.Element(block), pl.Element(1), pl.Element(piece), pl.Element(channels)),
        lambda g, t, p: (g * block + first, jnp.bitwise_xor(p[2], t), 0, 0),
    )
    grads = pl.BlockSpec((block, piece, channels), lambda g, t, p: (g, 0, 0))
    anywhere = pl.BlockSpec(memory_space=pl.ANY)
    outs = pl.pallas_call(
        functools.partial(update_kernel, rate, len(parts)),
        grid_spec=pltpu.PrefetchScalarGridSpec(
            num_scalar_prefetch=1,
            grid=(count // block, rows),
            in_specs=[state] * 3 + [grads] * len(parts) + [anywhere] * len(earlier),
            out_specs=[state] * 4,
        ),
        out_shape=[jax.ShapeDtypeStruct(split, F32)] * 4,
        input_output_aliases={4 + len(parts) + i: i for i in range(len(earlier))},
        compiler_params=pltpu.CompilerParams(vmem_limit_bytes=VMEM_LIMIT),
        cost_estimate=pl.CostEstimate(
            flops=0, bytes_accessed=30 * count * depth * channels, transcendentals=0
        ),
    )(place_of(), weight, moment, average, *parts, *earlier)
    return [a.reshape(groups, depth, channels) for a in outs]


def place_of():
    place = jnp.stack([lax.axis_index("chips"), lax.axis_index("core"), lax.axis_index("rows")])
    return place.astype(jnp.int32)


def halves(array):
    core = lax.axis_index("core")
    half = array.shape[-1] // 2
    mine = lax.dynamic_slice_in_dim(array, core * half, half, axis=array.ndim - 1)
    other = lax.dynamic_slice_in_dim(array, (1 - core) * half, half, axis=array.ndim - 1)
    return mine, lax.ppermute(other, "core", PAIR)


def refresh(weight, gradient, moment, average, step_rate):
    descent = gradient + WEIGHT_DECAY * weight
    mom_new = MOMENTUM * moment + descent
    weight_new = weight - step_rate * (descent + MOMENTUM * mom_new)
    avg_new = AVERAGE * average + (1.0 - AVERAGE) * weight_new
    return (mom_new, weight_new, avg_new)


def shards(
    features,
    extent,
    cotangent,
    wide_w,
    wide_mom,
    wide_avg,
    point_w,
    point_mom,
    point_avg,
    norm_w,
    norm_mom,
    norm_avg,
):
    tasks = point_w.shape[0] // 2
    images, rows, cols, channels = features.shape
    half_rows, half_cols = rows // 2, cols // 2
    rate_wide = 0.4 / (9.0 * channels) ** 0.5
    rate_point = 2.0 / float(channels) ** 0.5
    devices = lax.axis_size("rows") * lax.axis_size("chips") * lax.axis_size("core")
    row_start = lax.axis_index("rows") * rows
    col_start = (lax.axis_index("chips") * lax.axis_size("core") + lax.axis_index("core")) * cols
    starts = jnp.stack([row_start, col_start]).astype(jnp.int32)[:, None]
    full_ext = jnp.broadcast_to((extent - starts)[:, :, None], (2, images, channels))
    half_ext = jnp.broadcast_to((extent // 2 - starts // 2)[:, :, None], (2, images, channels))
    full_count = jnp.sum(extent[0] * extent[1]).astype(F32)
    all_rows = jnp.arange(lax.axis_size("rows"), dtype=jnp.int32)[:, None, None] * rows
    all_cols = jnp.arange(devices // lax.axis_size("rows"), dtype=jnp.int32)[None, :, None] * cols
    valid = jnp.clip(extent[0] - all_rows, 0, rows) * jnp.clip(extent[1] - all_cols, 0, cols)
    counts = jnp.sum(valid, axis=2).astype(F32).reshape(devices)
    own_count = jnp.sum(
        jnp.clip(extent[0] - row_start, 0, rows) * jnp.clip(extent[1] - col_start, 0, cols)
    ).astype(F32)
    own_inv = 1.0 / jnp.maximum(own_count, 1.0)
    meta = jnp.broadcast_to(
        jnp.stack(
            [
                1.0 / full_count,
                4.0 / full_count,
                lax.rsqrt(full_count / 16.0),
                own_count,
                own_inv,
                0.25 * own_count,
                4.0 * own_inv,
            ]
        )[:, None],
        (7, channels),
    )
    counts = jnp.broadcast_to(
        jnp.stack([counts, 0.25 * counts])[:, :, None, None], (2, devices, 1, channels)
    )
    place = place_of()
    shared_own = jnp.concatenate([wide_w[0], point_w.reshape(-1, channels)], axis=0).astype(BF16)
    hops = spread_chips(shared_own)
    features, line, full_ext, half_ext, meta, counts = lax.optimization_barrier(
        (features, jnp.stack(hops), full_ext, half_ext, meta, counts)
    )
    pieces = spread_rows(shared_own, line)
    maps = features.transpose(1, 2, 0, 3)
    row_ids = jnp.arange(rows, dtype=jnp.int32)[:, None, None]
    col_ids = jnp.arange(cols, dtype=jnp.int32)[None, :, None]
    inside = (row_ids < (extent[0] - row_start)[None, None]) & (col_ids < (extent[1] - col_start)[None, None])
    maps = jnp.where(inside[..., None], maps, jnp.zeros((), BF16))
    x_tall = joined(rims(maps, 0, shift_rows), maps, 0)
    later_w, x_tall = lax.optimization_barrier((wide_w[1:], x_tall))
    x_pad = joined(rims(x_tall, 1, shift_cols), x_tall, 1)
    pieces[-1], x_pad = lax.optimization_barrier((pieces[-1], x_pad))
    branch_w = gather_weights(later_w)
    branch_in = (branch_w, leading((1,) + branch_w.shape[1:]))
    pieces = spread_cores(pieces)
    x_other = lax.ppermute(x_pad, "core", PAIR)
    cot = cotangent.transpose(0, 2, 3, 1, 4)

    full = (rows, cols, images, channels)
    half = (half_rows, half_cols, images, channels)
    wide = (half_rows + 2, half_cols + 2, images, channels)
    quarter = (half_rows // 2, half_cols // 2, images, channels)
    stat = (devices, 2, channels)
    task_stat = (devices, tasks, 2, channels)
    one_stat = second_dim((devices, 1, 2, channels))
    meta_in = (meta, whole(meta.shape))
    count_in = (counts, whole(counts.shape))
    norm_in = (norm_w, whole(norm_w.shape))
    full_in = (full_ext, whole(full_ext.shape))
    half_in = (half_ext, whole(half_ext.shape))
    vec = pltpu.VMEM((2, channels), F32)
    place_in = (place, pl.BlockSpec(memory_space=pltpu.SMEM))
    anywhere = pl.BlockSpec(memory_space=pl.ANY)
    copies = 4 * (1 + lax.axis_size("rows") * (lax.axis_size("chips") - 1))

    point_split = (2 * lax.axis_size("chips"), 2 * tasks, point_w.shape[1], channels)
    point_flat = (point_split[0], point_split[1] * point_split[2], channels)
    point_block = (point_split[0], 1) + point_split[2:]
    weight = (9 * channels, channels)

    full_flops = 2 * 9 * rows * cols * images * channels * channels
    half_flops = full_flops // 4 * tasks
    task_of = lambda shape: leading((1,) + shape)

    block = 4
    z, local, shared_w, point_full = call(
        functools.partial(shared_fwd_kernel, block),
        rows // block,
        [place_in, (x_pad, whole(x_pad.shape)), meta_in, full_in] + [(p, anywhere) for p in pieces],
        [
            (shape_of(full, F32), leading((block,) + full[1:])),
            (shape_of(stat, BF16), whole(stat)),
            (shape_of(weight, BF16), anywhere),
            (shape_of(point_flat, BF16), anywhere),
        ],
        [
            vec,
            pltpu.VMEM(weight, BF16),
            pltpu.VMEM(point_flat, BF16),
            pltpu.SemaphoreType.DMA((copies,)),
            pltpu.SemaphoreType.DMA((2,)),
        ],
        full_flops,
    )
    point_full = point_full.reshape(point_split)
    first_ws = (point_full, pl.BlockSpec(point_block, lambda i: (0, i, 0, 0)))
    second_ws = (point_full, pl.BlockSpec(point_block, lambda i: (0, i + tasks, 0, 0)))
    stat0 = spread_all(local)

    pooled, local = call(
        functools.partial(pool_kernel, block),
        rows // block,
        [
            (z, leading((block,) + full[1:])),
            (stat0, whole(stat)),
            count_in,
            meta_in,
            norm_in,
            full_in,
            (
                point_full,
                pl.BlockSpec((point_split[0], tasks) + point_split[2:], lambda i: (0, 0, 0, 0)),
            ),
        ],
        [
            (shape_of(half, BF16), leading((block // 2,) + half[1:])),
            (shape_of(task_stat, BF16), whole(task_stat)),
        ],
        [pltpu.VMEM(half, BF16), vec],
    )
    pooled_wide = extended(pooled, 0)
    stat1 = spread_all(local)

    first, hidden, second, local = call(
        attend_kernel,
        tasks,
        [
            (pooled_wide, whole(wide)),
            (stat1, one_stat),
            count_in,
            meta_in,
            norm_in,
            half_in,
            first_ws,
            second_ws,
        ],
        [
            (shape_of((tasks,) + half, F32), task_of(half)),
            (shape_of((tasks,) + half, BF16), task_of(half)),
            (shape_of((tasks,) + wide, F32), task_of(wide)),
            (shape_of(task_stat, BF16), one_stat),
        ],
    )
    stat2 = spread_all(local)

    masked, branch, local = call(
        branch_fwd_kernel,
        tasks,
        [
            (second, task_of(wide)),
            (pooled_wide, whole(wide)),
            (stat2, one_stat),
            count_in,
            meta_in,
            norm_in,
            half_in,
            branch_in,
        ],
        [
            (shape_of((tasks,) + wide, BF16), task_of(wide)),
            (shape_of((tasks,) + half, F32), task_of(half)),
            (shape_of(task_stat, BF16), one_stat),
        ],
        flops=half_flops,
    )
    masked_other = lax.ppermute(masked, "core", PAIR)
    stat3 = spread_all(local)

    branch_ins = [
        (branch, task_of(half)),
        (cot, task_of(quarter)),
        (stat3, one_stat),
    ]
    result, local = call(
        result_kernel,
        tasks,
        branch_ins + [count_in, meta_in, norm_in, half_in],
        [
            (shape_of((tasks,) + quarter, BF16), task_of(quarter)),
            (shape_of(task_stat, BF16), one_stat),
        ],
    )
    back3 = spread_all(local)

    (branch_dz,) = call(
        branch_dz_kernel,
        tasks,
        branch_ins + [(back3, one_stat), count_in, meta_in, norm_in, half_in],
        [(shape_of((tasks,) + half, BF16), task_of(half))],
    )
    dz_other = halves(branch_dz)[1]
    dz_tall = joined(rims(branch_dz, 1, shift_rows), branch_dz, 1)
    dz_rim = rims(dz_tall, 2, shift_cols)
    narrow = half[:-1] + (channels // 2,)
    chips, quarters = lax.axis_size("chips"), lax.axis_size("rows")
    piece = 9 * channels // (2 * chips * quarters)
    (branch_grad,) = call(
        branch_wgrad_kernel,
        tasks,
        [
            place_in,
            (masked, task_of(wide)),
            (masked_other, task_of(wide)),
            (branch_dz, task_of(half)),
            (dz_other, task_of(narrow)),
        ],
        [
            (
                shape_of((quarters, chips, tasks, 2, piece, channels // 2), BF16),
                pl.BlockSpec(
                    (quarters, chips, 1, 2, piece, channels // 2), lambda i: (0, 0, i, 0, 0, 0)
                ),
            )
        ],
        flops=half_flops,
    )
    branch_grad, dz_rim = lax.optimization_barrier((branch_grad, dz_rim))
    branch_parts = lax.psum_scatter(branch_grad, "rows", scatter_dimension=0, tiled=True)[0]
    dz_wide = joined(dz_rim, dz_tall, 2)

    ga, product, local = call(
        branch_dgrad_kernel,
        tasks,
        [
            (dz_wide, task_of(wide)),
            branch_in,
            (second, task_of(wide)),
            (pooled, whole(half)),
            (stat2, one_stat),
            count_in,
            meta_in,
            norm_in,
        ],
        [
            (shape_of((tasks,) + half, F32), task_of(half)),
            (shape_of(half, F32), whole(half)),
            (shape_of(task_stat, BF16), one_stat),
        ],
        flops=half_flops,
    )
    back2 = spread_all(local)

    square = (channels, channels)
    second_grad, gl, local = call(
        attend_back_kernel,
        tasks,
        [
            (ga, task_of(half)),
            (second, task_of(wide)),
            (stat2, one_stat),
            (back2, one_stat),
            (hidden, task_of(half)),
            second_ws,
            (first, task_of(half)),
            (stat1, one_stat),
            count_in,
            meta_in,
            norm_in,
            half_in,
        ],
        [
            (shape_of((tasks,) + square, BF16), task_of(square)),
            (shape_of((tasks,) + half, F32), task_of(half)),
            (shape_of(task_stat, BF16), one_stat),
        ],
    )
    back1 = spread_all(local)

    first_grad, grad_pooled, local = call(
        functools.partial(pooled_back_kernel, block),
        tasks,
        [
            (gl, task_of(half)),
            (first, task_of(half)),
            (stat1, one_stat),
            (back1, one_stat),
            (pooled, whole(half)),
            first_ws,
            (product, whole(half)),
            (z, whole(full)),
            (stat0, whole(stat)),
            count_in,
            meta_in,
            norm_in,
            half_in,
            full_in,
        ],
        [
            (shape_of((tasks,) + square, BF16), task_of(square)),
            (shape_of(half, F32), whole(half)),
            (shape_of(stat, BF16), whole(stat)),
        ],
    )
    back0 = spread_all(local)
    point_local = jnp.concatenate([first_grad, second_grad], axis=0)
    point_own, point_other = halves(point_local)
    point_half, back0 = lax.optimization_barrier((point_own + point_other, back0))
    point_shape = (2 * tasks, chips, 2, quarters, channels // (2 * chips * quarters), channels // 2)
    point_parts = reduce_rows(row_sends(point_half.reshape(point_shape).transpose(3, 1, 0, 2, 4, 5)))

    (shared_dz,) = call(
        functools.partial(shared_dz_kernel, block),
        rows // block,
        [
            (z, leading((block,) + full[1:])),
            (grad_pooled, leading((block // 2,) + half[1:])),
            (stat0, whole(stat)),
            (back0, whole(stat)),
            count_in,
            meta_in,
            norm_in,
            full_in,
        ],
        [(shape_of(full, BF16), leading((block,) + full[1:]))],
    )
    branch_parts, shared_dz = lax.optimization_barrier((branch_parts, shared_dz))
    branch_parts = lax.psum_scatter(branch_parts, "chips", scatter_dimension=0, tiled=True)
    dz_other = halves(shared_dz)[1]
    dz_rim = rims(shared_dz, 0, shift_rows)
    (shared_grad,) = call(
        shared_wgrad_kernel,
        9,
        [
            place_in,
            (x_pad, whole(x_pad.shape)),
            (x_other, whole(x_other.shape)),
            (shared_dz, whole(full)),
            (dz_other, whole(dz_other.shape)),
        ],
        [
            (
                shape_of((quarters, chips, 1, 2, piece, channels // 2), BF16),
                whole((quarters, chips, 1, 2, piece, channels // 2)),
            )
        ],
        flops=full_flops,
    )
    sends = row_sends(shared_grad)
    point_parts, sends, dz_rim = lax.optimization_barrier((point_parts, sends, dz_rim))
    branch_parts, _ = lax.optimization_barrier((branch_parts, sends))
    shared_parts = reduce_rows(sends)
    dz_tall = joined(dz_rim, shared_dz, 0)
    dz_pad = joined(rims(dz_tall, 1, shift_cols), dz_tall, 1)
    branch_parts, dz_pad = lax.optimization_barrier((pair_share(branch_parts), dz_pad))
    branch_share = share_rows(branch_parts)
    point_parts = reduce_chips(point_parts)
    (input_grad,) = call(
        functools.partial(shared_dgrad_kernel, block),
        rows // block,
        [(dz_pad, whole(dz_pad.shape)), (shared_w, whole(weight)), full_in],
        [(shape_of(full, F32), leading((block,) + full[1:]))],
        flops=full_flops,
    )
    shared_parts, point_parts, input_grad = lax.optimization_barrier(
        (shared_parts, point_parts, input_grad)
    )
    shared_parts = reduce_chips(shared_parts)
    (back0, back1, back2, back3), _ = lax.optimization_barrier(
        ((back0, back1, back2, back3), input_grad)
    )
    branch_share, _ = lax.optimization_barrier((branch_share, input_grad))
    branch_state = update(branch_share, wide_w, wide_mom, wide_avg, rate_wide, 1, tasks)
    point_share = share_rows(pair_share(point_parts))
    shared_parts, branch_state = lax.optimization_barrier((shared_parts, branch_state))
    shared_share = share_rows(pair_share(shared_parts))
    input_grad = input_grad.transpose(2, 0, 1, 3)
    point_state = update(point_share, point_w, point_mom, point_avg, rate_point, 0, 2 * tasks)
    shared_share, point_state, input_grad = lax.optimization_barrier(
        (shared_share, point_state, input_grad)
    )
    point_share, point_mom_new, point_new, point_avg_new = point_state

    wide_share, wide_mom_new, wide_new, wide_avg_new = update(
        shared_share, wide_w, wide_mom, wide_avg, rate_wide, 0, 1, branch_state
    )
    bsum = jnp.stack([jnp.sum(b.astype(F32), axis=0) for b in (back1, back2, back3)], axis=1)
    bsum = bsum.transpose(2, 0, 1, 3).reshape(2, 3 * tasks, channels)
    norm_grad = jnp.concatenate([jnp.sum(back0.astype(F32), axis=0)[:, None], bsum], axis=1)[::-1]
    norm_mom_new, norm_new, norm_avg_new = refresh(norm_w, norm_grad, norm_mom, norm_avg, RATE_NORM)
    return (
        result.transpose(0, 3, 1, 2, 4),
        input_grad,
        wide_share,
        wide_mom_new,
        wide_new,
        wide_avg_new,
        point_share,
        point_mom_new,
        point_new,
        point_avg_new,
        norm_grad,
        norm_mom_new,
        norm_new,
        norm_avg_new,
    )


def solution(mesh):
    rows, cols = mesh.devices.shape
    cores = 2
    fine = Mesh(mesh.devices.reshape(rows, cols // cores, cores), EVERY)
    across = ("chips", "core")
    weights = P(None, across, None)
    placed = (
        P(None, "rows", across, None),
        P(),
        P(None, None, "rows", across, None),
        weights,
        weights,
        weights,
        weights,
        weights,
        weights,
        P(),
        P(),
        P(),
    )
    return jax.shard_map(
        shards,
        mesh=fine,
        in_specs=placed,
        out_specs=(
            P(None, None, "rows", across, None),
            P(None, "rows", across, None),
            weights,
            weights,
            weights,
            weights,
            weights,
            weights,
            weights,
            weights,
            P(),
            P(),
            P(),
            P(),
        ),
        check_vma=False,
    )
```

```python
import functools

import jax
import jax.numpy as jnp
from jax import lax
from jax.experimental import pallas as pl
from jax.experimental.pallas import tpu as pltpu
from jax.sharding import Mesh
from jax.sharding import PartitionSpec as P

EPSILON = 1e-05
MOMENTUM = 0.9
WEIGHT_DECAY = 0.0001
AVERAGE = 0.6
RATE_NORM = 0.4
F32 = jnp.float32
BF16 = jnp.bfloat16
EVERY = ("rows", "chips", "core")
PAIR = [(0, 1), (1, 0)]
VMEM_LIMIT = 56 * 1024 * 1024


def sigmoid(values):
    return 0.5 * jnp.tanh(0.5 * values) + 0.5


def flat(values):
    return values.reshape((-1, values.shape[-1]))


def square_of(ref):
    return ref[...].reshape(ref.shape[-1], ref.shape[-1])


def mask_of(ext_ref, row, col, rows, cols):
    shape = (rows, cols) + ext_ref.shape[1:]
    row_ids = row + lax.broadcasted_iota(jnp.int32, shape, 0)
    col_ids = col + lax.broadcasted_iota(jnp.int32, shape, 1)
    inside = (row_ids < ext_ref[0][None, None]) & (col_ids < ext_ref[1][None, None])
    return inside


def keep(inside, values):
    return jnp.where(inside, values, 0.0)


def sums_of(first, second):
    return jnp.concatenate(
        [jnp.sum(flat(first), axis=0, keepdims=True), jnp.sum(flat(second), axis=0, keepdims=True)],
        axis=0,
    )


def centered(sums, local):
    center = (sums[0:1] * local[1:2]).astype(BF16)
    wide = center.astype(F32)
    spread = sums[1:2] - 2.0 * wide * sums[0:1] + local[0:1] * wide * wide
    return jnp.concatenate([wide, spread], axis=0).astype(BF16)


def moments(stats, counts, inv_count):
    stats = stats.astype(F32)
    centers = stats[:, 0:1]
    center = jnp.sum(counts * centers, axis=0) * inv_count
    off = centers - center[None]
    spread = jnp.sum(stats[:, 1:2] + counts * off * off, axis=0) * inv_count
    return center, lax.rsqrt(spread + EPSILON)


def taps_dot(source, weight, rows, cols, row, mirrored):
    channels = weight.shape[-1]
    total = None
    for tap in range(9):
        dr, dc = tap // 3, tap % 3
        if mirrored:
            dr, dc = 2 - dr, 2 - dc
        window = flat(source[pl.ds(row + dr, rows), dc : dc + cols])
        block = weight[tap * channels : (tap + 1) * channels, :]
        dims = (((1,), (1,)), ((), ())) if mirrored else (((1,), (0,)), ((), ()))
        part = lax.dot_general(window, block, dims, preferred_element_type=F32)
        total = part if total is None else total + part
    return total


def dot(left, right):
    return jnp.dot(left, right, preferred_element_type=F32)


def dot_nt(left, right):
    return lax.dot_general(left, right, (((1,), (1,)), ((), ())), preferred_element_type=F32)


def dot_tn(left, right):
    return lax.dot_general(left, right, (((0,), (0,)), ((), ())), preferred_element_type=F32)


def assemble(place_ref, pieces, w_ref, point_ref, sem, start):
    chip, core, row = place_ref[0], place_ref[1], place_ref[2]
    half = len(pieces) // 2
    depth = w_ref.shape[0] // point_ref.shape[0]
    count = 0
    for side in range(2):
        own, parts = pieces[side * half], pieces[side * half + 1 : (side + 1) * half]
        width = parts[0].shape[-1]
        at_core = core if side == 0 else 1 - core

        def run(source, shard, lanes, at):
            base = pl.multiple_of(shard * depth, 16)
            rest = source.shape[0] - depth
            pairs = (
                (source.at[pl.ds(0, depth)], w_ref.at[pl.ds(base, depth), lanes]),
                (source.at[pl.ds(depth, rest)], point_ref.at[shard, :, lanes]),
            )
            for i, (left, right) in enumerate(pairs):
                copy = pltpu.make_async_copy(left, right, sem.at[at + i])
                copy.start() if start else copy.wait()

        run(own, 2 * chip + at_core, pl.ds(0, own.shape[1]), count)
        count += 2
        for flip, part in enumerate(parts):
            lane = pl.multiple_of(jnp.bitwise_xor(row, flip) * width, 128)
            for hop in range(part.shape[0]):
                shard = 2 * jnp.bitwise_xor(chip, hop + 1) + at_core
                run(part.at[hop], shard, pl.ds(lane, width), count)
                count += 2


def gathered(place_ref, pieces, w_ref, point_ref, sem, w_out, point_out, out_sem):
    copies = (
        pltpu.make_async_copy(w_ref, w_out, out_sem.at[0]),
        pltpu.make_async_copy(point_ref, point_out, out_sem.at[1]),
    )

    @pl.when(pl.program_id(0) == 0)
    def _():
        assemble(place_ref, pieces, w_ref, point_ref, sem, True)
        assemble(place_ref, pieces, w_ref, point_ref, sem, False)
        for copy in copies:
            copy.start()

    @pl.when(pl.program_id(0) == pl.num_programs(0) - 1)
    def _():
        for copy in copies:
            copy.wait()


def shared_fwd_kernel(rows, place_ref, x_ref, meta_ref, ext_ref, *refs):
    *pieces, z_ref, stat_ref, w_out, point_out, acc_ref, w_ref, point_ref, sem, out_sem = refs
    gathered(place_ref, pieces, w_ref, point_ref, sem, w_out, point_out, out_sem)
    step = pl.program_id(0)
    cols = z_ref.shape[1]
    z = taps_dot(x_ref, w_ref, rows, cols, step * rows, False).reshape(z_ref.shape)
    z_ref[...] = z
    zm = keep(mask_of(ext_ref, step * rows, 0, rows, cols), z)
    part = sums_of(zm, zm * z)

    @pl.when(step == 0)
    def _():
        acc_ref[...] = part

    @pl.when(step > 0)
    def _():
        acc_ref[...] += part

    @pl.when(step == pl.num_programs(0) - 1)
    def _():
        stat_ref[...] = jnp.broadcast_to(centered(acc_ref[...], meta_ref[3:5])[None], stat_ref.shape)


def pool_kernel(rows, z_ref, stat_ref, count_ref, meta_ref, norm_ref, ext_ref, p_ref, out_ref, st_ref, pool_ref, aff_ref):
    step = pl.program_id(0)
    cols = z_ref.shape[1]

    @pl.when(step == 0)
    def _():
        center, inverse = moments(stat_ref[...], count_ref[0], meta_ref[0:1])
        scale = inverse * norm_ref[0, 0:1]
        aff_ref[0:1] = scale
        aff_ref[1:2] = norm_ref[1, 0:1] - center * scale

    v = z_ref[...] * aff_ref[0:1] + aff_ref[1:2]
    lifted = keep(mask_of(ext_ref, step * rows, 0, rows, cols), v * sigmoid(v))
    grouped = lifted.reshape((rows // 2, 2, cols // 2, 2) + lifted.shape[2:])
    mean = 0.25 * (
        (grouped[:, 0, :, 0] + grouped[:, 0, :, 1]) + (grouped[:, 1, :, 0] + grouped[:, 1, :, 1])
    )
    low = mean.astype(BF16)
    out_ref[...] = low
    pool_ref[pl.ds(step * (rows // 2), rows // 2)] = low

    @pl.when(step == pl.num_programs(0) - 1)
    def _():
        left = flat(pool_ref[...])
        channels = left.shape[-1]
        for task in range(p_ref.shape[1]):
            f = dot(left, p_ref[:, task].reshape(channels, channels))
            st_ref[:, task] = jnp.broadcast_to(
                centered(sums_of(f, f * f), meta_ref[5:7])[None], (st_ref.shape[0],) + st_ref.shape[2:]
            )


def task_norm(stat_ref, count_ref, meta_ref, norm_ref, task, slot):
    center, inverse = moments(stat_ref[:, 0], count_ref[1], meta_ref[1:2])
    row = 1 + 3 * task + slot
    gain = norm_ref[0, pl.ds(row, 1)]
    bias = norm_ref[1, pl.ds(row, 1)]
    return center, inverse, gain, bias


def attend_kernel(pe_ref, stat_ref, count_ref, meta_ref, norm_ref, ext_ref, p1_ref, p2_ref, first_ref, hidden_ref, second_ref, st_ref):
    task = pl.program_id(0)
    shape = pe_ref.shape
    rows, cols = shape[0] - 2, shape[1] - 2
    center, inverse, gain, bias = task_norm(stat_ref, count_ref, meta_ref, norm_ref, task, 0)
    scale = inverse * gain
    shift = bias - center * scale
    first = dot(flat(pe_ref[...]), square_of(p1_ref))
    first_ref[0] = first.reshape(shape)[1 : 1 + rows, 1 : 1 + cols]
    v = first * scale + shift
    inside = mask_of(ext_ref, -1, -1, rows + 2, cols + 2)
    hidden = keep(inside, (v * sigmoid(v)).reshape(shape)).astype(BF16)
    hidden_ref[0] = hidden[1 : 1 + rows, 1 : 1 + cols]
    second = dot(flat(hidden), square_of(p2_ref)).reshape(shape)
    second_ref[0] = second
    own = second[1 : 1 + rows, 1 : 1 + cols]
    local = centered(sums_of(own, own * own), meta_ref[5:7])
    st_ref[:, 0] = jnp.broadcast_to(local[None], (st_ref.shape[0],) + st_ref.shape[2:])


def branch_fwd_kernel(second_ref, pe_ref, stat_ref, count_ref, meta_ref, norm_ref, ext_ref, w_ref, masked_ref, branch_ref, st_ref):
    task = pl.program_id(0)
    rows, cols = branch_ref.shape[1:3]
    center, inverse, gain, bias = task_norm(stat_ref, count_ref, meta_ref, norm_ref, task, 1)
    scale = inverse * gain
    shift = bias - center * scale
    attention = sigmoid(second_ref[0] * scale + shift)
    masked_ref[0] = (attention * pe_ref[...].astype(F32)).astype(BF16)
    z = taps_dot(masked_ref.at[0], w_ref.at[0], rows, cols, 0, False).reshape(branch_ref.shape[1:])
    branch_ref[0] = z
    zm = keep(mask_of(ext_ref, 0, 0, rows, cols), z)
    local = centered(sums_of(zm, zm * z), meta_ref[5:7])
    st_ref[:, 0] = jnp.broadcast_to(local[None], (st_ref.shape[0],) + st_ref.shape[2:])


def branch_grad_terms(branch_ref, cot_ref, stat_ref, count_ref, meta_ref, norm_ref, ext_ref, task):
    rows, cols = branch_ref.shape[1:3]
    center, inverse, gain, bias = task_norm(stat_ref, count_ref, meta_ref, norm_ref, task, 2)
    zhat = (branch_ref[0] - center) * inverse
    v = zhat * gain + bias
    s = sigmoid(v)
    inside = mask_of(ext_ref, 0, 0, rows, cols)
    c = cot_ref[0].astype(F32) * (0.25 * meta_ref[2:3])
    spread = jnp.broadcast_to(c[:, None, :, None], (rows // 2, 2, cols // 2, 2) + c.shape[2:])
    upstream = keep(inside, spread.reshape(v.shape) * (s * (1.0 + v * (1.0 - s))))
    return zhat, v, s, inside, upstream, gain * inverse


def result_kernel(branch_ref, cot_ref, stat_ref, count_ref, meta_ref, norm_ref, ext_ref, out_ref, st_ref):
    task = pl.program_id(0)
    rows, cols = branch_ref.shape[1:3]
    zhat, v, s, inside, upstream, _ = branch_grad_terms(
        branch_ref, cot_ref, stat_ref, count_ref, meta_ref, norm_ref, ext_ref, task
    )
    active = keep(inside, v * s)
    grouped = active.reshape((rows // 2, 2, cols // 2, 2) + active.shape[2:])
    mean = 0.25 * (
        (grouped[:, 0, :, 0] + grouped[:, 0, :, 1]) + (grouped[:, 1, :, 0] + grouped[:, 1, :, 1])
    )
    out_ref[0] = mean.astype(BF16)
    st_ref[:, 0] = jnp.broadcast_to(
        sums_of(upstream, upstream * zhat).astype(BF16)[None], (st_ref.shape[0],) + st_ref.shape[2:]
    )


def back_sums(stat_ref, inv_count):
    total = jnp.sum(stat_ref[:, 0].astype(F32), axis=0)
    return total[0:1] * inv_count, total[1:2] * inv_count


def branch_dz_kernel(branch_ref, cot_ref, stat_ref, back_ref, count_ref, meta_ref, norm_ref, ext_ref, dz_ref):
    task = pl.program_id(0)
    zhat, v, s, inside, upstream, factor = branch_grad_terms(
        branch_ref, cot_ref, stat_ref, count_ref, meta_ref, norm_ref, ext_ref, task
    )
    bias_mean, gain_mean = back_sums(back_ref, meta_ref[1:2])
    dz_ref[0] = keep(inside, factor * (upstream - bias_mean - zhat * gain_mean)).astype(BF16)


def branch_dgrad_kernel(dz_ref, w_ref, second_ref, pooled_ref, stat_ref, count_ref, meta_ref, norm_ref, ga_ref, prod_ref, st_ref):
    task = pl.program_id(0)
    shape = pooled_ref.shape
    rows, cols = shape[:2]
    center, inverse, gain, bias = task_norm(stat_ref, count_ref, meta_ref, norm_ref, task, 1)
    grad = taps_dot(dz_ref.at[0], w_ref.at[0], rows, cols, 0, True).reshape(shape)
    zhat = (second_ref[0, 1 : 1 + rows, 1 : 1 + cols] - center) * inverse
    attention = sigmoid(zhat * gain + bias)
    through = grad * attention
    ga = through * pooled_ref[...].astype(F32) * (1.0 - attention)
    ga_ref[0] = ga

    @pl.when(task == 0)
    def _():
        prod_ref[...] = through

    @pl.when(task > 0)
    def _():
        prod_ref[...] += through

    st_ref[:, 0] = jnp.broadcast_to(sums_of(ga, ga * zhat).astype(BF16)[None], (st_ref.shape[0],) + st_ref.shape[2:])


def scatter_tap(out_ref, task, tap, total):
    quarters, piece = out_ref.shape[0], out_ref.shape[4]
    channels = total.shape[0]
    at, end = tap * channels, (tap + 1) * channels
    while at < end:
        block, inside = at // piece, at % piece
        size = min(piece - inside, end - at)
        shard, quarter = block // quarters, block % quarters
        out_ref[quarter, shard // 2, task, shard % 2, inside : inside + size] = total[
            at - tap * channels : at - tap * channels + size
        ]
        at += size


def own_half(place_ref, ref):
    half = ref.shape[-1] // 2
    lanes = pl.ds(pl.multiple_of(place_ref[1] * half, 128), half)
    return flat(ref[..., lanes].reshape(-1, half))


def branch_wgrad_kernel(place_ref, own_ref, other_ref, dz_own_ref, dz_other_ref, out_ref):
    rows, cols = dz_own_ref.shape[1:3]
    own = own_half(place_ref, dz_own_ref)
    other = flat(dz_other_ref[0])
    for tap in range(9):
        dr, dc = tap // 3, tap % 3
        total = dot_tn(flat(own_ref[0, dr : dr + rows, dc : dc + cols]), own)
        total += dot_tn(flat(other_ref[0, dr : dr + rows, dc : dc + cols]), other)
        scatter_tap(out_ref, 0, tap, total.astype(BF16))


def by_halves(ref, values):
    half = values.shape[1] // 2
    ref[0, 0] = values[:, :half].astype(BF16)
    ref[1, 0] = values[:, half:].astype(BF16)


def attend_back_kernel(ga_ref, second_ref, stat2_ref, back_ref, hidden_ref, p2_ref, first_ref, stat1_ref, count_ref, meta_ref, norm_ref, ext_ref, wg_ref, gl_ref, st_ref):
    task = pl.program_id(0)
    shape = ga_ref.shape[1:]
    rows, cols = shape[:2]
    center, inverse, gain, _ = task_norm(stat2_ref, count_ref, meta_ref, norm_ref, task, 1)
    zhat = (second_ref[0, 1 : 1 + rows, 1 : 1 + cols] - center) * inverse
    bias_mean, gain_mean = back_sums(back_ref, meta_ref[1:2])
    inside = mask_of(ext_ref, 0, 0, rows, cols)
    dz = keep(inside, gain * inverse * (ga_ref[0] - bias_mean - zhat * gain_mean)).astype(BF16)
    by_halves(wg_ref, dot_tn(flat(hidden_ref[0]), flat(dz)))
    grad_hidden = dot_nt(flat(dz), square_of(p2_ref)).reshape(shape)
    center, inverse, gain, bias = task_norm(stat1_ref, count_ref, meta_ref, norm_ref, task, 0)
    zhat = (first_ref[0] - center) * inverse
    v = zhat * gain + bias
    s = sigmoid(v)
    gl = keep(inside, grad_hidden * (s * (1.0 + v * (1.0 - s))))
    gl_ref[0] = gl
    st_ref[:, 0] = jnp.broadcast_to(sums_of(gl, gl * zhat).astype(BF16)[None], (st_ref.shape[0],) + st_ref.shape[2:])


def unpool(grad, rows, cols):
    spread = jnp.broadcast_to(grad[:, None, :, None], (rows // 2, 2, cols // 2, 2) + grad.shape[2:])
    return spread.reshape((rows, cols) + grad.shape[2:])


def shared_grad_terms(z, grad, center, inverse, gain, bias, inside):
    zhat = (z - center) * inverse
    v = zhat * gain + bias
    s = sigmoid(v)
    upstream = keep(inside, unpool(0.25 * grad, z.shape[0], z.shape[1]) * (s * (1.0 + v * (1.0 - s))))
    return zhat, upstream


def pooled_back_kernel(chunk, gl_ref, first_ref, stat1_ref, back_ref, pooled_ref, p1_ref, prod_ref, z_ref, stat0_ref, count_ref, meta_ref, norm_ref, ext_ref, full_ref, earlier_ref, wg_ref, gp_ref, st_ref):
    task = pl.program_id(0)
    shape = gl_ref.shape[1:]
    rows, cols = shape[:2]
    center, inverse, gain, _ = task_norm(stat1_ref, count_ref, meta_ref, norm_ref, task, 0)
    zhat = (first_ref[0] - center) * inverse
    bias_mean, gain_mean = back_sums(back_ref, meta_ref[1:2])
    inside = mask_of(ext_ref, 0, 0, rows, cols)
    dz = keep(inside, gain * inverse * (gl_ref[0] - bias_mean - zhat * gain_mean)).astype(BF16)
    by_halves(wg_ref, dot_tn(flat(pooled_ref[...]), flat(dz)))
    grad = dot_nt(flat(dz), square_of(p1_ref)).reshape(shape)

    @pl.when(task == 0)
    def _():
        gp_ref[...] = prod_ref[...] + grad

    @pl.when(task > 0)
    def _():
        gp_ref[...] += grad

    @pl.when(task == pl.num_programs(0) - 1)
    def _():
        center, inverse = moments(stat0_ref[...], count_ref[0], meta_ref[0:1])
        gain, bias = norm_ref[0, 0:1], norm_ref[1, 0:1]
        full_rows, full_cols = z_ref.shape[:2]

        def body(i, total):
            row = i * chunk
            inside = mask_of(full_ref, row, 0, chunk, full_cols)
            zhat, upstream = shared_grad_terms(
                z_ref[pl.ds(row, chunk)], gp_ref[pl.ds(i * (chunk // 2), chunk // 2)],
                center, inverse, gain, bias, inside,
            )
            return total + sums_of(upstream, upstream * zhat)

        total = lax.fori_loop(0, full_rows // chunk, body, jnp.zeros((2, st_ref.shape[2]), F32))
        st_ref[...] = jnp.broadcast_to(total.astype(BF16)[None], st_ref.shape)


def shared_dz_kernel(rows, z_ref, gp_ref, stat_ref, back_ref, count_ref, meta_ref, norm_ref, ext_ref, dz_ref):
    step = pl.program_id(0)
    cols = z_ref.shape[1]
    center, inverse = moments(stat_ref[...], count_ref[0], meta_ref[0:1])
    gain, bias = norm_ref[0, 0:1], norm_ref[1, 0:1]
    total = jnp.sum(back_ref[...].astype(F32), axis=0) * meta_ref[0:1]
    inside = mask_of(ext_ref, step * rows, 0, rows, cols)
    zhat, upstream = shared_grad_terms(z_ref[...], gp_ref[...], center, inverse, gain, bias, inside)
    dz = gain * inverse * (upstream - total[0:1] - zhat * total[1:2])
    dz_ref[...] = keep(inside, dz).astype(BF16)


def shared_wgrad_kernel(place_ref, own_ref, other_ref, dz_own_ref, dz_other_ref, out_ref):
    turn = pl.program_id(0)
    rows, cols = dz_own_ref.shape[:2]
    own = own_half(place_ref, dz_own_ref)
    other = flat(dz_other_ref[...])
    for tap in range(9):

        @pl.when(turn == tap)
        def _():
            dr, dc = tap // 3, tap % 3
            total = dot_tn(flat(own_ref[dr : dr + rows, dc : dc + cols]), own)
            total += dot_tn(flat(other_ref[dr : dr + rows, dc : dc + cols]), other)
            scatter_tap(out_ref, 0, tap, total.astype(BF16))


def shared_dgrad_kernel(rows, dz_ref, w_ref, ext_ref, out_ref):
    step = pl.program_id(0)
    images, _, cols, channels = out_ref.shape
    grad = taps_dot(dz_ref, w_ref, rows, cols, step * rows, True)
    grad = grad.reshape(rows, cols, images, channels)
    grad = keep(mask_of(ext_ref, step * rows, 0, rows, cols), grad)
    for row in range(rows):
        for col in range(cols):
            out_ref[:, row, col] = grad[row, col]


def whole(shape):
    return pl.BlockSpec(shape, lambda i: (0,) * len(shape))


def leading(shape):
    return pl.BlockSpec(shape, lambda i: (i,) + (0,) * (len(shape) - 1))


def second_dim(shape):
    return pl.BlockSpec(shape, lambda i: (0, i) + (0,) * (len(shape) - 2))


def call(kernel, grid, ins, outs, scratch=(), flops=0, aliases=None):
    arrays = [array for array, _ in ins]
    moved = sum(a.size * a.dtype.itemsize for a in arrays)
    moved += sum(s.size * s.dtype.itemsize for s, _ in outs)
    return pl.pallas_call(
        kernel,
        grid=(grid,),
        in_specs=[spec for _, spec in ins],
        out_specs=[spec for _, spec in outs],
        out_shape=[shape for shape, _ in outs],
        scratch_shapes=list(scratch),
        input_output_aliases=aliases or {},
        compiler_params=pltpu.CompilerParams(vmem_limit_bytes=VMEM_LIMIT),
        cost_estimate=pl.CostEstimate(flops=flops, bytes_accessed=moved, transcendentals=0),
    )(*arrays)


def shape_of(shape, dtype):
    return jax.ShapeDtypeStruct(shape, dtype)


def shift_cols(array, step):
    chips, cores = lax.axis_size("chips"), lax.axis_size("core")
    total = chips * cores
    pairs = [(i, i + step) for i in range(total) if 0 <= i + step < total]
    return lax.ppermute(array, ("chips", "core"), pairs)


def shift_rows(array, step):
    total = lax.axis_size("rows")
    pairs = [(i, i + step) for i in range(total) if 0 <= i + step < total]
    return lax.ppermute(array, "rows", pairs)


def rims(array, dim, shift):
    length = array.shape[dim]
    before = shift(lax.slice_in_dim(array, length - 1, length, axis=dim), 1)
    after = shift(lax.slice_in_dim(array, 0, 1, axis=dim), -1)
    return before, after


def joined(rim, array, dim):
    return jnp.concatenate([rim[0], array, rim[1]], axis=dim)


def extended(array, row_dim):
    array = joined(rims(array, row_dim, shift_rows), array, row_dim)
    return joined(rims(array, row_dim + 1, shift_cols), array, row_dim + 1)


def spread_all(stats):
    return lax.all_to_all(stats, EVERY, 0, 0)


def swap(array, axis, flip):
    total = lax.axis_size(axis)
    return lax.ppermute(array, axis, [(i, i ^ flip) for i in range(total)])


def spread_chips(shard):
    chips, rows = lax.axis_size("chips"), lax.axis_size("rows")
    width = shard.shape[-1] // rows
    mine = lax.dynamic_slice_in_dim(shard, lax.axis_index("rows") * width, width, axis=1)
    return [swap(mine, "chips", hop) for hop in range(1, chips)]


def spread_rows(shard, line):
    return [shard, line] + [swap(line, "rows", flip) for flip in range(1, lax.axis_size("rows"))]


def spread_cores(pieces):
    return pieces + [swap(piece, "core", 1) for piece in pieces]


def gather_weights(shard):
    rows = lax.axis_size("rows")
    part = shard.shape[1] // rows
    mine = lax.dynamic_slice_in_dim(shard, lax.axis_index("rows") * part, part, axis=1)
    return lax.all_gather(mine.astype(BF16), ("chips", "core", "rows"), axis=1, tiled=True)


def pick(array, axis, index):
    return lax.dynamic_index_in_dim(array, index, axis=axis, keepdims=False)


def summed(parts):
    total = parts[0].astype(F32)
    for part in parts[1:]:
        total = total + part.astype(F32)
    return total.astype(BF16)


def row_sends(parts):
    row = lax.axis_index("rows")
    return [pick(parts, 0, row ^ flip) for flip in range(lax.axis_size("rows"))]


def reduce_rows(sends):
    return [sends[0]] + [swap(part, "rows", flip) for flip, part in enumerate(sends) if flip]


def reduce_chips(parts):
    total = summed(parts)
    chip = lax.axis_index("chips")
    chips = lax.axis_size("chips")
    return [pick(total, 0, chip)] + [
        swap(pick(total, 0, chip ^ hop), "chips", hop) for hop in range(1, chips)
    ]


def pair_share(parts):
    total = summed(parts)
    core = lax.axis_index("core")
    kept = pick(total, 1, core)
    got = swap(pick(total, 1, 1 - core), "core", 1)
    low = jnp.where(core == 0, kept, got)
    high = jnp.where(core == 0, got, kept)
    return jnp.concatenate([low, high], axis=-1)


def share_rows(share):
    return [share] + [swap(share, "rows", flip) for flip in range(1, lax.axis_size("rows"))]


def update_kernel(rate, count, place_ref, weight_ref, moment_ref, average_ref, *refs):
    parts, outs = refs[:count], refs[-4:]
    turn = pl.program_id(1)
    for flip, part in enumerate(parts):

        @pl.when(turn == flip)
        def _():
            grad = part[...].astype(F32)[:, None]
            weight = weight_ref[...]
            descent = grad + WEIGHT_DECAY * weight
            mom_new = MOMENTUM * moment_ref[...] + descent
            weight_new = weight - rate * (descent + MOMENTUM * mom_new)
            outs[0][...] = grad
            outs[1][...] = mom_new
            outs[2][...] = weight_new
            outs[3][...] = AVERAGE * average_ref[...] + (1.0 - AVERAGE) * weight_new


def update(parts, weight, moment, average, rate, first, block, earlier=()):
    groups, depth, channels = weight.shape
    rows = lax.axis_size("rows")
    piece = depth // rows
    count = parts[0].shape[0]
    split = (groups, rows, piece, channels)
    weight, moment, average = (a.reshape(split) for a in (weight, moment, average))
    earlier = [a.reshape(split) for a in earlier]
    state = pl.BlockSpec(
        (pl.Element(block), pl.Element(1), pl.Element(piece), pl.Element(channels)),
        lambda g, t, p: (g * block + first, jnp.bitwise_xor(p[2], t), 0, 0),
    )
    grads = pl.BlockSpec((block, piece, channels), lambda g, t, p: (g, 0, 0))
    anywhere = pl.BlockSpec(memory_space=pl.ANY)
    outs = pl.pallas_call(
        functools.partial(update_kernel, rate, len(parts)),
        grid_spec=pltpu.PrefetchScalarGridSpec(
            num_scalar_prefetch=1,
            grid=(count // block, rows),
            in_specs=[state] * 3 + [grads] * len(parts) + [anywhere] * len(earlier),
            out_specs=[state] * 4,
        ),
        out_shape=[jax.ShapeDtypeStruct(split, F32)] * 4,
        input_output_aliases={4 + len(parts) + i: i for i in range(len(earlier))},
        compiler_params=pltpu.CompilerParams(vmem_limit_bytes=VMEM_LIMIT),
        cost_estimate=pl.CostEstimate(
            flops=0, bytes_accessed=30 * count * depth * channels, transcendentals=0
        ),
    )(place_of(), weight, moment, average, *parts, *earlier)
    return [a.reshape(groups, depth, channels) for a in outs]


def place_of():
    place = jnp.stack([lax.axis_index("chips"), lax.axis_index("core"), lax.axis_index("rows")])
    return place.astype(jnp.int32)


def halves(array):
    core = lax.axis_index("core")
    half = array.shape[-1] // 2
    mine = lax.dynamic_slice_in_dim(array, core * half, half, axis=array.ndim - 1)
    other = lax.dynamic_slice_in_dim(array, (1 - core) * half, half, axis=array.ndim - 1)
    return mine, lax.ppermute(other, "core", PAIR)


def refresh(weight, gradient, moment, average, step_rate):
    descent = gradient + WEIGHT_DECAY * weight
    mom_new = MOMENTUM * moment + descent
    weight_new = weight - step_rate * (descent + MOMENTUM * mom_new)
    avg_new = AVERAGE * average + (1.0 - AVERAGE) * weight_new
    return (mom_new, weight_new, avg_new)


def shards(
    features,
    extent,
    cotangent,
    wide_w,
    wide_mom,
    wide_avg,
    point_w,
    point_mom,
    point_avg,
    norm_w,
    norm_mom,
    norm_avg,
):
    tasks = point_w.shape[0] // 2
    images, rows, cols, channels = features.shape
    half_rows, half_cols = rows // 2, cols // 2
    rate_wide = 0.4 / (9.0 * channels) ** 0.5
    rate_point = 2.0 / float(channels) ** 0.5
    devices = lax.axis_size("rows") * lax.axis_size("chips") * lax.axis_size("core")
    row_start = lax.axis_index("rows") * rows
    col_start = (lax.axis_index("chips") * lax.axis_size("core") + lax.axis_index("core")) * cols
    starts = jnp.stack([row_start, col_start]).astype(jnp.int32)[:, None]
    full_ext = jnp.broadcast_to((extent - starts)[:, :, None], (2, images, channels))
    half_ext = jnp.broadcast_to((extent // 2 - starts // 2)[:, :, None], (2, images, channels))
    full_count = jnp.sum(extent[0] * extent[1]).astype(F32)
    all_rows = jnp.arange(lax.axis_size("rows"), dtype=jnp.int32)[:, None, None] * rows
    all_cols = jnp.arange(devices // lax.axis_size("rows"), dtype=jnp.int32)[None, :, None] * cols
    valid = jnp.clip(extent[0] - all_rows, 0, rows) * jnp.clip(extent[1] - all_cols, 0, cols)
    counts = jnp.sum(valid, axis=2).astype(F32).reshape(devices)
    own_count = jnp.sum(
        jnp.clip(extent[0] - row_start, 0, rows) * jnp.clip(extent[1] - col_start, 0, cols)
    ).astype(F32)
    own_inv = 1.0 / jnp.maximum(own_count, 1.0)
    meta = jnp.broadcast_to(
        jnp.stack(
            [
                1.0 / full_count,
                4.0 / full_count,
                lax.rsqrt(full_count / 16.0),
                own_count,
                own_inv,
                0.25 * own_count,
                4.0 * own_inv,
            ]
        )[:, None],
        (7, channels),
    )
    counts = jnp.broadcast_to(
        jnp.stack([counts, 0.25 * counts])[:, :, None, None], (2, devices, 1, channels)
    )
    place = place_of()
    shared_own = jnp.concatenate([wide_w[0], point_w.reshape(-1, channels)], axis=0).astype(BF16)
    hops = spread_chips(shared_own)
    features, line, full_ext, half_ext, meta, counts = lax.optimization_barrier(
        (features, jnp.stack(hops), full_ext, half_ext, meta, counts)
    )
    pieces = spread_rows(shared_own, line)
    maps = features.transpose(1, 2, 0, 3)
    row_ids = jnp.arange(rows, dtype=jnp.int32)[:, None, None]
    col_ids = jnp.arange(cols, dtype=jnp.int32)[None, :, None]
    inside = (row_ids < (extent[0] - row_start)[None, None]) & (col_ids < (extent[1] - col_start)[None, None])
    maps = jnp.where(inside[..., None], maps, jnp.zeros((), BF16))
    x_tall = joined(rims(maps, 0, shift_rows), maps, 0)
    later_w, x_tall = lax.optimization_barrier((wide_w, x_tall))
    x_pad = joined(rims(x_tall, 1, shift_cols), x_tall, 1)
    pieces[-1], x_pad = lax.optimization_barrier((pieces[-1], x_pad))
    branch_w = gather_weights(later_w[1:])
    branch_in = (branch_w, leading((1,) + branch_w.shape[1:]))
    pieces = spread_cores(pieces)
    x_other = lax.ppermute(x_pad, "core", PAIR)
    cot = cotangent.transpose(0, 2, 3, 1, 4)

    full = (rows, cols, images, channels)
    half = (half_rows, half_cols, images, channels)
    wide = (half_rows + 2, half_cols + 2, images, channels)
    quarter = (half_rows // 2, half_cols // 2, images, channels)
    stat = (devices, 2, channels)
    task_stat = (devices, tasks, 2, channels)
    one_stat = second_dim((devices, 1, 2, channels))
    meta_in = (meta, whole(meta.shape))
    count_in = (counts, whole(counts.shape))
    norm_in = (norm_w, whole(norm_w.shape))
    full_in = (full_ext, whole(full_ext.shape))
    half_in = (half_ext, whole(half_ext.shape))
    vec = pltpu.VMEM((2, channels), F32)
    place_in = (place, pl.BlockSpec(memory_space=pltpu.SMEM))
    anywhere = pl.BlockSpec(memory_space=pl.ANY)
    copies = 4 * (1 + lax.axis_size("rows") * (lax.axis_size("chips") - 1))

    point_split = (2 * lax.axis_size("chips"), 2 * tasks, point_w.shape[1], channels)
    point_flat = (point_split[0], point_split[1] * point_split[2], channels)
    point_block = (point_split[0], 1) + point_split[2:]
    weight = (9 * channels, channels)

    full_flops = 2 * 9 * rows * cols * images * channels * channels
    half_flops = full_flops // 4 * tasks
    task_of = lambda shape: leading((1,) + shape)

    block = 4
    z, local, shared_w, point_full = call(
        functools.partial(shared_fwd_kernel, block),
        rows // block,
        [place_in, (x_pad, whole(x_pad.shape)), meta_in, full_in] + [(p, anywhere) for p in pieces],
        [
            (shape_of(full, F32), leading((block,) + full[1:])),
            (shape_of(stat, BF16), whole(stat)),
            (shape_of(weight, BF16), anywhere),
            (shape_of(point_flat, BF16), anywhere),
        ],
        [
            vec,
            pltpu.VMEM(weight, BF16),
            pltpu.VMEM(point_flat, BF16),
            pltpu.SemaphoreType.DMA((copies,)),
            pltpu.SemaphoreType.DMA((2,)),
        ],
        full_flops,
    )
    point_full = point_full.reshape(point_split)
    first_ws = (point_full, pl.BlockSpec(point_block, lambda i: (0, i, 0, 0)))
    second_ws = (point_full, pl.BlockSpec(point_block, lambda i: (0, i + tasks, 0, 0)))
    stat0 = spread_all(local)

    pooled, local = call(
        functools.partial(pool_kernel, block),
        rows // block,
        [
            (z, leading((block,) + full[1:])),
            (stat0, whole(stat)),
            count_in,
            meta_in,
            norm_in,
            full_in,
            (
                point_full,
                pl.BlockSpec((point_split[0], tasks) + point_split[2:], lambda i: (0, 0, 0, 0)),
            ),
        ],
        [
            (shape_of(half, BF16), leading((block // 2,) + half[1:])),
            (shape_of(task_stat, BF16), whole(task_stat)),
        ],
        [pltpu.VMEM(half, BF16), vec],
    )
    pooled_wide = extended(pooled, 0)
    stat1 = spread_all(local)

    first, hidden, second, local = call(
        attend_kernel,
        tasks,
        [
            (pooled_wide, whole(wide)),
            (stat1, one_stat),
            count_in,
            meta_in,
            norm_in,
            half_in,
            first_ws,
            second_ws,
        ],
        [
            (shape_of((tasks,) + half, F32), task_of(half)),
            (shape_of((tasks,) + half, BF16), task_of(half)),
            (shape_of((tasks,) + wide, F32), task_of(wide)),
            (shape_of(task_stat, BF16), one_stat),
        ],
    )
    stat2 = spread_all(local)

    masked, branch, local = call(
        branch_fwd_kernel,
        tasks,
        [
            (second, task_of(wide)),
            (pooled_wide, whole(wide)),
            (stat2, one_stat),
            count_in,
            meta_in,
            norm_in,
            half_in,
            branch_in,
        ],
        [
            (shape_of((tasks,) + wide, BF16), task_of(wide)),
            (shape_of((tasks,) + half, F32), task_of(half)),
            (shape_of(task_stat, BF16), one_stat),
        ],
        flops=half_flops,
    )
    masked_other = lax.ppermute(masked, "core", PAIR)
    stat3 = spread_all(local)

    branch_ins = [
        (branch, task_of(half)),
        (cot, task_of(quarter)),
        (stat3, one_stat),
    ]
    result, local = call(
        result_kernel,
        tasks,
        branch_ins + [count_in, meta_in, norm_in, half_in],
        [
            (shape_of((tasks,) + quarter, BF16), task_of(quarter)),
            (shape_of(task_stat, BF16), one_stat),
        ],
    )
    back3 = spread_all(local)

    (branch_dz,) = call(
        branch_dz_kernel,
        tasks,
        branch_ins + [(back3, one_stat), count_in, meta_in, norm_in, half_in],
        [(shape_of((tasks,) + half, BF16), task_of(half))],
    )
    dz_other = halves(branch_dz)[1]
    dz_tall = joined(rims(branch_dz, 1, shift_rows), branch_dz, 1)
    dz_rim = rims(dz_tall, 2, shift_cols)
    narrow = half[:-1] + (channels // 2,)
    chips, quarters = lax.axis_size("chips"), lax.axis_size("rows")
    piece = 9 * channels // (2 * chips * quarters)
    (branch_grad,) = call(
        branch_wgrad_kernel,
        tasks,
        [
            place_in,
            (masked, task_of(wide)),
            (masked_other, task_of(wide)),
            (branch_dz, task_of(half)),
            (dz_other, task_of(narrow)),
        ],
        [
            (
                shape_of((quarters, chips, tasks, 2, piece, channels // 2), BF16),
                pl.BlockSpec(
                    (quarters, chips, 1, 2, piece, channels // 2), lambda i: (0, 0, i, 0, 0, 0)
                ),
            )
        ],
        flops=half_flops,
    )
    branch_grad, dz_rim = lax.optimization_barrier((branch_grad, dz_rim))
    branch_parts = lax.psum_scatter(branch_grad, "rows", scatter_dimension=0, tiled=True)[0]
    dz_wide = joined(dz_rim, dz_tall, 2)

    ga, product, local = call(
        branch_dgrad_kernel,
        tasks,
        [
            (dz_wide, task_of(wide)),
            branch_in,
            (second, task_of(wide)),
            (pooled, whole(half)),
            (stat2, one_stat),
            count_in,
            meta_in,
            norm_in,
        ],
        [
            (shape_of((tasks,) + half, F32), task_of(half)),
            (shape_of(half, F32), whole(half)),
            (shape_of(task_stat, BF16), one_stat),
        ],
        flops=half_flops,
    )
    back2 = spread_all(local)

    square = (channels, channels)
    point_shape = (2, 2 * tasks, channels, channels // 2)
    point_ref = (2, 1, channels, channels // 2)
    second_grad, gl, local = call(
        attend_back_kernel,
        tasks,
        [
            (ga, task_of(half)),
            (second, task_of(wide)),
            (stat2, one_stat),
            (back2, one_stat),
            (hidden, task_of(half)),
            second_ws,
            (first, task_of(half)),
            (stat1, one_stat),
            count_in,
            meta_in,
            norm_in,
            half_in,
        ],
        [
            (
                shape_of(point_shape, BF16),
                pl.BlockSpec(point_ref, lambda i: (0, i + tasks, 0, 0)),
            ),
            (shape_of((tasks,) + half, F32), task_of(half)),
            (shape_of(task_stat, BF16), one_stat),
        ],
    )
    back1 = spread_all(local)

    point_local, grad_pooled, local = call(
        functools.partial(pooled_back_kernel, block),
        tasks,
        [
            (gl, task_of(half)),
            (first, task_of(half)),
            (stat1, one_stat),
            (back1, one_stat),
            (pooled, whole(half)),
            first_ws,
            (product, whole(half)),
            (z, whole(full)),
            (stat0, whole(stat)),
            count_in,
            meta_in,
            norm_in,
            half_in,
            full_in,
            (second_grad, anywhere),
        ],
        [
            (shape_of(point_shape, BF16), second_dim(point_ref)),
            (shape_of(half, F32), whole(half)),
            (shape_of(stat, BF16), whole(stat)),
        ],
        aliases={14: 0},
    )
    back0 = spread_all(local)
    core = lax.axis_index("core")
    point_own = pick(point_local, 0, core)
    point_other = swap(pick(point_local, 0, 1 - core), "core", 1)
    point_half, back0 = lax.optimization_barrier((point_own + point_other, back0))
    point_parts_shape = (
        2 * tasks,
        chips,
        2,
        quarters,
        channels // (2 * chips * quarters),
        channels // 2,
    )
    point_parts = reduce_rows(row_sends(point_half.reshape(point_parts_shape).transpose(3, 1, 0, 2, 4, 5)))

    (shared_dz,) = call(
        functools.partial(shared_dz_kernel, block),
        rows // block,
        [
            (z, leading((block,) + full[1:])),
            (grad_pooled, leading((block // 2,) + half[1:])),
            (stat0, whole(stat)),
            (back0, whole(stat)),
            count_in,
            meta_in,
            norm_in,
            full_in,
        ],
        [(shape_of(full, BF16), leading((block,) + full[1:]))],
    )
    branch_parts, shared_dz = lax.optimization_barrier((branch_parts, shared_dz))
    branch_parts = lax.psum_scatter(branch_parts, "chips", scatter_dimension=0, tiled=True)
    dz_other = halves(shared_dz)[1]
    dz_rim = rims(shared_dz, 0, shift_rows)
    (shared_grad,) = call(
        shared_wgrad_kernel,
        9,
        [
            place_in,
            (x_pad, whole(x_pad.shape)),
            (x_other, whole(x_other.shape)),
            (shared_dz, whole(full)),
            (dz_other, whole(dz_other.shape)),
        ],
        [
            (
                shape_of((quarters, chips, 1, 2, piece, channels // 2), BF16),
                whole((quarters, chips, 1, 2, piece, channels // 2)),
            )
        ],
        flops=full_flops,
    )
    sends = row_sends(shared_grad)
    point_parts, sends, dz_rim = lax.optimization_barrier((point_parts, sends, dz_rim))
    branch_parts, _ = lax.optimization_barrier((branch_parts, sends))
    shared_parts = reduce_rows(sends)
    dz_tall = joined(dz_rim, shared_dz, 0)
    dz_pad = joined(rims(dz_tall, 1, shift_cols), dz_tall, 1)
    branch_parts, dz_pad = lax.optimization_barrier((pair_share(branch_parts), dz_pad))
    branch_share = share_rows(branch_parts)
    point_parts = reduce_chips(point_parts)
    (input_grad,) = call(
        functools.partial(shared_dgrad_kernel, block),
        rows // block,
        [(dz_pad, whole(dz_pad.shape)), (shared_w, whole(weight)), full_in],
        [
            (
                shape_of(features.shape, F32),
                second_dim((images, block, cols, channels)),
            )
        ],
        flops=full_flops,
    )
    shared_parts, point_parts, input_grad = lax.optimization_barrier(
        (shared_parts, point_parts, input_grad)
    )
    shared_parts = reduce_chips(shared_parts)
    (back0, back1, back2, back3), _ = lax.optimization_barrier(
        ((back0, back1, back2, back3), input_grad)
    )
    branch_share, _ = lax.optimization_barrier((branch_share, input_grad))
    branch_state = update(branch_share, wide_w, wide_mom, wide_avg, rate_wide, 1, tasks)
    point_share = share_rows(pair_share(point_parts))
    shared_parts, branch_state = lax.optimization_barrier((shared_parts, branch_state))
    shared_share = share_rows(pair_share(shared_parts))
    point_state = update(point_share, point_w, point_mom, point_avg, rate_point, 0, 2 * tasks)
    shared_share, point_state, input_grad = lax.optimization_barrier(
        (shared_share, point_state, input_grad)
    )
    point_share, point_mom_new, point_new, point_avg_new = point_state

    wide_share, wide_mom_new, wide_new, wide_avg_new = update(
        shared_share, wide_w, wide_mom, wide_avg, rate_wide, 0, 1, branch_state
    )
    bsum = jnp.stack([jnp.sum(b.astype(F32), axis=0) for b in (back1, back2, back3)], axis=1)
    bsum = bsum.transpose(2, 0, 1, 3).reshape(2, 3 * tasks, channels)
    norm_grad = jnp.concatenate([jnp.sum(back0.astype(F32), axis=0)[:, None], bsum], axis=1)[::-1]
    norm_mom_new, norm_new, norm_avg_new = refresh(norm_w, norm_grad, norm_mom, norm_avg, RATE_NORM)
    return (
        result.transpose(0, 3, 1, 2, 4),
        input_grad,
        wide_share,
        wide_mom_new,
        wide_new,
        wide_avg_new,
        point_share,
        point_mom_new,
        point_new,
        point_avg_new,
        norm_grad,
        norm_mom_new,
        norm_new,
        norm_avg_new,
    )


def solution(mesh):
    rows, cols = mesh.devices.shape
    cores = 2
    fine = Mesh(mesh.devices.reshape(rows, cols // cores, cores), EVERY)
    across = ("chips", "core")
    weights = P(None, across, None)
    placed = (
        P(None, "rows", across, None),
        P(),
        P(None, None, "rows", across, None),
        weights,
        weights,
        weights,
        weights,
        weights,
        weights,
        P(),
        P(),
        P(),
    )
    return jax.shard_map(
        shards,
        mesh=fine,
        in_specs=placed,
        out_specs=(
            P(None, None, "rows", across, None),
            P(None, "rows", across, None),
            weights,
            weights,
            weights,
            weights,
            weights,
            weights,
            weights,
            weights,
            P(),
            P(),
            P(),
            P(),
        ),
        check_vma=False,
    )
```
